32 devices in a mesh: expert: 8 (over z, y), dp: 4 (over x, core).
Axes of the slice: x: 2, y: 2, z: 4, core: 2. Of those that a mesh axis runs over, the one named last changes fastest.
Arguments:
- prenorm_input: bfloat16 [4096, 1280], P(('expert', 'dp')), may hold values from -6 to 6
- gain: float32 [1280], replicated, may hold values from 0.25 to 1.75
- router: bfloat16 [1280, 4], replicated, may hold values from -0.15625 to 0.15625
- routes: int32 [4096, 2], P(('expert', 'dp')), may hold values from 0 to 3, all different within a row; in each aligned block of 128 rows (0 to 127, 128 to 255, ...) at most 80 rows name the same one
- w_in: bfloat16 [8, 1280, 1280], P('expert', None, 'dp'), may hold values from -0.15625 to 0.15625
- w_out: bfloat16 [8, 1280, 1280], P('expert', 'dp'), may hold values from -0.125 to 0.125
- cotangent: bfloat16 [4096, 1280], P(('expert', 'dp')), may hold values from -18 to 18
Outputs:
- input_grad: bfloat16 [4096, 1280], P(('expert', 'dp'))
- grad_in: bfloat16 [8, 1280, 1280], P('expert', None, 'dp')
- grad_out: bfloat16 [8, 1280, 1280], P('expert', 'dp')
- grad_router: float32 [1280, 4], replicated
- grad_gain: float32 [1280], replicated
The draws below stay inside these ranges and needn't reach their ends.
Inputs may be any that keep to these rules, and one draw needn't show every extreme that they name: `routes`: each row names 2 different experts; among the rows of one device no expert is named more than 80 times.
All inputs are finite; a program needn't handle non-finite values.
Results may differ from the reference program's by a relative error of at most 0.015.
Values may be sent and summed in bfloat16 or wider, within the bound.
No kernel may reach another device: no remote copies, remote signals or barrier semaphores. Data moves between devices by JAX's collectives and lax.ppermute only.
A program may use at most 128 MiB of HBM per device.

```python
import math
import jax
import jax.numpy as jnp
import numpy as np
from jax import lax

MODEL_WIDTH = 1280
FF = 2560
CHOSEN_EXPERTS = 2
DEVICE_TOKENS = 128
EXPERTS = 4
CAP = 80
TOKENS = 4096


def draw_cotangent(key, part):
    key_base, key_rows, key_cols = jax.random.split(key, 3)
    positions = jnp.arange(TOKENS).astype(jnp.float32)
    ramp = 0.5 + positions / TOKENS
    row_scale = ramp * jnp.exp(jax.random.uniform(key_rows, (TOKENS,), jnp.float32, 0.0, math.log(4.0)))
    col_scale = jnp.exp(jax.random.uniform(key_cols, (MODEL_WIDTH,), jnp.float32, 0.0, math.log(3.0)))
    base = jnp.clip(jax.random.normal(key_base, (TOKENS, MODEL_WIDTH), jnp.float32), -4.0, 4.0)
    return (0.25 * base * row_scale[:, None] * col_scale[None, :]).astype(jnp.bfloat16)


def steps_of(stream_key, shape, cuts, smallest, top_value):
    def one(position, blocks):
        draws = jax.random.uniform(jax.random.fold_in(jax.random.fold_in(stream_key, 6), position), (blocks,), jnp.float32, smallest / len(cuts), top_value / len(cuts))
        return jnp.repeat(jnp.exp(draws), shape[position] // blocks).reshape((-1,) + (1,) * (len(shape) - position - 1))

    level = one(*cuts[0])
    for cut in cuts[1:]:
        level = level * one(*cut)
    return level


def shared_out(stream_key, own, number, rows, number_of, top, bound, lean):
    sequence = jax.random.permutation(stream_key, number_of)
    crowded, usual = portions_of(number_of, rows * top, bound, lean, True), portions_of(number_of, rows * top, bound, lean, False)
    places = jnp.arange(number_of)

    def named(sizes, rotation):
        used = int((sizes > 0).sum())
        fixed = max(1, used // 4)
        passed = fixed + (places - fixed + rotation * (used - fixed)) % max(1, number_of - fixed)
        return jnp.zeros((number_of,), jnp.int32).at[sequence[jnp.where(places < fixed, places, passed)]].set(jnp.asarray(sizes, jnp.int32))

    sizes = jnp.where(number % 4 == 0, named(crowded, number // 4), named(usual, number - number // 4 - 1))
    mixed = jax.random.permutation(jax.random.fold_in(own, 3), number_of)
    giver, sink = mixed[0:number_of // 2 * 2:2], mixed[1:number_of // 2 * 2:2]
    slack = jnp.minimum(sizes[giver] - 1, bound - sizes[sink]) // 2
    slack = jnp.where((giver == sequence[0]) | (sink == sequence[0]) | (sizes[sink] == 0), 0, jnp.maximum(slack, 0))
    passed = jax.random.randint(jax.random.fold_in(own, 4), (number_of // 2,), 0, 1 << 20) % (slack + 1)
    sizes = sizes.at[giver].add(-passed).at[sink].add(passed)
    members = jnp.searchsorted(jnp.cumsum(sizes), jnp.arange(rows * top), side="right").astype(jnp.int32)
    table = members.reshape(top, rows).T
    table = table[jax.random.permutation(jax.random.fold_in(own, 1), rows)]
    rotation = jax.random.randint(jax.random.fold_in(own, 2), (rows, 1), 0, top)
    return jnp.take_along_axis(table, (jnp.arange(top)[None, :] + rotation) % top, axis=1)


def portions_of(count, total, most, skew, full):
    portions = [(1 << 20) // math.isqrt(rank ** skew) + 1 for rank in range(1, count + 1)]
    largest = most if full else min(most, max(-(-total // count), total * portions[0] // sum(portions)))
    least = 1 if total - largest >= count - 1 else 0
    given, surplus = [largest] + [least] * (count - 1), total - largest - least * (count - 1)
    while surplus > 0:
        free = [i for i in range(1, count) if given[i] < largest] or [i for i in range(1, count) if given[i] < most]
        mass, left = sum([portions[i] for i in free]), surplus
        for i in free:
            more = min(most - given[i], max(1, left * portions[i] // mass), surplus)
            given[i] = given[i] + more
            surplus = surplus - more
    return np.array(given)


def bell_draw(key, extent, spread, most, cuts=(), kind=jnp.bfloat16):
    values = spread * jax.random.normal(key, extent, jnp.float32)
    if cuts:
        values = values * steps_of(key, extent, cuts, -0.22, 0.18)
    return jnp.clip(values, -most, most).astype(kind)


def setup_inputs(seed: int = 0) -> dict:
    seeds = jax.random.split(jax.random.key(seed), 8)
    prenorm_input = bell_draw(seeds[0], (TOKENS, MODEL_WIDTH), 1.0, 6.0, ((0, 32),))
    gain = jnp.clip(1.0 + 0.15 * jax.random.normal(seeds[1], (MODEL_WIDTH,), jnp.float32), 0.25, 1.75)
    router = bell_draw(seeds[2], (MODEL_WIDTH, EXPERTS), MODEL_WIDTH ** -0.5, 0.15625)
    routes_keys = jax.random.split(jax.random.fold_in(seeds[3], 1), TOKENS // DEVICE_TOKENS)
    routes_turns = jax.random.permutation(jax.random.fold_in(seeds[3], 3), TOKENS // DEVICE_TOKENS)
    routes = jax.vmap(lambda own, number: shared_out(jax.random.fold_in(seeds[3], 2), own, number, DEVICE_TOKENS, EXPERTS, CHOSEN_EXPERTS, CAP, 2))(routes_keys, routes_turns).reshape((TOKENS, CHOSEN_EXPERTS))
    w_in = bell_draw(seeds[4], (2 * EXPERTS, MODEL_WIDTH, FF // 2), MODEL_WIDTH ** -0.5, 0.15625, ((0, 8), (2, 4)))
    w_out = bell_draw(seeds[5], (2 * EXPERTS, FF // 2, MODEL_WIDTH), FF ** -0.5, 0.125, ((0, 8), (1, 4)))
    cotangent = draw_cotangent(jax.random.fold_in(seeds[7], 71), 0)
    return dict(prenorm_input=prenorm_input, gain=gain, router=router, routes=routes, w_in=w_in, w_out=w_out, cotangent=cotangent)


def gelu_parts(pre):
    coeff = math.sqrt(2.0 / math.pi)
    inner = coeff * (pre + 0.044715 * pre * pre * pre)
    tanh_val = jnp.tanh(inner)
    value = 0.5 * pre * (1.0 + tanh_val)
    slope = 0.5 * (1.0 + tanh_val) + 0.5 * pre * (1.0 - tanh_val * tanh_val) * coeff * (1.0 + 3.0 * 0.044715 * pre * pre)
    return (value, slope)

def norm_pieces(block, gain):
    values = block.astype(jnp.float32)
    centred_rows = values - lax.optimization_barrier(jnp.mean(values, axis=1, keepdims=True))
    inverse_deviation = lax.rsqrt(lax.optimization_barrier(jnp.mean(centred_rows * centred_rows, axis=1, keepdims=True)) + 1e-06)
    normalized_rows = centred_rows * inverse_deviation
    return (normalized_rows, inverse_deviation, (normalized_rows * gain[None, :]).astype(jnp.bfloat16))

def slot_index(routing_rows, expert_list, expert_capacity):
    flat = routing_rows.reshape(-1).astype(jnp.int32)
    onehot = (flat[:, None] == jnp.arange(expert_list, dtype=jnp.int32)[None, :]).astype(jnp.int32)
    before = (jnp.cumsum(onehot, axis=0) - onehot).astype(jnp.int32)
    slot = lax.optimization_barrier(jnp.sum(before * onehot, axis=1)).astype(jnp.int32)
    return (flat * expert_capacity + slot).astype(jnp.int32)

def place_matrix(where, slots):
    return where[None, :] == jnp.arange(slots, dtype=jnp.int32)[:, None]

def expert_pass(rows_m, rows_d, column, w_first, w_second):
    gate = jax.nn.sigmoid(jnp.dot(rows_m, column, preferred_element_type=jnp.float32)[:, 0])
    pre = jnp.dot(rows_m, w_first, preferred_element_type=jnp.float32)
    value, slope = gelu_parts(pre)
    hidden = value.astype(jnp.bfloat16)
    back = jnp.dot(rows_d, w_second.T, preferred_element_type=jnp.float32)
    gate_gradient = lax.optimization_barrier(jnp.sum(hidden.astype(jnp.float32) * back, axis=1))
    grad_pre = (gate[:, None] * back * slope).astype(jnp.bfloat16)
    grad_y = (gate[:, None] * rows_d.astype(jnp.float32)).astype(jnp.bfloat16)
    grad_second = jnp.dot(hidden.T, grad_y, preferred_element_type=jnp.float32)
    grad_first = jnp.dot(rows_m.T, grad_pre, preferred_element_type=jnp.float32)
    row_gradient = jnp.dot(grad_pre, w_first.T, preferred_element_type=jnp.float32)
    return (row_gradient, gate_gradient, grad_first, grad_second)

def token_gradient(mixed_rows, normalized_rows, inverse_deviation, cotangent, routing_rows, gain, router, slot_gradient, slot_gate_gradient, expert_list, expert_capacity):
    where = slot_index(routing_rows, expert_list, expert_capacity)
    tok = mixed_rows.shape[0]
    top = routing_rows.shape[1]
    hi = lax.Precision.HIGHEST
    grad_assign = jnp.take(slot_gradient, where, axis=0)
    grad_expert = lax.optimization_barrier(jnp.sum(grad_assign.reshape(tok, top, -1), axis=1))
    gate_gradient = jnp.take(slot_gate_gradient, where, axis=0).reshape(tok, top)
    logits = jnp.dot(mixed_rows, router, preferred_element_type=jnp.float32)
    choose = (routing_rows[:, :, None] == jnp.arange(expert_list, dtype=jnp.int32)[None, None, :]).astype(jnp.float32)
    gates = jax.nn.sigmoid(lax.optimization_barrier(jnp.sum(choose * logits[:, None, :], axis=2)))
    dlogit = lax.optimization_barrier(jnp.sum(choose * (gate_gradient * gates * (1.0 - gates))[:, :, None], axis=1))
    mixed_gradient = grad_expert + jnp.dot(dlogit, router.astype(jnp.float32).T, precision=hi)
    router_term = jnp.dot(mixed_rows.astype(jnp.float32).T, dlogit, precision=hi)
    gain_product = lax.optimization_barrier(jnp.sum(mixed_gradient * normalized_rows, axis=0))
    scaled_rows = mixed_gradient * gain[None, :]
    mean_first_term = lax.optimization_barrier(jnp.mean(scaled_rows, axis=1, keepdims=True))
    mean_second_term = lax.optimization_barrier(jnp.mean(scaled_rows * normalized_rows, axis=1, keepdims=True))
    norm_backward = inverse_deviation * (scaled_rows - mean_first_term - normalized_rows * mean_second_term)
    final_result = (cotangent.astype(jnp.float32) + norm_backward).astype(jnp.bfloat16)
    return (final_result, router_term, gain_product)

def reference(prenorm_input, gain, router, routes, w_in, w_out, cotangent):
    block_list = TOKENS // DEVICE_TOKENS
    slots = EXPERTS * CAP
    half = FF // 2
    normalized_rows, inverse_deviation, mixed_rows = norm_pieces(prenorm_input, gain)
    full_in = w_in.reshape(EXPERTS, 2, MODEL_WIDTH, half).transpose(0, 2, 1, 3).reshape(EXPERTS, MODEL_WIDTH, FF)
    full_out = w_out.reshape(EXPERTS, FF, MODEL_WIDTH)

    def dispatch(items):
        m_blk, d_blk, r_blk = items
        places = place_matrix(slot_index(r_blk, EXPERTS, CAP), slots).astype(jnp.bfloat16)
        send_m = jnp.dot(places, jnp.repeat(m_blk, CHOSEN_EXPERTS, axis=0), preferred_element_type=jnp.float32).astype(jnp.bfloat16)
        send_d = jnp.dot(places, jnp.repeat(d_blk, CHOSEN_EXPERTS, axis=0), preferred_element_type=jnp.float32).astype(jnp.bfloat16)
        return (send_m, send_d)
    send_m, send_d = lax.map(dispatch, (mixed_rows.reshape(block_list, DEVICE_TOKENS, MODEL_WIDTH), cotangent.reshape(block_list, DEVICE_TOKENS, MODEL_WIDTH), routes.reshape(block_list, DEVICE_TOKENS, CHOSEN_EXPERTS)))

    def by_expert(stack):
        return stack.reshape(block_list, EXPERTS, CAP, MODEL_WIDTH).transpose(1, 0, 2, 3).reshape(EXPERTS, block_list * CAP, MODEL_WIDTH)
    columns = router.T[:, :, None]

    def per_expert(items):
        rows_m, rows_d, column, w_first, w_second = items
        return expert_pass(rows_m, rows_d, column, w_first, w_second)
    row_gradient, gate_gradient, grad_first, grad_second = lax.map(per_expert, (by_expert(send_m), by_expert(send_d), columns, full_in, full_out))
    row_gradient = row_gradient.reshape(EXPERTS, block_list, CAP, MODEL_WIDTH).transpose(1, 0, 2, 3).reshape(block_list, slots, MODEL_WIDTH)
    gate_gradient = gate_gradient.reshape(EXPERTS, block_list, CAP).transpose(1, 0, 2).reshape(block_list, slots)

    def combine_rows(items):
        m_blk, x_blk, s_blk, d_blk, r_blk, g_blk, q_blk = items
        return token_gradient(m_blk, x_blk, s_blk, d_blk, r_blk, gain, router, g_blk, q_blk, EXPERTS, CAP)
    final_result, router_pieces, gain_products = lax.map(combine_rows, (mixed_rows.reshape(block_list, DEVICE_TOKENS, MODEL_WIDTH), normalized_rows.reshape(block_list, DEVICE_TOKENS, MODEL_WIDTH), inverse_deviation.reshape(block_list, DEVICE_TOKENS, 1), cotangent.reshape(block_list, DEVICE_TOKENS, MODEL_WIDTH), routes.reshape(block_list, DEVICE_TOKENS, CHOSEN_EXPERTS), row_gradient, gate_gradient))
    grad_in = grad_first.astype(jnp.bfloat16).reshape(EXPERTS, MODEL_WIDTH, 2, half).transpose(0, 2, 1, 3).reshape(2 * EXPERTS, MODEL_WIDTH, half)
    grad_out = grad_second.astype(jnp.bfloat16).reshape(2 * EXPERTS, half, MODEL_WIDTH)
    return (final_result.reshape(TOKENS, MODEL_WIDTH), grad_in, grad_out, lax.optimization_barrier(jnp.sum(router_pieces, axis=0)), lax.optimization_barrier(jnp.sum(gain_products, axis=0)))
```

```python
import math

import jax
import jax.numpy as jnp
from jax import lax
from jax.sharding import PartitionSpec as P

F32 = jnp.float32
BF16 = jnp.bfloat16


def gelu_parts(pre):
    coeff = math.sqrt(2.0 / math.pi)
    inner = coeff * (pre + 0.044715 * pre * pre * pre)
    tanh_val = jnp.tanh(inner)
    value = 0.5 * pre * (1.0 + tanh_val)
    slope = 0.5 * (1.0 + tanh_val) + 0.5 * pre * (1.0 - tanh_val * tanh_val) * coeff * (
        1.0 + 3.0 * 0.044715 * pre * pre
    )
    return (value, slope)


def norm_pieces(block, gain):
    values = block.astype(F32)
    centred_rows = values - jnp.mean(values, axis=1, keepdims=True)
    inverse_deviation = lax.rsqrt(
        jnp.mean(centred_rows * centred_rows, axis=1, keepdims=True) + 1e-06
    )
    normalized_rows = centred_rows * inverse_deviation
    return (
        normalized_rows,
        inverse_deviation,
        (normalized_rows * gain[None, :]).astype(BF16),
    )


def dot(a, b, a_dim, b_dim):
    return lax.dot_general(a, b, (((a_dim,), (b_dim,)), ((), ())), preferred_element_type=F32)


def body(prenorm_input, gain, router, routes, w_in, w_out, cotangent):
    halves = lax.axis_size("expert")
    experts = halves // 2
    groups = lax.axis_size("dp")
    columns = groups // 2
    tokens, width = prenorm_input.shape
    top = routes.shape[1]
    capacity = max(2, 5 * tokens * top // (4 * experts))
    slots = experts * capacity
    own = lax.axis_index("expert") // 2

    swap_half = [(i, i ^ 1) for i in range(halves)]
    swap_pair = [(i, i ^ 1) for i in range(groups)]

    def turn_columns(step):
        return [(i, (i + 2 * step) % groups) for i in range(groups)]

    def turn_experts(step):
        return [(i, (i + 2 * step) % halves) for i in range(halves)]

    first = w_in[0].T
    second = w_out[0]
    first_y = lax.ppermute(first, "expert", swap_half)
    second_y = lax.ppermute(second, "expert", swap_half)
    first_c = lax.ppermute(first, "dp", swap_pair)
    second_c = lax.ppermute(second, "dp", swap_pair)
    first_yc = lax.ppermute(first_y, "dp", swap_pair)
    second_yc = lax.ppermute(second_y, "dp", swap_pair)

    normalized_rows, inverse_deviation, mixed_rows = norm_pieces(prenorm_input, gain)
    relative = (own + jnp.arange(experts, dtype=jnp.int32)) % experts
    chosen = jnp.any(routes[None, :, :] == relative[:, None, None], axis=2)
    order = jnp.arange(tokens, dtype=jnp.int32)
    earlier = (order[:, None] < order[None, :]).astype(BF16)
    before = dot(chosen.astype(BF16), earlier, 1, 0).astype(jnp.int32)
    places = (
        chosen[:, None, :]
        & (before[:, None, :] == jnp.arange(capacity, dtype=jnp.int32)[None, :, None])
    ).astype(BF16).reshape(slots, tokens)
    send_m = dot(places, mixed_rows, 1, 0).astype(BF16).reshape(experts, 1, capacity, width)
    send_d = dot(places, cotangent, 1, 0).astype(BF16).reshape(experts, 1, capacity, width)
    send = jnp.concatenate([send_m, send_d], axis=1)

    near = [send[0]]
    for step in range(1, experts):
        near.append(lax.ppermute(send[step], "expert", turn_experts(step)))
    parts = [near]
    for step in range(1, columns):
        parts.append([lax.ppermute(piece, "dp", turn_columns(step)) for piece in near])
    pieces = [piece for part in parts for piece in part]
    rows_m = jnp.concatenate([piece[0] for piece in pieces], axis=0)
    rows_d = jnp.concatenate([piece[1] for piece in pieces], axis=0)

    column = lax.dynamic_slice_in_dim(router, own, 1, 1)
    all_first = jnp.concatenate([first, first_c, first_y, first_yc], axis=0)
    all_second = jnp.concatenate([second, second_c, second_y, second_yc], axis=0)
    gate = jax.nn.sigmoid(jnp.dot(rows_m, column, preferred_element_type=F32))
    value, slope = gelu_parts(dot(rows_m, all_first, 1, 1))
    hidden = value.astype(BF16)
    back = dot(rows_d, all_second, 1, 1)
    gate_gradient = jnp.sum(hidden.astype(F32) * back, axis=1, keepdims=True)
    logit_gradient = gate_gradient * gate * (1.0 - gate)
    grad_pre = (gate * back * slope).astype(BF16)
    grad_y = (gate * rows_d.astype(F32)).astype(BF16)
    router_row = column[:, 0].astype(F32)[None, :]

    def row_gradient(at, kind):
        part = slice(at * slots, (at + 1) * slots)
        return (
            dot(grad_pre[part], all_first, 1, 0) + logit_gradient[part] * router_row
        ).astype(kind)

    back_rows = [
        lax.ppermute(row_gradient(step, BF16), "dp", turn_columns(columns - step))
        for step in range(1, columns)
    ]
    grad_second = dot(hidden, grad_y, 0, 0)
    grad_first = dot(grad_pre, rows_m, 0, 0)
    own_rows = row_gradient(0, F32)
    for piece in back_rows:
        own_rows = own_rows + piece.astype(F32)
    own_rows = own_rows.astype(BF16).reshape(experts, capacity, width)
    returned = [own_rows[0]]
    for step in range(1, experts):
        returned.append(lax.ppermute(own_rows[step], "expert", turn_experts(experts - step)))

    units = first.shape[0]

    def weight_gradient(whole):
        blocks = whole.reshape(4, units, width)
        mine, pair, half, both = blocks[0], blocks[1], blocks[2], blocks[3]
        half = half + lax.ppermute(both.astype(BF16), "dp", swap_pair).astype(F32)
        mine = mine + lax.ppermute(pair.astype(BF16), "dp", swap_pair).astype(F32)
        return (mine + lax.ppermute(half.astype(BF16), "expert", swap_half).astype(F32)).astype(BF16)

    grad_out = weight_gradient(grad_second)[None]
    grad_in = weight_gradient(grad_first).T[None]

    partial = jnp.stack(
        [
            jnp.sum(rows_m.astype(F32) * logit_gradient, axis=0),
            jnp.sum(all_first.astype(F32) * grad_first, axis=0),
        ]
    )
    gathered = lax.all_gather(partial, ("expert", "dp"), axis=0)
    gathered = jnp.sum(gathered.reshape(experts, 2 * groups, 2, width), axis=1)
    router_t = gathered[:, 0]
    grad_router = router_t.T
    grad_gain = (
        jnp.sum(gathered[:, 1], axis=0) + jnp.sum(router_t * router.astype(F32).T, axis=0)
    ) / gain

    mixed_gradient = dot(places, jnp.concatenate(returned, axis=0), 0, 0)
    scaled_rows = mixed_gradient * gain[None, :]
    mean_first_term = jnp.mean(scaled_rows, axis=1, keepdims=True)
    mean_second_term = jnp.mean(scaled_rows * normalized_rows, axis=1, keepdims=True)
    norm_backward = inverse_deviation * (
        scaled_rows - mean_first_term - normalized_rows * mean_second_term
    )
    input_grad = (cotangent.astype(F32) + norm_backward).astype(BF16)
    return (input_grad, grad_in, grad_out, grad_router, grad_gain)


def solution(mesh):
    in_specs = (
        P(("expert", "dp"), None),
        P(),
        P(),
        P(("expert", "dp"), None),
        P("expert", None, "dp"),
        P("expert", "dp", None),
        P(("expert", "dp"), None),
    )
    out_specs = (
        P(("expert", "dp"), None),
        P("expert", None, "dp"),
        P("expert", "dp", None),
        P(),
        P(),
    )
    return jax.shard_map(body, mesh=mesh, in_specs=in_specs, out_specs=out_specs, check_vma=False)
```

```python
import math

import jax
import jax.numpy as jnp
from jax import lax
from jax.sharding import PartitionSpec as P

F32 = jnp.float32
BF16 = jnp.bfloat16


def gelu_parts(pre):
    coeff = math.sqrt(2.0 / math.pi)
    inner = coeff * (pre + 0.044715 * pre * pre * pre)
    tanh_val = jnp.tanh(inner)
    value = 0.5 * pre * (1.0 + tanh_val)
    slope = 0.5 * (1.0 + tanh_val) + 0.5 * pre * (1.0 - tanh_val * tanh_val) * coeff * (
        1.0 + 3.0 * 0.044715 * pre * pre
    )
    return (value, slope)


def norm_pieces(block, gain):
    values = block.astype(F32)
    centred_rows = values - jnp.mean(values, axis=1, keepdims=True)
    inverse_deviation = lax.rsqrt(
        jnp.mean(centred_rows * centred_rows, axis=1, keepdims=True) + 1e-06
    )
    normalized_rows = centred_rows * inverse_deviation
    return (
        normalized_rows,
        inverse_deviation,
        (normalized_rows * gain[None, :]).astype(BF16),
    )


def dot(a, b, a_dim, b_dim):
    return lax.dot_general(a, b, (((a_dim,), (b_dim,)), ((), ())), preferred_element_type=F32)


def body(prenorm_input, gain, router, routes, w_in, w_out, cotangent):
    halves = lax.axis_size("expert")
    experts = halves // 2
    groups = lax.axis_size("dp")
    columns = groups // 2
    tokens, width = prenorm_input.shape
    top = routes.shape[1]
    capacity = max(2, 5 * tokens * top // (4 * experts))
    slots = experts * capacity
    own = lax.axis_index("expert") // 2

    swap_half = [(i, i ^ 1) for i in range(halves)]
    swap_pair = [(i, i ^ 1) for i in range(groups)]

    def turn_columns(step):
        return [(i, (i + 2 * step) % groups) for i in range(groups)]

    def turn_experts(step):
        return [(i, (i + 2 * step) % halves) for i in range(halves)]

    first = w_in[0].T
    second = w_out[0]
    first_y = lax.ppermute(first, "expert", swap_half)
    first_c = lax.ppermute(first, "dp", swap_pair)
    second_c = lax.ppermute(second, "dp", swap_pair)
    second_held, first_y = lax.optimization_barrier((second, first_y))
    second_y = lax.ppermute(second_held, "expert", swap_half)
    first_yc = lax.ppermute(first_y, "dp", swap_pair)
    second_yc = lax.ppermute(second_y, "dp", swap_pair)

    normalized_rows, inverse_deviation, mixed_rows = norm_pieces(prenorm_input, gain)
    relative = (own + jnp.arange(experts, dtype=jnp.int32)) % experts
    chosen = jnp.any(routes[None, :, :] == relative[:, None, None], axis=2)
    order = jnp.arange(tokens, dtype=jnp.int32)
    earlier = (order[:, None] < order[None, :]).astype(BF16)
    before = dot(chosen.astype(BF16), earlier, 1, 0).astype(jnp.int32)
    places = (
        chosen[:, None, :]
        & (before[:, None, :] == jnp.arange(capacity, dtype=jnp.int32)[None, :, None])
    ).astype(BF16).reshape(slots, tokens)
    send_m = dot(places, mixed_rows, 1, 0).astype(BF16).reshape(experts, 1, capacity, width)
    send_d = dot(places, cotangent, 1, 0).astype(BF16).reshape(experts, 1, capacity, width)
    send = jnp.concatenate([send_m, send_d], axis=1)

    send, first_c, second_c = lax.optimization_barrier((send, first_c, second_c))
    near = [send[0]] + [None] * (experts - 1)
    ranks = sorted(range(1, experts), key=lambda step: min(step, experts - step))
    waves = [[step for step in ranks if min(step, experts - step) == reach] for reach in range(1, experts)]
    waves = [wave for wave in waves if wave]
    held = [send[step] for step in range(experts)]
    for number, wave in enumerate(waves):
        for step in wave:
            near[step] = lax.ppermute(held[step], "expert", turn_experts(step))
        for step in waves[number + 1] if number + 1 < len(waves) else ():
            held[step], *_ = lax.optimization_barrier((held[step], *[near[one] for one in wave]))
    parts = [near]
    for step in range(1, columns):
        parts.append([lax.ppermute(piece, "dp", turn_columns(step)) for piece in near])
    pieces = [piece for part in parts for piece in part]
    rows_m = jnp.concatenate([piece[0] for piece in pieces], axis=0)
    rows_d = jnp.concatenate([piece[1] for piece in pieces], axis=0)

    column = lax.dynamic_slice_in_dim(router, own, 1, 1)
    all_first = jnp.concatenate([first, first_c, first_y, first_yc], axis=0)
    all_second = jnp.concatenate([second, second_c, second_y, second_yc], axis=0)
    gate = jax.nn.sigmoid(jnp.dot(rows_m, column, preferred_element_type=F32))
    value, slope = gelu_parts(dot(rows_m, all_first, 1, 1))
    hidden = value.astype(BF16)
    grad_y = (gate * rows_d.astype(F32)).astype(BF16)
    grad_second = dot(hidden, grad_y, 0, 0)
    units = first.shape[0]

    def pair_sum(whole):
        blocks = whole.reshape(4, units, width)
        half = blocks[2] + lax.ppermute(blocks[3].astype(BF16), "dp", swap_pair).astype(F32)
        mine = blocks[0] + lax.ppermute(blocks[1].astype(BF16), "dp", swap_pair).astype(F32)
        return mine, half.astype(BF16)

    out_mine, out_half = pair_sum(grad_second)
    held_d, grad_second = lax.optimization_barrier((rows_d, grad_second))
    back = dot(held_d, all_second, 1, 1)
    gate_gradient = jnp.sum(hidden.astype(F32) * back, axis=1, keepdims=True)
    logit_gradient = gate_gradient * gate * (1.0 - gate)
    grad_pre = (gate * back * slope).astype(BF16)
    out_half, grad_pre = lax.optimization_barrier((out_half, grad_pre))
    out_other = lax.ppermute(out_half, "expert", swap_half)
    grad_first = dot(grad_pre, rows_m, 0, 0)
    in_mine, in_half = pair_sum(grad_first)
    grad_pre, grad_first = lax.optimization_barrier((grad_pre, grad_first))
    router_row = column[:, 0].astype(F32)[None, :]

    def row_gradient(at, kind):
        part = slice(at * slots, (at + 1) * slots)
        return (
            dot(grad_pre[part], all_first, 1, 0) + logit_gradient[part] * router_row
        ).astype(kind)

    back_rows = [
        lax.ppermute(row_gradient(step, BF16), "dp", turn_columns(columns - step))
        for step in range(1, columns)
    ]
    own_rows = row_gradient(0, F32)
    in_half, own_rows = lax.optimization_barrier((in_half, own_rows))
    in_other = lax.ppermute(in_half, "expert", swap_half)
    for piece in back_rows:
        own_rows = own_rows + piece.astype(F32)
    own_rows = own_rows.astype(BF16).reshape(experts, capacity, width)
    returned = [own_rows[0]]
    for step in range(1, experts):
        returned.append(lax.ppermute(own_rows[step], "expert", turn_experts(experts - step)))
    grad_out = (out_mine + out_other.astype(F32)).astype(BF16)[None]
    grad_in = (in_mine + in_other.astype(F32)).astype(BF16).T[None]

    router_part = jnp.sum(rows_m.astype(F32) * logit_gradient, axis=0)
    gain_part = jnp.sum(all_first.astype(F32) * grad_first, axis=0)
    is_own = (jnp.arange(experts + 1, dtype=jnp.int32) == own)[:, None]
    is_last = (jnp.arange(experts + 1, dtype=jnp.int32) == experts)[:, None]
    router_part, gain_part, in_half = lax.optimization_barrier((router_part, gain_part, in_half))
    total = jnp.where(is_own, router_part[None], jnp.where(is_last, gain_part[None], 0.0))
    for name, size in (("dp", groups), ("expert", halves)):
        bit = 1
        while bit < size:
            total = total + lax.ppermute(total, name, [(i, i ^ bit) for i in range(size)])
            bit *= 2
    router_t = total[:experts]
    grad_router = router_t.T
    grad_gain = (total[experts] + jnp.sum(router_t * router.astype(F32).T, axis=0)) / gain

    mixed_gradient = dot(places, jnp.concatenate(returned, axis=0), 0, 0)
    scaled_rows = mixed_gradient * gain[None, :]
    mean_first_term = jnp.mean(scaled_rows, axis=1, keepdims=True)
    mean_second_term = jnp.mean(scaled_rows * normalized_rows, axis=1, keepdims=True)
    norm_backward = inverse_deviation * (
        scaled_rows - mean_first_term - normalized_rows * mean_second_term
    )
    input_grad = (cotangent.astype(F32) + norm_backward).astype(BF16)
    return (input_grad, grad_in, grad_out, grad_router, grad_gain)


def solution(mesh):
    in_specs = (
        P(("expert", "dp"), None),
        P(),
        P(),
        P(("expert", "dp"), None),
        P("expert", None, "dp"),
        P("expert", "dp", None),
        P(("expert", "dp"), None),
    )
    out_specs = (
        P(("expert", "dp"), None),
        P("expert", None, "dp"),
        P("expert", "dp", None),
        P(),
        P(),
    )
    return jax.shard_map(body, mesh=mesh, in_specs=in_specs, out_specs=out_specs, check_vma=False)
```

```python
import functools
import math

import jax
import jax.numpy as jnp
from jax import lax
from jax.experimental import pallas as pl
from jax.experimental.pallas import tpu as pltpu
from jax.sharding import PartitionSpec as P

F32 = jnp.float32
BF16 = jnp.bfloat16


def gelu_parts(pre):
    coeff = math.sqrt(2.0 / math.pi)
    inner = coeff * (pre + 0.044715 * pre * pre * pre)
    tanh_val = jnp.tanh(inner)
    value = 0.5 * pre * (1.0 + tanh_val)
    slope = 0.5 * (1.0 + tanh_val) + 0.5 * pre * (1.0 - tanh_val * tanh_val) * coeff * (
        1.0 + 3.0 * 0.044715 * pre * pre
    )
    return (value, slope)


def dot(a, b, a_dim, b_dim):
    return lax.dot_general(a, b, (((a_dim,), (b_dim,)), ((), ())), preferred_element_type=F32)


def norm_pieces(block):
    values = block.astype(F32)
    centred_rows = values - jnp.mean(values, axis=1, keepdims=True)
    inverse_deviation = lax.rsqrt(
        jnp.mean(centred_rows * centred_rows, axis=1, keepdims=True) + 1e-06
    )
    return centred_rows * inverse_deviation, inverse_deviation


def slot_of(own, routes, experts, capacity):
    top, tokens = routes.shape
    relative = routes - own
    relative = jnp.where(relative < 0, relative + experts, relative)
    lanes = max(16, experts)
    expert = lax.broadcasted_iota(jnp.int32, (lanes, tokens), 0)
    picks = [expert == relative[j : j + 1, :] for j in range(top)]
    chosen = sum(jnp.where(pick, 1.0, 0.0) for pick in picks)
    earlier = lax.broadcasted_iota(jnp.int32, (tokens, tokens), 0) < lax.broadcasted_iota(
        jnp.int32, (tokens, tokens), 1
    )
    before = dot(chosen.astype(BF16), jnp.where(earlier, 1.0, 0.0).astype(BF16), 1, 0)
    return [
        relative[j : j + 1, :] * capacity
        + jnp.sum(jnp.where(pick, before, 0.0), axis=0, keepdims=True).astype(jnp.int32)
        for j, pick in enumerate(picks)
    ]


def place_matrix(slots, first, count, tokens):
    row = lax.broadcasted_iota(jnp.int32, (count, tokens), 0) + first
    hit = slots[0] == row
    for slot in slots[1:]:
        hit = hit | (slot == row)
    return jnp.where(hit, 1.0, 0.0).astype(BF16)


def dispatch_kernel(experts, capacity, own_ref, x_ref, gain_ref, routes_ref, d_ref, *send_refs):
    tokens = x_ref.shape[0]
    normalized_rows, _ = norm_pieces(x_ref[...])
    mixed_rows = (normalized_rows * gain_ref[...]).astype(BF16)
    cotangent = d_ref[...]
    slots = slot_of(own_ref[0], routes_ref[...], experts, capacity)
    for step in range(experts):
        places = place_matrix(slots, step * capacity, capacity, tokens)
        send_refs[step][0] = dot(places, mixed_rows, 1, 0).astype(BF16)
        send_refs[step][1] = dot(places, cotangent, 1, 0).astype(BF16)


def combine_kernel(experts, capacity, own_ref, x_ref, gain_ref, routes_ref, d_ref, rows_ref, out_ref):
    tokens = x_ref.shape[0]
    normalized_rows, inverse_deviation = norm_pieces(x_ref[...])
    slots = slot_of(own_ref[0], routes_ref[...], experts, capacity)
    places = place_matrix(slots, 0, experts * capacity, tokens)
    scaled_rows = dot(places, rows_ref[...], 0, 0) * gain_ref[...]
    mean_first_term = jnp.mean(scaled_rows, axis=1, keepdims=True)
    mean_second_term = jnp.mean(scaled_rows * normalized_rows, axis=1, keepdims=True)
    norm_backward = inverse_deviation * (
        scaled_rows - mean_first_term - normalized_rows * mean_second_term
    )
    out_ref[...] = (d_ref[...].astype(F32) + norm_backward).astype(BF16)


VMEM = pl.BlockSpec(memory_space=pltpu.VMEM)
SMEM = pl.BlockSpec(memory_space=pltpu.SMEM)


def tied(values, after):
    held, _ = lax.optimization_barrier((values, after))
    return held


def body(prenorm_input, gain, router, routes, w_in, w_out, cotangent):
    halves = lax.axis_size("expert")
    experts = halves // 2
    groups = lax.axis_size("dp")
    columns = groups // 2
    tokens, width = prenorm_input.shape
    top = routes.shape[1]
    capacity = max(2, 5 * tokens * top // (4 * experts))
    own = lax.axis_index("expert") // 2

    swap_half = [(i, i ^ 1) for i in range(halves)]
    swap_pair = [(i, i ^ 1) for i in range(groups)]

    def turn_columns(step):
        return [(i, (i + 2 * step) % groups) for i in range(groups)]

    def turn_experts(step):
        return [(i, (i + 2 * step) % halves) for i in range(halves)]

    own_scalar = own.astype(jnp.int32).reshape(1)
    token_args = (own_scalar, prenorm_input, gain[None, :], routes.T, cotangent)
    send = pl.pallas_call(
        functools.partial(dispatch_kernel, experts, capacity),
        out_shape=[jax.ShapeDtypeStruct((2, capacity, width), BF16)] * experts,
        in_specs=[SMEM, VMEM, VMEM, VMEM, VMEM],
        out_specs=[VMEM] * experts,
        compiler_params=pltpu.CompilerParams(vmem_limit_bytes=32 * 2**20),
        name="dispatch",
    )(*token_args)

    def over_experts(value, step):
        return lax.ppermute(value, "expert", turn_experts(step))

    def over_columns(value):
        return [lax.ppermute(value, "dp", turn_columns(step)) for step in range(1, columns)]

    def over_half(value):
        return lax.ppermute(value, "expert", swap_half)

    def over_pair(value):
        return lax.ppermute(value, "dp", swap_pair)

    first = w_in[0].T
    second = w_out[0]
    reach = [min(step, experts - step) for step in range(experts)]
    close = [step for step in range(experts) if reach[step] == 1]
    far = [step for step in range(experts) if reach[step] > 1]
    near = {0: send[0]}
    for step in close:
        near[step] = over_experts(send[step], step)
    side = {0: over_columns(send[0])}
    first_y = over_half(tied(first, send[0]))
    first_c = over_pair(tied(first, send[0]))

    stage = (first_y, first_c, side[0], [near[step] for step in close])
    second_held, far_held, close_held, first_y = tied(
        (second, [send[step] for step in far], [near[step] for step in close], first_y), stage
    )
    for step, value in zip(far, far_held):
        near[step] = over_experts(value, step)
    for step, value in zip(close, close_held):
        side[step] = over_columns(value)
    second_y = over_half(second_held)
    first_yc = over_pair(first_y)

    stage = (second_y, first_yc, [near[step] for step in far], [side[step] for step in close])
    second_held, far_held, second_y = tied(
        (second_held, [near[step] for step in far], second_y), stage
    )
    for step, value in zip(far, far_held):
        side[step] = over_columns(value)
    second_c = over_pair(second_held)
    second_yc = over_pair(second_y)

    column = lax.dynamic_slice_in_dim(router, own, 1, 1)
    all_first = jnp.concatenate([first, first_c, first_y, first_yc], axis=0)
    all_second = jnp.concatenate([second, second_c, second_y, second_yc], axis=0)

    def gather_rows(steps):
        pieces = [near[step] for step in steps]
        for turn in range(columns - 1):
            pieces = pieces + [side[step][turn] for step in steps]
        return (
            jnp.concatenate([piece[0] for piece in pieces], axis=0),
            jnp.concatenate([piece[1] for piece in pieces], axis=0),
        )

    def front(rows_m, rows_d):
        gate = jax.nn.sigmoid(jnp.dot(rows_m, column, preferred_element_type=F32))
        value, slope = gelu_parts(dot(rows_m, all_first, 1, 1))
        grad_y = (gate * rows_d.astype(F32)).astype(BF16)
        return gate, value.astype(BF16), slope, grad_y

    def middle(rows_d, gate, hidden, slope):
        back = dot(rows_d, all_second, 1, 1)
        gate_gradient = jnp.sum(hidden.astype(F32) * back, axis=1, keepdims=True)
        logit_gradient = gate_gradient * gate * (1.0 - gate)
        return logit_gradient, (gate * back * slope).astype(BF16)

    groups_of = [[0] + close] + ([far] if far else [])
    done = []
    for steps in groups_of:
        m, d = gather_rows(steps)
        gate, hidden, slope, grad_y = front(m, d)
        logit_gradient, grad_pre = middle(d, gate, hidden, slope)
        done.append((m, hidden, grad_y, logit_gradient, grad_pre))
    rows_m, hidden, grad_y, logit_gradient, grad_pre = (
        jnp.concatenate(parts, axis=0) for parts in zip(*done)
    )
    units = first.shape[0]

    def pair_sum(whole):
        blocks = whole.reshape(4, units, width)
        half = blocks[2] + over_pair(blocks[3].astype(BF16)).astype(F32)
        mine = blocks[0] + over_pair(blocks[1].astype(BF16)).astype(F32)
        return mine, half.astype(BF16)

    grad_second = dot(hidden, grad_y, 0, 0)
    out_mine, out_half = pair_sum(grad_second)
    grad_pre = tied(grad_pre, grad_second)
    router_row = column[:, 0].astype(F32)[None, :]

    def row_gradient(turn, kind):
        parts = []
        for steps, (_, _, _, logit_part, grad_part) in zip(groups_of, done):
            count = len(steps) * capacity
            part = slice(turn * count, (turn + 1) * count)
            parts.append(
                (dot(grad_part[part], all_first, 1, 0) + logit_part[part] * router_row).astype(kind)
            )
        return jnp.concatenate(parts, axis=0)

    back_rows = [
        lax.ppermute(row_gradient(turn, BF16), "dp", turn_columns(columns - turn))
        for turn in range(1, columns)
    ]
    out_half, grad_pre = lax.optimization_barrier((out_half, grad_pre))
    out_other = over_half(out_half)
    grad_first = dot(grad_pre, rows_m, 0, 0)
    in_mine, in_half = pair_sum(grad_first)
    own_rows = row_gradient(0, F32)
    in_other = over_half(in_half)
    for piece in back_rows:
        own_rows = own_rows + piece.astype(F32)
    own_rows = own_rows.astype(BF16).reshape(experts, capacity, width)
    order = [step for steps in groups_of for step in steps]
    returned = [None] * experts
    for place, step in enumerate(order):
        if step == 0:
            returned[step] = own_rows[place]
        else:
            returned[step] = over_experts(own_rows[place], experts - step)
    grad_out = (out_mine + out_other.astype(F32)).astype(BF16)[None]
    grad_in = (in_mine + in_other.astype(F32)).astype(BF16).T[None]

    router_part = jnp.sum(rows_m.astype(F32) * logit_gradient, axis=0)
    gain_part = jnp.sum(all_first.astype(F32) * grad_first, axis=0)
    is_own = (jnp.arange(experts + 1, dtype=jnp.int32) == own)[:, None]
    is_last = (jnp.arange(experts + 1, dtype=jnp.int32) == experts)[:, None]
    router_part, gain_part, in_half = lax.optimization_barrier((router_part, gain_part, in_half))
    total = jnp.where(is_own, router_part[None], jnp.where(is_last, gain_part[None], 0.0))
    for name, size in (("dp", groups), ("expert", halves)):
        bit = 1
        while bit < size:
            total = total + lax.ppermute(total, name, [(i, i ^ bit) for i in range(size)])
            bit *= 2
    router_t = total[:experts]
    grad_router = router_t.T
    grad_gain = (total[experts] + jnp.sum(router_t * router.astype(F32).T, axis=0)) / gain

    input_grad = pl.pallas_call(
        functools.partial(combine_kernel, experts, capacity),
        out_shape=jax.ShapeDtypeStruct((tokens, width), BF16),
        in_specs=[SMEM, VMEM, VMEM, VMEM, VMEM, VMEM],
        out_specs=VMEM,
        compiler_params=pltpu.CompilerParams(vmem_limit_bytes=32 * 2**20),
        name="combine",
    )(*token_args, jnp.concatenate(returned, axis=0))
    return (input_grad, grad_in, grad_out, grad_router, grad_gain)


def solution(mesh):
    in_specs = (
        P(("expert", "dp"), None),
        P(),
        P(),
        P(("expert", "dp"), None),
        P("expert", None, "dp"),
        P("expert", "dp", None),
        P(("expert", "dp"), None),
    )
    out_specs = (
        P(("expert", "dp"), None),
        P("expert", None, "dp"),
        P("expert", "dp", None),
        P(),
        P(),
    )
    return jax.shard_map(body, mesh=mesh, in_specs=in_specs, out_specs=out_specs, check_vma=False)
```

```python
import functools
import math

import jax
import jax.numpy as jnp
from jax import lax
from jax.experimental import pallas as pl
from jax.experimental.pallas import tpu as pltpu
from jax.sharding import PartitionSpec as P

F32 = jnp.float32
BF16 = jnp.bfloat16


def gelu_parts(pre):
    coeff = math.sqrt(2.0 / math.pi)
    inner = coeff * (pre + 0.044715 * pre * pre * pre)
    tanh_val = jnp.tanh(inner)
    value = 0.5 * pre * (1.0 + tanh_val)
    slope = 0.5 * (1.0 + tanh_val) + 0.5 * pre * (1.0 - tanh_val * tanh_val) * coeff * (
        1.0 + 3.0 * 0.044715 * pre * pre
    )
    return (value, slope)


def dot(a, b, a_dim, b_dim):
    return lax.dot_general(a, b, (((a_dim,), (b_dim,)), ((), ())), preferred_element_type=F32)


def norm_pieces(block):
    values = block.astype(F32)
    centred_rows = values - jnp.mean(values, axis=1, keepdims=True)
    inverse_deviation = lax.rsqrt(
        jnp.mean(centred_rows * centred_rows, axis=1, keepdims=True) + 1e-06
    )
    return centred_rows * inverse_deviation, inverse_deviation


def slot_of(own, routes, experts, capacity):
    top, tokens = routes.shape
    relative = routes - own
    relative = jnp.where(relative < 0, relative + experts, relative)
    lanes = max(16, experts)
    expert = lax.broadcasted_iota(jnp.int32, (lanes, tokens), 0)
    picks = [expert == relative[j : j + 1, :] for j in range(top)]
    chosen = sum(jnp.where(pick, 1.0, 0.0) for pick in picks)
    earlier = lax.broadcasted_iota(jnp.int32, (tokens, tokens), 0) < lax.broadcasted_iota(
        jnp.int32, (tokens, tokens), 1
    )
    before = dot(chosen.astype(BF16), jnp.where(earlier, 1.0, 0.0).astype(BF16), 1, 0)
    return [
        relative[j : j + 1, :] * capacity
        + jnp.sum(jnp.where(pick, before, 0.0), axis=0, keepdims=True).astype(jnp.int32)
        for j, pick in enumerate(picks)
    ]


def place_matrix(slots, first, count, tokens):
    row = lax.broadcasted_iota(jnp.int32, (count, tokens), 0) + first
    hit = slots[0] == row
    for slot in slots[1:]:
        hit = hit | (slot == row)
    return jnp.where(hit, 1.0, 0.0).astype(BF16)


def dispatch_kernel(experts, capacity, own_ref, x_ref, gain_ref, routes_ref, d_ref, *send_refs):
    tokens = x_ref.shape[0]
    normalized_rows, _ = norm_pieces(x_ref[...])
    mixed_rows = (normalized_rows * gain_ref[...]).astype(BF16)
    cotangent = d_ref[...]
    slots = slot_of(own_ref[0], routes_ref[...], experts, capacity)
    for step in range(experts):
        places = place_matrix(slots, step * capacity, capacity, tokens)
        send_refs[step][0] = dot(places, mixed_rows, 1, 0).astype(BF16)
        send_refs[step][1] = dot(places, cotangent, 1, 0).astype(BF16)


def combine_kernel(experts, capacity, own_ref, x_ref, gain_ref, routes_ref, d_ref, rows_ref, out_ref):
    tokens = x_ref.shape[0]
    normalized_rows, inverse_deviation = norm_pieces(x_ref[...])
    slots = slot_of(own_ref[0], routes_ref[...], experts, capacity)
    places = place_matrix(slots, 0, experts * capacity, tokens)
    scaled_rows = dot(places, rows_ref[...], 0, 0) * gain_ref[...]
    mean_first_term = jnp.mean(scaled_rows, axis=1, keepdims=True)
    mean_second_term = jnp.mean(scaled_rows * normalized_rows, axis=1, keepdims=True)
    norm_backward = inverse_deviation * (
        scaled_rows - mean_first_term - normalized_rows * mean_second_term
    )
    out_ref[...] = (d_ref[...].astype(F32) + norm_backward).astype(BF16)


def front_kernel(tile, m_ref, d_ref, first_ref, second_ref, router_ref, hidden_ref, pre_ref, y_ref, logit_ref):
    rows_m = m_ref[...]
    rows_d = d_ref[...]
    gate = jax.nn.sigmoid(jnp.sum(rows_m.astype(F32) * router_ref[...], axis=1, keepdims=True))
    y_ref[...] = (gate * rows_d.astype(F32)).astype(BF16)
    share = jnp.zeros_like(gate)
    for at in range(0, first_ref.shape[0], tile):
        units = pl.ds(at, tile)
        value, slope = gelu_parts(dot(rows_m, first_ref[units, :], 1, 1))
        back = dot(rows_d, second_ref[units, :], 1, 1)
        hidden = value.astype(BF16)
        hidden_ref[:, units] = hidden
        pre_ref[:, units] = (gate * back * slope).astype(BF16)
        share = share + jnp.sum(hidden.astype(F32) * back, axis=1, keepdims=True)
    logit_ref[...] = jnp.broadcast_to(share * gate * (1.0 - gate), logit_ref.shape)


def rows_kernel(tile, pre_ref, logit_ref, first_ref, router_ref, own_ref, side_ref):
    count = own_ref.shape[0]
    pre = pre_ref[...]
    logit = logit_ref[:, :1]
    for at in range(0, first_ref.shape[1], tile):
        lanes = pl.ds(at, tile)
        rows = dot(pre, first_ref[:, lanes], 1, 0) + logit * router_ref[:, lanes]
        own_ref[:, lanes] = rows[:count]
        side_ref[:, lanes] = rows[count:].astype(BF16)


def weight_kernel(half, tile, left_ref, right_ref, out_ref, turned):
    units = out_ref.shape[0]
    turned[...] = left_ref[:, pl.ds(half * units, units)].T
    for at in range(0, right_ref.shape[1], tile):
        lanes = pl.ds(at, tile)
        out_ref[:, lanes] = dot(turned[...], right_ref[:, lanes], 1, 0).astype(out_ref.dtype)


def sums_kernel(experts, own_ref, m_ref, logit_ref, first_ref, leave_ref, stay_ref, out_ref):
    units = stay_ref.shape[0]
    router_part = jnp.sum(m_ref[...].astype(F32) * logit_ref[:, :1], axis=0, keepdims=True)
    gain_part = jnp.sum(
        first_ref[:units, :].astype(F32) * leave_ref[...].astype(F32), axis=0, keepdims=True
    ) + jnp.sum(first_ref[units:, :].astype(F32) * stay_ref[...], axis=0, keepdims=True)
    row = lax.broadcasted_iota(jnp.int32, out_ref.shape, 0)
    out_ref[...] = jnp.where(
        row == own_ref[0], router_part, jnp.where(row == experts, gain_part, 0.0)
    )


VMEM = pl.BlockSpec(memory_space=pltpu.VMEM)
SMEM = pl.BlockSpec(memory_space=pltpu.SMEM)


PARAMS = pltpu.CompilerParams(vmem_limit_bytes=40 * 2**20)


def tied(values, after):
    held, _ = lax.optimization_barrier((values, after))
    return held


def body(prenorm_input, gain, router, routes, w_in, w_out, cotangent):
    halves = lax.axis_size("expert")
    experts = halves // 2
    groups = lax.axis_size("dp")
    columns = groups // 2
    tokens, width = prenorm_input.shape
    top = routes.shape[1]
    capacity = max(2, 5 * tokens * top // (4 * experts))
    own = lax.axis_index("expert") // 2

    swap_half = [(i, i ^ 1) for i in range(halves)]
    swap_pair = [(i, i ^ 1) for i in range(groups)]

    def turn_columns(step):
        return [(i, (i + 2 * step) % groups) for i in range(groups)]

    def turn_experts(step):
        return [(i, (i + 2 * step) % halves) for i in range(halves)]

    own_scalar = own.astype(jnp.int32).reshape(1)
    token_args = (own_scalar, prenorm_input, gain[None, :], routes.T, cotangent)
    send = pl.pallas_call(
        functools.partial(dispatch_kernel, experts, capacity),
        out_shape=[jax.ShapeDtypeStruct((2, capacity, width), BF16)] * experts,
        in_specs=[SMEM, VMEM, VMEM, VMEM, VMEM],
        out_specs=[VMEM] * experts,
        compiler_params=PARAMS,
        name="dispatch",
    )(*token_args)

    def over_experts(value, step):
        return lax.ppermute(value, "expert", turn_experts(step))

    def over_columns(value):
        return [lax.ppermute(value, "dp", turn_columns(step)) for step in range(1, columns)]

    def over_half(value):
        return lax.ppermute(value, "expert", swap_half)

    def over_pair(value):
        return lax.ppermute(value, "dp", swap_pair)

    first = w_in[0].T
    second = w_out[0]
    units = first.shape[0]
    steps = sorted(range(experts), key=lambda step: min(step, experts - step))
    early, late = steps[: 3 * experts // 4], steps[3 * experts // 4 :]
    near = {0: send[0]}
    for step in early[1:]:
        near[step] = over_experts(send[step], step)
    side = {0: over_columns(send[0])}
    first_y = over_half(tied(first, send[0]))
    first_c = over_pair(tied(first, send[0]))

    stage = (first_y, first_c, side[0], [near[step] for step in early[1:]])
    second_held, late_held, early_held, first_y = tied(
        (second, [send[step] for step in late], [near[step] for step in early[1:]], first_y), stage
    )
    for step, value in zip(late, late_held):
        near[step] = over_experts(value, step)
    for step, value in zip(early[1:], early_held):
        side[step] = over_columns(value)
    second_y = over_half(second_held)
    first_yc = over_pair(first_y)

    stage = (second_y, first_yc, [near[step] for step in late], [side[step] for step in early[1:]])
    second_held, late_held, second_y = tied(
        (second_held, [near[step] for step in late], second_y), stage
    )
    for step, value in zip(late, late_held):
        side[step] = over_columns(value)
    second_c = over_pair(second_held)
    second_yc = over_pair(second_y)

    router_row = lax.dynamic_slice_in_dim(router, own, 1, 1).astype(F32).T
    all_first = jnp.concatenate([first_yc, first_c, first_y, first], axis=0)
    all_second = jnp.concatenate([second_yc, second_c, second_y, second], axis=0)
    hidden_units = 4 * units
    tile = 256 if hidden_units % 256 == 0 else hidden_units

    def gather_rows(steps):
        pieces = [near[step] for step in steps]
        for turn in range(columns - 1):
            pieces = pieces + [side[step][turn] for step in steps]
        return (
            jnp.concatenate([piece[0] for piece in pieces], axis=0),
            jnp.concatenate([piece[1] for piece in pieces], axis=0),
        )

    def front(rows_m, rows_d):
        count = rows_m.shape[0]
        return pl.pallas_call(
            functools.partial(front_kernel, tile),
            out_shape=[jax.ShapeDtypeStruct((count, hidden_units), BF16)] * 2
            + [
                jax.ShapeDtypeStruct((count, width), BF16),
                jax.ShapeDtypeStruct((count, 128), F32),
            ],
            in_specs=[VMEM] * 5,
            out_specs=[VMEM] * 4,
            compiler_params=PARAMS,
            cost_estimate=pl.CostEstimate(
                flops=4 * count * width * hidden_units,
                bytes_accessed=4 * width * hidden_units,
                transcendentals=count * hidden_units,
            ),
            name="front",
        )(rows_m, rows_d, all_first, all_second, router_row)

    def row_gradients(grad_pre, logit_gradient):
        count = grad_pre.shape[0] // columns
        return pl.pallas_call(
            functools.partial(rows_kernel, tile),
            out_shape=[
                jax.ShapeDtypeStruct((count, width), F32),
                jax.ShapeDtypeStruct((grad_pre.shape[0] - count, width), BF16),
            ],
            in_specs=[VMEM] * 4,
            out_specs=[VMEM] * 2,
            compiler_params=PARAMS,
            cost_estimate=pl.CostEstimate(
                flops=2 * grad_pre.shape[0] * width * hidden_units,
                bytes_accessed=2 * width * hidden_units,
                transcendentals=0,
            ),
            name="rows",
        )(grad_pre, logit_gradient, all_first, router_row)

    def weight_half(half, left, right, kind):
        return pl.pallas_call(
            functools.partial(weight_kernel, half, tile),
            out_shape=jax.ShapeDtypeStruct((2 * units, width), kind),
            in_specs=[VMEM] * 2,
            out_specs=VMEM,
            scratch_shapes=[pltpu.VMEM((2 * units, left.shape[0]), BF16)],
            compiler_params=PARAMS,
            cost_estimate=pl.CostEstimate(
                flops=4 * left.shape[0] * width * units,
                bytes_accessed=8 * width * units,
                transcendentals=0,
            ),
            name="weights",
        )(left, right)

    early_m, early_d = gather_rows(early)
    early_hidden, early_pre, early_y, early_logit = front(early_m, early_d)
    early_own, early_side = row_gradients(early_pre, early_logit)
    for step in late:
        near[step], side[step] = tied((near[step], side[step]), (early_own, early_side))
    late_m, late_d = gather_rows(late)
    late_hidden, late_pre, late_y, late_logit = front(late_m, late_d)
    rows_m = jnp.concatenate([early_m, late_m], axis=0)
    logit_gradient = jnp.concatenate([early_logit, late_logit], axis=0)
    grad_pre = jnp.concatenate([early_pre, late_pre], axis=0)
    hidden = jnp.concatenate([early_hidden, late_hidden], axis=0)
    grad_y = jnp.concatenate([early_y, late_y], axis=0)

    def pairwise(value, name, size, bit):
        return value + lax.ppermute(value, name, [(i, i ^ bit) for i in range(size)])

    in_leave = weight_half(0, grad_pre, rows_m, BF16)
    in_pair = over_pair(in_leave)
    in_stay = weight_half(1, tied(grad_pre, in_leave), rows_m, F32)
    total = pl.pallas_call(
        functools.partial(sums_kernel, experts),
        out_shape=jax.ShapeDtypeStruct((-(-(experts + 1) // 8) * 8, width), F32),
        in_specs=[SMEM] + [VMEM] * 5,
        out_specs=VMEM,
        compiler_params=PARAMS,
        cost_estimate=pl.CostEstimate(
            flops=6 * width * hidden_units, bytes_accessed=6 * width * hidden_units, transcendentals=0
        ),
        name="sums",
    )(own_scalar, rows_m, logit_gradient, all_first, in_leave, in_stay)
    total = pairwise(total, "expert", halves, 1)
    late_own, late_side = row_gradients(tied(late_pre, in_stay), late_logit)
    out_leave = weight_half(0, tied(hidden, late_own), grad_y, BF16)

    stage = (in_pair, in_stay, total, late_own, late_side, out_leave)
    in_pair, in_stay, total, late_side, early_side, out_leave, hidden = tied(
        (in_pair, in_stay, total, late_side, early_side, out_leave, hidden), stage
    )
    in_sum = in_stay + in_pair.astype(F32)
    in_half = in_sum[:units].astype(BF16)
    in_other = over_half(in_half)

    def by_turn(rows):
        return rows.reshape(columns - 1, -1, width)

    leaving = jnp.concatenate([by_turn(early_side), by_turn(late_side)], axis=1)
    rows_back = [
        lax.ppermute(leaving[turn - 1], "dp", turn_columns(columns - turn))
        for turn in range(1, columns)
    ]
    out_pair = over_pair(out_leave)
    out_stay = weight_half(1, tied(hidden, (in_half, leaving)), grad_y, F32)
    total = tied(total, out_stay)
    bit = 2
    while bit < halves:
        total = pairwise(total, "expert", halves, bit)
        bit *= 2
    total = pairwise(total, "dp", groups, 1)

    stage = (in_other, rows_back, out_pair, out_stay, total)
    in_other, rows_back, out_pair, out_stay, total = tied(stage, stage)
    out_sum = out_stay + out_pair.astype(F32)
    out_other = over_half(out_sum[:units].astype(BF16))
    own_rows = jnp.concatenate([early_own, late_own], axis=0)
    for piece in rows_back:
        own_rows = own_rows + piece.astype(F32)
    own_rows = own_rows.astype(BF16).reshape(experts, capacity, width)
    returned = [None] * experts
    for place, step in enumerate(steps):
        value = own_rows[place]
        returned[step] = over_experts(value, experts - step) if step else value
    bit = 2
    while bit < groups:
        total = pairwise(total, "dp", groups, bit)
        bit *= 2
    router_t = total[:experts]
    grad_router = router_t.T
    grad_gain = (total[experts] + jnp.sum(router_t * router.astype(F32).T, axis=0)) / gain
    grad_in = (in_sum[units:] + in_other.astype(F32)).astype(BF16).T[None]

    input_grad = pl.pallas_call(
        functools.partial(combine_kernel, experts, capacity),
        out_shape=jax.ShapeDtypeStruct((tokens, width), BF16),
        in_specs=[SMEM, VMEM, VMEM, VMEM, VMEM, VMEM],
        out_specs=VMEM,
        compiler_params=PARAMS,
        name="combine",
    )(*token_args, jnp.concatenate(returned, axis=0))
    out_mine = tied(out_sum[units:], (input_grad, grad_in))
    grad_out = (out_mine + out_other.astype(F32)).astype(BF16)[None]
    return (input_grad, grad_in, grad_out, grad_router, grad_gain)


def solution(mesh):
    in_specs = (
        P(("expert", "dp"), None),
        P(),
        P(),
        P(("expert", "dp"), None),
        P("expert", None, "dp"),
        P("expert", "dp", None),
        P(("expert", "dp"), None),
    )
    out_specs = (
        P(("expert", "dp"), None),
        P("expert", None, "dp"),
        P("expert", "dp", None),
        P(),
        P(),
    )
    return jax.shard_map(body, mesh=mesh, in_specs=in_specs, out_specs=out_specs, check_vma=False)
```

```python
import functools
import math

import jax
import jax.numpy as jnp
from jax import lax
from jax.experimental import pallas as pl
from jax.experimental.pallas import tpu as pltpu
from jax.sharding import PartitionSpec as P

F32 = jnp.float32
BF16 = jnp.bfloat16


def gelu_parts(pre):
    coeff = math.sqrt(2.0 / math.pi)
    inner = coeff * (pre + 0.044715 * pre * pre * pre)
    tanh_val = jnp.tanh(inner)
    value = 0.5 * pre * (1.0 + tanh_val)
    slope = 0.5 * (1.0 + tanh_val) + 0.5 * pre * (1.0 - tanh_val * tanh_val) * coeff * (
        1.0 + 3.0 * 0.044715 * pre * pre
    )
    return (value, slope)


def dot(a, b, a_dim, b_dim):
    return lax.dot_general(a, b, (((a_dim,), (b_dim,)), ((), ())), preferred_element_type=F32)


def norm_pieces(block):
    values = block.astype(F32)
    centred_rows = values - jnp.mean(values, axis=1, keepdims=True)
    inverse_deviation = lax.rsqrt(
        jnp.mean(centred_rows * centred_rows, axis=1, keepdims=True) + 1e-06
    )
    return centred_rows * inverse_deviation, inverse_deviation


def slot_of(own, routes, experts, capacity):
    top, tokens = routes.shape
    relative = routes - own
    relative = jnp.where(relative < 0, relative + experts, relative)
    lanes = max(16, experts)
    expert = lax.broadcasted_iota(jnp.int32, (lanes, tokens), 0)
    picks = [expert == relative[j : j + 1, :] for j in range(top)]
    chosen = sum(jnp.where(pick, 1.0, 0.0) for pick in picks)
    earlier = lax.broadcasted_iota(jnp.int32, (tokens, tokens), 0) < lax.broadcasted_iota(
        jnp.int32, (tokens, tokens), 1
    )
    before = dot(chosen.astype(BF16), jnp.where(earlier, 1.0, 0.0).astype(BF16), 1, 0)
    return [
        relative[j : j + 1, :] * capacity
        + jnp.sum(jnp.where(pick, before, 0.0), axis=0, keepdims=True).astype(jnp.int32)
        for j, pick in enumerate(picks)
    ]


def place_matrix(slots, first, count, tokens):
    row = lax.broadcasted_iota(jnp.int32, (count, tokens), 0) + first
    hit = slots[0] == row
    for slot in slots[1:]:
        hit = hit | (slot == row)
    return jnp.where(hit, 1.0, 0.0).astype(BF16)


def dispatch_kernel(experts, capacity, own_ref, x_ref, gain_ref, routes_ref, d_ref, *send_refs):
    tokens = x_ref.shape[0]
    normalized_rows, _ = norm_pieces(x_ref[...])
    mixed_rows = (normalized_rows * gain_ref[...]).astype(BF16)
    cotangent = d_ref[...]
    slots = slot_of(own_ref[0], routes_ref[...], experts, capacity)
    for step in range(experts):
        places = place_matrix(slots, step * capacity, capacity, tokens)
        send_refs[step][0] = dot(places, mixed_rows, 1, 0).astype(BF16)
        send_refs[step][1] = dot(places, cotangent, 1, 0).astype(BF16)


def combine_kernel(experts, capacity, own_ref, x_ref, gain_ref, routes_ref, d_ref, rows_ref, out_ref):
    tokens = x_ref.shape[0]
    normalized_rows, inverse_deviation = norm_pieces(x_ref[...])
    slots = slot_of(own_ref[0], routes_ref[...], experts, capacity)
    places = place_matrix(slots, 0, experts * capacity, tokens)
    scaled_rows = dot(places, rows_ref[...], 0, 0) * gain_ref[...]
    mean_first_term = jnp.mean(scaled_rows, axis=1, keepdims=True)
    mean_second_term = jnp.mean(scaled_rows * normalized_rows, axis=1, keepdims=True)
    norm_backward = inverse_deviation * (
        scaled_rows - mean_first_term - normalized_rows * mean_second_term
    )
    out_ref[...] = (d_ref[...].astype(F32) + norm_backward).astype(BF16)


def front_kernel(tile, m_ref, d_ref, first_ref, second_ref, router_ref, hidden_ref, pre_ref, y_ref, logit_ref):
    rows_m = m_ref[...]
    rows_d = d_ref[...]
    gate = jax.nn.sigmoid(jnp.sum(rows_m.astype(F32) * router_ref[...], axis=1, keepdims=True))
    y_ref[...] = (gate * rows_d.astype(F32)).astype(BF16)
    share = jnp.zeros_like(gate)
    for at in range(0, first_ref.shape[0], tile):
        units = pl.ds(at, tile)
        value, slope = gelu_parts(dot(rows_m, first_ref[units, :], 1, 1))
        back = dot(rows_d, second_ref[units, :], 1, 1)
        hidden = value.astype(BF16)
        hidden_ref[:, units] = hidden
        pre_ref[:, units] = (gate * back * slope).astype(BF16)
        share = share + jnp.sum(hidden.astype(F32) * back, axis=1, keepdims=True)
    logit_ref[...] = jnp.broadcast_to(share * gate * (1.0 - gate), logit_ref.shape)


def first_kernel(tile, m_ref, d_ref, first_ref, router_ref, hidden_ref, slope_ref, y_ref, gate_ref):
    rows_m = m_ref[...]
    gate = jax.nn.sigmoid(jnp.sum(rows_m.astype(F32) * router_ref[...], axis=1, keepdims=True))
    y_ref[...] = (gate * d_ref[...].astype(F32)).astype(BF16)
    gate_ref[...] = jnp.broadcast_to(gate, gate_ref.shape)
    for at in range(0, first_ref.shape[0], tile):
        units = pl.ds(at, tile)
        value, slope = gelu_parts(dot(rows_m, first_ref[units, :], 1, 1))
        hidden_ref[:, units] = value.astype(BF16)
        slope_ref[:, units] = gate * slope


def second_kernel(tile, d_ref, second_ref, hidden_ref, slope_ref, gate_ref, pre_ref, logit_ref):
    rows_d = d_ref[...]
    gate = gate_ref[:, :1]
    share = jnp.zeros_like(gate)
    for at in range(0, second_ref.shape[0], tile):
        units = pl.ds(at, tile)
        back = dot(rows_d, second_ref[units, :], 1, 1)
        pre_ref[:, units] = (back * slope_ref[:, units]).astype(BF16)
        share = share + jnp.sum(hidden_ref[:, units].astype(F32) * back, axis=1, keepdims=True)
    logit_ref[...] = jnp.broadcast_to(share * gate * (1.0 - gate), logit_ref.shape)


def rows_kernel(tile, m_ref, pre_ref, logit_ref, first_ref, router_ref, own_ref, side_ref, sums_ref):
    count = own_ref.shape[0]
    pre = pre_ref[...]
    logit = logit_ref[:, :1]
    row = lax.broadcasted_iota(jnp.int32, (sums_ref.shape[0], tile), 0)
    for at in range(0, first_ref.shape[1], tile):
        lanes = pl.ds(at, tile)
        rows = dot(pre, first_ref[:, lanes], 1, 0) + logit * router_ref[:, lanes]
        own_ref[:, lanes] = rows[:count]
        side_ref[:, lanes] = rows[count:].astype(BF16)
        rows_m = m_ref[:, lanes].astype(F32)
        router_part = jnp.sum(rows_m * logit, axis=0, keepdims=True)
        gain_part = jnp.sum(rows_m * rows, axis=0, keepdims=True)
        sums_ref[:, lanes] = jnp.where(row == 0, router_part, jnp.where(row == 1, gain_part, 0.0))


def weight_kernel(half, tile, left_ref, right_ref, out_ref, turned):
    units = out_ref.shape[0]
    turned[...] = left_ref[:, pl.ds(half * units, units)].T
    for at in range(0, right_ref.shape[1], tile):
        lanes = pl.ds(at, tile)
        out_ref[:, lanes] = dot(turned[...], right_ref[:, lanes], 1, 0).astype(out_ref.dtype)


VMEM = pl.BlockSpec(memory_space=pltpu.VMEM)
SMEM = pl.BlockSpec(memory_space=pltpu.SMEM)


PARAMS = pltpu.CompilerParams(vmem_limit_bytes=40 * 2**20)


def tied(values, after):
    held, _ = lax.optimization_barrier((values, after))
    return held


def body(prenorm_input, gain, router, routes, w_in, w_out, cotangent):
    halves = lax.axis_size("expert")
    experts = halves // 2
    groups = lax.axis_size("dp")
    columns = groups // 2
    tokens, width = prenorm_input.shape
    top = routes.shape[1]
    capacity = max(2, 5 * tokens * top // (4 * experts))
    own = lax.axis_index("expert") // 2

    swap_half = [(i, i ^ 1) for i in range(halves)]
    swap_pair = [(i, i ^ 1) for i in range(groups)]

    def turn_columns(step):
        return [(i, (i + 2 * step) % groups) for i in range(groups)]

    def turn_experts(step):
        return [(i, (i + 2 * step) % halves) for i in range(halves)]

    def over_experts(value, step):
        return lax.ppermute(value, "expert", turn_experts(step))

    def over_columns(value):
        return [lax.ppermute(value, "dp", turn_columns(step)) for step in range(1, columns)]

    def over_half(value):
        return lax.ppermute(value, "expert", swap_half)

    def over_pair(value):
        return lax.ppermute(value, "dp", swap_pair)

    own_scalar = own.astype(jnp.int32).reshape(1)
    first = w_in[0].T
    second = w_out[0]
    units = first.shape[0]
    first_y = over_half(first)
    first_c = over_pair(first)
    token_args = (own_scalar, prenorm_input, gain[None, :], routes.T, cotangent)
    send = pl.pallas_call(
        functools.partial(dispatch_kernel, experts, capacity),
        out_shape=[jax.ShapeDtypeStruct((2, capacity, width), BF16)] * experts,
        in_specs=[SMEM, VMEM, VMEM, VMEM, VMEM],
        out_specs=[VMEM] * experts,
        compiler_params=PARAMS,
        cost_estimate=pl.CostEstimate(
            flops=4 * experts * capacity * tokens * width,
            bytes_accessed=8 * tokens * width,
            transcendentals=0,
        ),
        name="dispatch",
    )(*token_args)

    steps = sorted(range(experts), key=lambda step: min(step, experts - step))
    early, late = steps[: 3 * experts // 4], steps[3 * experts // 4 :]
    near = {0: send[0]}
    for step in early[1:]:
        near[step] = over_experts(send[step], step)
    side = {0: over_columns(send[0])}

    stage = (first_y, first_c, [near[step] for step in early[1:]], side[0])
    second_held, late_held, early_held, first_y, side[0] = tied(
        (second, [send[step] for step in late], [near[step] for step in early[1:]], first_y, side[0]),
        stage,
    )
    for step, value in zip(late, late_held):
        near[step] = over_experts(value, step)
    for step, value in zip(early[1:], early_held):
        near[step] = value
        side[step] = over_columns(value)
    second_y = over_half(second_held)
    first_yc = over_pair(first_y)

    stage = (second_y, first_yc, [near[step] for step in late], [side[step] for step in early[1:]])
    second_held, late_held, second_y, early_side_held = tied(
        (second_held, [near[step] for step in late], second_y, [side[step] for step in early[1:]]),
        stage,
    )
    for step, value in zip(early[1:], early_side_held):
        side[step] = value
    for step, value in zip(late, late_held):
        near[step] = value
        side[step] = over_columns(value)
    second_c = over_pair(second_held)
    second_yc = over_pair(second_y)

    router_row = lax.dynamic_slice_in_dim(router, own, 1, 1).astype(F32).T
    all_first = jnp.concatenate([first_yc, first_c, first_y, first], axis=0)
    all_second = jnp.concatenate([second_yc, second_c, second_y, second], axis=0)
    hidden_units = 4 * units
    tile = 256 if hidden_units % 256 == 0 else hidden_units

    def gather_rows(steps):
        pieces = [near[step] for step in steps]
        for turn in range(columns - 1):
            pieces = pieces + [side[step][turn] for step in steps]
        return (
            jnp.concatenate([piece[0] for piece in pieces], axis=0),
            jnp.concatenate([piece[1] for piece in pieces], axis=0),
        )

    def front(rows_m, rows_d):
        count = rows_m.shape[0]
        return pl.pallas_call(
            functools.partial(front_kernel, tile),
            out_shape=[jax.ShapeDtypeStruct((count, hidden_units), BF16)] * 2
            + [
                jax.ShapeDtypeStruct((count, width), BF16),
                jax.ShapeDtypeStruct((count, 128), F32),
            ],
            in_specs=[VMEM] * 5,
            out_specs=[VMEM] * 4,
            compiler_params=PARAMS,
            cost_estimate=pl.CostEstimate(
                flops=4 * count * width * hidden_units,
                bytes_accessed=4 * width * hidden_units,
                transcendentals=count * hidden_units,
            ),
            name="front",
        )(rows_m, rows_d, all_first, all_second, router_row)

    def front_first(rows_m, rows_d):
        count = rows_m.shape[0]
        return pl.pallas_call(
            functools.partial(first_kernel, tile),
            out_shape=[
                jax.ShapeDtypeStruct((count, hidden_units), BF16),
                jax.ShapeDtypeStruct((count, hidden_units), F32),
                jax.ShapeDtypeStruct((count, width), BF16),
                jax.ShapeDtypeStruct((count, 128), F32),
            ],
            in_specs=[VMEM] * 4,
            out_specs=[VMEM] * 4,
            compiler_params=PARAMS,
            cost_estimate=pl.CostEstimate(
                flops=2 * count * width * hidden_units,
                bytes_accessed=2 * width * hidden_units,
                transcendentals=count * hidden_units,
            ),
            name="first",
        )(rows_m, rows_d, all_first, router_row)

    def front_second(rows_d, hidden, slope, gate):
        count = rows_d.shape[0]
        return pl.pallas_call(
            functools.partial(second_kernel, tile),
            out_shape=[
                jax.ShapeDtypeStruct((count, hidden_units), BF16),
                jax.ShapeDtypeStruct((count, 128), F32),
            ],
            in_specs=[VMEM] * 5,
            out_specs=[VMEM] * 2,
            compiler_params=PARAMS,
            cost_estimate=pl.CostEstimate(
                flops=2 * count * width * hidden_units,
                bytes_accessed=2 * width * hidden_units,
                transcendentals=0,
            ),
            name="second",
        )(rows_d, all_second, hidden, slope, gate)

    def row_gradients(rows_m, grad_pre, logit_gradient):
        count = grad_pre.shape[0] // columns
        return pl.pallas_call(
            functools.partial(rows_kernel, tile),
            out_shape=[
                jax.ShapeDtypeStruct((count, width), F32),
                jax.ShapeDtypeStruct((grad_pre.shape[0] - count, width), BF16),
                jax.ShapeDtypeStruct((8, width), F32),
            ],
            in_specs=[VMEM] * 5,
            out_specs=[VMEM] * 3,
            compiler_params=PARAMS,
            cost_estimate=pl.CostEstimate(
                flops=2 * grad_pre.shape[0] * width * hidden_units,
                bytes_accessed=2 * width * hidden_units,
                transcendentals=0,
            ),
            name="rows",
        )(rows_m, grad_pre, logit_gradient, all_first, router_row)

    def weight_half(half, left, right, kind):
        return pl.pallas_call(
            functools.partial(weight_kernel, half, tile),
            out_shape=jax.ShapeDtypeStruct((2 * units, width), kind),
            in_specs=[VMEM] * 2,
            out_specs=VMEM,
            scratch_shapes=[pltpu.VMEM((2 * units, left.shape[0]), BF16)],
            compiler_params=PARAMS,
            cost_estimate=pl.CostEstimate(
                flops=4 * left.shape[0] * width * units,
                bytes_accessed=8 * width * units,
                transcendentals=0,
            ),
            name="weights",
        )(left, right)

    early_m, early_d = gather_rows(early)
    early_hidden, early_pre, early_y, early_logit = front(early_m, early_d)
    early_own, early_side, early_sums = row_gradients(early_m, early_pre, early_logit)
    for step in late:
        near[step], side[step] = tied((near[step], side[step]), (early_own, early_side))
    late_m, late_d = gather_rows(late)

    def pairwise(value, name, size, bit):
        return value + lax.ppermute(value, name, [(i, i ^ bit) for i in range(size)])

    late_hidden, late_slope, late_y, late_gate = front_first(late_m, late_d)
    hidden = jnp.concatenate([early_hidden, late_hidden], axis=0)
    grad_y = jnp.concatenate([early_y, late_y], axis=0)
    out_leave = weight_half(0, hidden, grad_y, BF16)
    out_pair = over_pair(out_leave)
    late_pre, late_logit = front_second(
        tied(late_d, out_leave), late_hidden, late_slope, late_gate
    )
    late_own, late_side, late_sums = row_gradients(late_m, late_pre, late_logit)
    sums = early_sums + late_sums
    line = jnp.arange(-(-(experts + 1) // 8) * 8, dtype=jnp.int32)[:, None]
    total = jnp.where(line == own, sums[:1], jnp.where(line == experts, sums[1:2], 0.0))
    hidden = tied(hidden, total)
    total = pairwise(total, "expert", halves, 1)
    out_stay = weight_half(1, hidden, grad_y, F32)
    rows_m = jnp.concatenate([early_m, late_m], axis=0)
    grad_pre = jnp.concatenate([early_pre, late_pre], axis=0)
    in_leave = weight_half(0, tied(grad_pre, out_stay), rows_m, BF16)

    stage = (out_pair, out_stay, total, late_own, late_side, in_leave)
    out_pair, out_stay, total, late_side, early_side, in_leave, grad_pre = tied(
        (out_pair, out_stay, total, late_side, early_side, in_leave, grad_pre), stage
    )
    out_sum = out_stay + out_pair.astype(F32)
    out_half = out_sum[:units].astype(BF16)
    out_other = over_half(out_half)

    def by_turn(rows):
        return rows.reshape(columns - 1, -1, width)

    leaving = jnp.concatenate([by_turn(early_side), by_turn(late_side)], axis=1)
    rows_back = [
        lax.ppermute(leaving[turn - 1], "dp", turn_columns(columns - turn))
        for turn in range(1, columns)
    ]
    in_pair = over_pair(in_leave)
    in_stay = weight_half(1, tied(grad_pre, (out_half, leaving)), rows_m, F32)
    total = tied(total, in_stay)
    bit = 2
    while bit < halves:
        total = pairwise(total, "expert", halves, bit)
        bit *= 2
    total = pairwise(total, "dp", groups, 1)

    stage = (out_other, rows_back, in_pair, in_stay, total)
    out_other, rows_back, in_pair, in_stay, total = tied(stage, stage)
    in_sum = in_stay + in_pair.astype(F32)
    in_other = over_half(in_sum[:units].astype(BF16))
    own_rows = jnp.concatenate([early_own, late_own], axis=0)
    for piece in rows_back:
        own_rows = own_rows + piece.astype(F32)
    own_rows = own_rows.astype(BF16).reshape(experts, capacity, width)
    returned = [None] * experts
    for place, step in enumerate(steps):
        value = own_rows[place]
        returned[step] = over_experts(value, experts - step) if step else value
    bit = 2
    while bit < groups:
        total = pairwise(total, "dp", groups, bit)
        bit *= 2
    grad_router = total[:experts].T
    grad_gain = total[experts] / gain
    grad_out = (out_sum[units:] + out_other.astype(F32)).astype(BF16)[None]
    grad_in = (in_sum[units:] + in_other.astype(F32)).astype(BF16).T[None]
    returned = tied(returned, (in_other, grad_out))

    input_grad = pl.pallas_call(
        functools.partial(combine_kernel, experts, capacity),
        out_shape=jax.ShapeDtypeStruct((tokens, width), BF16),
        in_specs=[SMEM, VMEM, VMEM, VMEM, VMEM, VMEM],
        out_specs=VMEM,
        compiler_params=PARAMS,
        name="combine",
    )(*token_args, jnp.concatenate(returned, axis=0))
    return (input_grad, grad_in, grad_out, grad_router, grad_gain)


def solution(mesh):
    in_specs = (
        P(("expert", "dp"), None),
        P(),
        P(),
        P(("expert", "dp"), None),
        P("expert", None, "dp"),
        P("expert", "dp", None),
        P(("expert", "dp"), None),
    )
    out_specs = (
        P(("expert", "dp"), None),
        P("expert", None, "dp"),
        P("expert", "dp", None),
        P(),
        P(),
    )
    return jax.shard_map(body, mesh=mesh, in_specs=in_specs, out_specs=out_specs, check_vma=False)
```

```python
import functools
import math

import jax
import jax.numpy as jnp
from jax import lax
from jax.experimental import pallas as pl
from jax.experimental.pallas import tpu as pltpu
from jax.sharding import PartitionSpec as P

F32 = jnp.float32
BF16 = jnp.bfloat16
VMEM = pl.BlockSpec(memory_space=pltpu.VMEM)
SMEM = pl.BlockSpec(memory_space=pltpu.SMEM)
ANY = pl.BlockSpec(memory_space=pl.ANY)
PARAMS = pltpu.CompilerParams(vmem_limit_bytes=40 * 2**20)


def gelu_parts(pre):
    coeff = math.sqrt(2.0 / math.pi)
    inner = coeff * (pre + 0.044715 * pre * pre * pre)
    tanh_val = jnp.tanh(inner)
    value = 0.5 * pre * (1.0 + tanh_val)
    slope = 0.5 * (1.0 + tanh_val) + 0.5 * pre * (1.0 - tanh_val * tanh_val) * coeff * (
        1.0 + 3.0 * 0.044715 * pre * pre
    )
    return (value, slope)


def dot(a, b, a_dim, b_dim):
    return lax.dot_general(a, b, (((a_dim,), (b_dim,)), ((), ())), preferred_element_type=F32)


def spans(total, size=256):
    return [(at, min(size, total - at)) for at in range(0, total, size)]


def norm_pieces(block):
    values = block.astype(F32)
    centred_rows = values - jnp.mean(values, axis=1, keepdims=True)
    inverse_deviation = lax.rsqrt(
        jnp.mean(centred_rows * centred_rows, axis=1, keepdims=True) + 1e-06
    )
    return centred_rows * inverse_deviation, inverse_deviation


def slot_of(own, routes, experts, capacity):
    top, tokens = routes.shape
    relative = routes - own
    relative = jnp.where(relative < 0, relative + experts, relative)
    lanes = max(16, experts)
    expert = lax.broadcasted_iota(jnp.int32, (lanes, tokens), 0)
    picks = [expert == relative[j : j + 1, :] for j in range(top)]
    chosen = sum(jnp.where(pick, 1.0, 0.0) for pick in picks)
    earlier = lax.broadcasted_iota(jnp.int32, (tokens, tokens), 0) < lax.broadcasted_iota(
        jnp.int32, (tokens, tokens), 1
    )
    before = dot(chosen.astype(BF16), jnp.where(earlier, 1.0, 0.0).astype(BF16), 1, 0)
    return [
        relative[j : j + 1, :] * capacity
        + jnp.sum(jnp.where(pick, before, 0.0), axis=0, keepdims=True).astype(jnp.int32)
        for j, pick in enumerate(picks)
    ]


def place_matrix(slots, first, count, tokens):
    row = lax.broadcasted_iota(jnp.int32, (count, tokens), 0) + first
    hit = slots[0] == row
    for slot in slots[1:]:
        hit = hit | (slot == row)
    return jnp.where(hit, 1.0, 0.0).astype(BF16)


def dispatch_kernel(experts, capacity, own_ref, x_hbm, gain_ref, routes_ref, d_hbm, *refs):
    send_refs, (x_ref, d_ref, sems) = refs[:experts], refs[experts:]
    x_copy = pltpu.make_async_copy(x_hbm, x_ref, sems.at[0])
    d_copy = pltpu.make_async_copy(d_hbm, d_ref, sems.at[1])
    x_copy.start()
    d_copy.start()
    tokens = x_ref.shape[0]
    slots = slot_of(own_ref[0], routes_ref[...], experts, capacity)
    x_copy.wait()
    normalized_rows, _ = norm_pieces(x_ref[...])
    mixed_rows = (normalized_rows * gain_ref[...]).astype(BF16)
    d_copy.wait()
    cotangent = d_ref[...]
    for step in range(experts):
        places = place_matrix(slots, step * capacity, capacity, tokens)
        send_refs[step][0] = dot(places, mixed_rows, 1, 0).astype(BF16)
        send_refs[step][1] = dot(places, cotangent, 1, 0).astype(BF16)


def prepare_kernel(experts, capacity, own_ref, x_ref, routes_ref, norm_ref, deviation_ref, places_ref):
    normalized_rows, inverse_deviation = norm_pieces(x_ref[...])
    norm_ref[...] = normalized_rows
    deviation_ref[...] = jnp.broadcast_to(inverse_deviation, deviation_ref.shape)
    slots = slot_of(own_ref[0], routes_ref[...], experts, capacity)
    places_ref[...] = place_matrix(slots, 0, experts * capacity, x_ref.shape[0])


def finish_kernel(
    norm_ref, deviation_ref, places_ref, gain_ref, d_ref, rows_ref, stay_ref, pair_ref, other_ref, *refs
):
    out_ref, sum_ref, router_ref, gain_grad_ref = refs[-4:]
    sum_ref[...] = (
        stay_ref[...] + pair_ref[...].astype(F32) + other_ref[...].astype(F32)
    ).astype(BF16)
    normalized_rows = norm_ref[...]
    scaled_rows = dot(places_ref[...], rows_ref[...], 0, 0) * gain_ref[...]
    mean_first_term = jnp.mean(scaled_rows, axis=1, keepdims=True)
    mean_second_term = jnp.mean(scaled_rows * normalized_rows, axis=1, keepdims=True)
    norm_backward = deviation_ref[:, :1] * (
        scaled_rows - mean_first_term - normalized_rows * mean_second_term
    )
    out_ref[...] = (d_ref[...].astype(F32) + norm_backward).astype(BF16)
    parts = [ref[...] for ref in refs[:-4]]
    while len(parts) > 1:
        parts = [parts[i] + parts[i + 1] for i in range(0, len(parts), 2)]
    experts = router_ref.shape[0]
    router_ref[...] = parts[0][:experts]
    gain_grad_ref[...] = jnp.sum(parts[0][experts:], axis=0, keepdims=True) / gain_ref[...]


def first_kernel(m_ref, d_ref, first_ref, router_ref, hidden_ref, slope_ref, y_ref, gate_ref):
    rows_m = m_ref[...]
    gate = jax.nn.sigmoid(jnp.sum(rows_m.astype(F32) * router_ref[...], axis=1, keepdims=True))
    y_ref[...] = (gate * d_ref[...].astype(F32)).astype(BF16)
    gate_ref[...] = jnp.broadcast_to(gate, gate_ref.shape)
    for at, size in spans(first_ref.shape[0]):
        units = pl.ds(at, size)
        value, slope = gelu_parts(dot(rows_m, first_ref[units, :], 1, 1))
        hidden_ref[:, units] = value.astype(BF16)
        slope_ref[:, units] = gate * slope


def second_kernel(d_ref, second_ref, hidden_ref, slope_ref, gate_ref, pre_ref, logit_ref):
    rows_d = d_ref[...]
    gate = gate_ref[:, :1]
    share = jnp.zeros_like(gate)
    for at, size in spans(second_ref.shape[0]):
        units = pl.ds(at, size)
        back = dot(rows_d, second_ref[units, :], 1, 1)
        pre_ref[:, units] = (back * slope_ref[:, units]).astype(BF16)
        share = share + jnp.sum(hidden_ref[:, units].astype(F32) * back, axis=1, keepdims=True)
    logit_ref[...] = jnp.broadcast_to(share * gate * (1.0 - gate), logit_ref.shape)


def rows_kernel(m_ref, pre_ref, logit_ref, first_ref, router_ref, own_ref, side_ref, sums_ref):
    count = own_ref.shape[0]
    pre = pre_ref[...]
    logit = logit_ref[:, :1]
    for at, size in spans(first_ref.shape[1]):
        lanes = pl.ds(at, size)
        rows = dot(pre, first_ref[:, lanes], 1, 0) + logit * router_ref[:, lanes]
        own_ref[:, lanes] = rows[:count]
        side_ref[:, lanes] = rows[count:].astype(BF16)
        rows_m = m_ref[:, lanes].astype(F32)
        router_part = jnp.sum(rows_m * logit, axis=0, keepdims=True)
        gain_part = jnp.sum(rows_m * rows, axis=0, keepdims=True)
        row = lax.broadcasted_iota(jnp.int32, (sums_ref.shape[0], size), 0)
        sums_ref[:, lanes] = jnp.where(row == 0, router_part, jnp.where(row == 1, gain_part, 0.0))


def weight_kernel(first, left_ref, right_ref, out_ref, turned):
    units = out_ref.shape[0]
    low = first // 128 * 128
    high = -(-(first + units) // 128) * 128
    turned[...] = left_ref[:, low:high].T
    for at, size in spans(right_ref.shape[1]):
        lanes = pl.ds(at, size)
        out_ref[:, lanes] = dot(
            turned[first - low : first - low + units, :], right_ref[:, lanes], 1, 0
        ).astype(out_ref.dtype)


def join_kernel(*refs):
    at = 0
    for ref in refs[:-1]:
        refs[-1][at : at + ref.shape[0], :] = ref[...]
        at += ref.shape[0]


def half_kernel(stay_ref, pair_ref, out_ref):
    out_ref[...] = (stay_ref[...] + pair_ref[...].astype(F32)).astype(BF16)


def tied(values, after):
    held, _ = lax.optimization_barrier((values, after))
    return held


def shape(kind, *sizes):
    return jax.ShapeDtypeStruct(sizes, kind)


def call(kernel, name, outs, args, flops=0, specs=None, scratch=()):
    return pl.pallas_call(
        kernel,
        out_shape=outs,
        in_specs=specs or [VMEM] * len(args),
        out_specs=jax.tree.map(lambda _: VMEM, outs),
        scratch_shapes=list(scratch),
        compiler_params=PARAMS,
        cost_estimate=pl.CostEstimate(flops=flops, bytes_accessed=flops // 512, transcendentals=0),
        name=name,
    )(*args)


def body(prenorm_input, gain, router, routes, w_in, w_out, cotangent):
    halves = lax.axis_size("expert")
    experts = halves // 2
    groups = lax.axis_size("dp")
    columns = groups // 2
    tokens, width = prenorm_input.shape
    top = routes.shape[1]
    capacity = max(2, 5 * tokens * top // (4 * experts))
    slots = experts * capacity
    own = lax.axis_index("expert") // 2

    def over_half(value):
        return lax.ppermute(value, "expert", [(i, i ^ 1) for i in range(halves)])

    def over_pair(value):
        return lax.ppermute(value, "dp", [(i, i ^ 1) for i in range(groups)])

    def over_columns(value):
        return [
            lax.ppermute(value, "dp", [(i, (i + 2 * step) % groups) for i in range(groups)])
            for step in range(1, columns)
        ]

    def back_over_columns(values):
        return [
            lax.ppermute(value, "dp", [(i, (i - 2 * step) % groups) for i in range(groups)])
            for step, value in enumerate(values, 1)
        ]

    def over_experts(value, step):
        return lax.ppermute(value, "expert", [(i, (i + 2 * step) % halves) for i in range(halves)])

    def over_groups(value):
        return [value] + [
            lax.ppermute(value, "dp", [(i, i ^ bit) for i in range(groups)]) for bit in range(1, groups)
        ]

    first = w_in[0].T
    second = w_out[0]
    units = first.shape[0]
    hidden_units = 4 * units

    own_scalar = own.astype(jnp.int32).reshape(1)
    gain_row = gain[None, :]
    routes_t = routes.T
    send = call(
        functools.partial(dispatch_kernel, experts, capacity),
        "dispatch",
        [shape(BF16, 2, capacity, width)] * experts,
        (own_scalar, prenorm_input, gain_row, routes_t, cotangent),
        flops=4 * slots * tokens * width,
        specs=[SMEM, ANY, VMEM, VMEM, ANY],
        scratch=[
            pltpu.VMEM((tokens, width), BF16),
            pltpu.VMEM((tokens, width), BF16),
            pltpu.SemaphoreType.DMA((2,)),
        ],
    )

    steps = sorted(range(experts), key=lambda step: min(step, experts - step))
    quarter = experts // 4
    early, late = steps[: 3 * quarter], steps[3 * quarter :]
    near = {0: send[0]}
    for step in early[1:]:
        near[step] = over_experts(send[step], step)
    side = {0: over_columns(send[0])}
    first_y = over_half(tied(first, send[0]))
    first_c = over_pair(tied(first, send[0]))

    stage = (first_y, first_c, [near[step] for step in early], side[0])
    second_held, late_held, early_held, first_y, side[0] = tied(
        (second, [send[step] for step in late], [near[step] for step in early], first_y, side[0]),
        stage,
    )
    for step, value in zip(late, late_held):
        near[step] = over_experts(value, step)
    for step, value in zip(early, early_held):
        near[step] = value
        if step:
            side[step] = over_columns(value)
    second_y = over_half(second_held)
    first_yc = over_pair(first_y)
    prepared = call(
        functools.partial(prepare_kernel, experts, capacity),
        "prepare",
        [shape(F32, tokens, width), shape(F32, tokens, 128), shape(BF16, slots, tokens)],
        (own_scalar, prenorm_input, routes_t),
        specs=[SMEM, VMEM, VMEM],
    )

    stage = (
        second_y,
        first_yc,
        [near[step] for step in late],
        [side[step] for step in early[1:]],
        prepared,
    )
    late_held, second_held, second_y, early_held, first_yc, prepared = tied(
        (
            [near[step] for step in late],
            second_held,
            second_y,
            [side[step] for step in early[1:]],
            first_yc,
            prepared,
        ),
        stage,
    )
    for step, value in zip(early[1:], early_held):
        side[step] = value
    for step, value in zip(late, late_held):
        near[step] = value
        side[step] = over_columns(value)
    second_c = over_pair(second_held)
    second_yc = over_pair(second_y)

    def join(*parts):
        return call(join_kernel, "join", shape(BF16, hidden_units, width), parts)

    all_first = join(first_yc, first_c, first_y, first)
    all_second = join(second_yc, second_c, second_y, second_held)

    router_row = lax.dynamic_slice_in_dim(router, own, 1, 1).astype(F32).T

    def gather_rows(chosen):
        pieces = [near[step] for step in chosen]
        for turn in range(columns - 1):
            pieces = pieces + [side[step][turn] for step in chosen]
        return (
            jnp.concatenate([piece[0] for piece in pieces], axis=0),
            jnp.concatenate([piece[1] for piece in pieces], axis=0),
        )

    def first_product(rows_m, rows_d):
        count = rows_m.shape[0]
        return call(
            first_kernel,
            "first",
            [
                shape(BF16, count, hidden_units),
                shape(F32, count, hidden_units),
                shape(BF16, count, width),
                shape(F32, count, 128),
            ],
            (rows_m, rows_d, all_first, router_row),
            flops=2 * count * width * hidden_units,
        )

    def second_product(rows_d, hidden, slope, gate):
        count = rows_d.shape[0]
        return call(
            second_kernel,
            "second",
            [shape(BF16, count, hidden_units), shape(F32, count, 128)],
            (rows_d, all_second, hidden, slope, gate),
            flops=2 * count * width * hidden_units,
        )

    def row_gradients(rows_m, grad_pre, logit_gradient):
        count = grad_pre.shape[0]
        return call(
            rows_kernel,
            "rows",
            [
                shape(F32, count // columns, width),
                shape(BF16, count - count // columns, width),
                shape(F32, 8, width),
            ],
            (rows_m, grad_pre, logit_gradient, all_first, router_row),
            flops=2 * count * width * hidden_units,
        )

    def weight_gradient(at, blocks, left, right, kind):
        low = at * units // 128 * 128
        high = -(-(at + blocks) * units // 128) * 128
        return call(
            functools.partial(weight_kernel, at * units),
            "weights",
            shape(kind, blocks * units, width),
            (left, right),
            flops=2 * left.shape[0] * width * blocks * units,
            scratch=[pltpu.VMEM((high - low, left.shape[0]), BF16)],
        )

    def half_sum(stay, pair):
        return call(half_kernel, "half", shape(BF16, units, width), (stay, pair))

    early_m, early_d = gather_rows(early)
    early_hidden, early_slope, early_y, early_gate = first_product(early_m, early_d)
    early_pre, early_logit = second_product(early_d, early_hidden, early_slope, early_gate)
    early_own, early_side, early_sums = row_gradients(early_m, early_pre, early_logit)
    for step in late:
        near[step], side[step] = tied((near[step], side[step]), (early_own, early_side))
    late_m, late_d = gather_rows(late)

    block = quarter * capacity

    def by_turn(rows):
        return rows.reshape(columns - 1, -1, width)

    early_side = by_turn(early_side)

    moved = back_over_columns(list(early_side[:, block : 2 * block]))
    late_hidden, late_slope, late_y, late_gate = first_product(late_m, late_d)
    hidden = jnp.concatenate([early_hidden, late_hidden], axis=0)
    grad_y = jnp.concatenate([early_y, late_y], axis=0)
    out_leave = weight_gradient(0, 1, hidden, grad_y, BF16)
    out_pair = over_pair(out_leave)
    hidden = tied(hidden, out_leave)
    out_stay = weight_gradient(2, 1, hidden, grad_y, F32)
    late_pre, late_logit = second_product(tied(late_d, out_stay), late_hidden, late_slope, late_gate)
    late_own, late_side, late_sums = row_gradients(late_m, late_pre, late_logit)
    sums = early_sums + late_sums
    line = jnp.arange(2 * experts, dtype=jnp.int32)[:, None]
    total = jnp.where(line == own, sums[:1], jnp.where(line == experts + own, sums[1:2], 0.0))
    total = total + over_half(total)
    out_half = half_sum(out_stay, out_pair)

    stage = (out_half, total, late_own, late_side, moved)
    out_half, total, late_side, moved, hidden = tied((out_half, total, late_side, moved, hidden), stage)
    out_other = over_half(out_half)
    late_side = by_turn(late_side)
    leaving = jnp.concatenate([early_side[:, :block], early_side[:, 2 * block :], late_side], axis=1)
    rows_back = back_over_columns(list(leaving))

    def add_rows(own_rows, pieces):
        for piece in pieces:
            own_rows = own_rows + piece.astype(F32)
        return own_rows.astype(BF16).reshape(-1, capacity, width)

    returned = [None] * experts

    def send_back(chosen, rows):
        for step, value in zip(chosen, rows):
            returned[step] = over_experts(value, experts - step) if step else value

    moved_steps = steps[quarter : 2 * quarter]
    other_steps = steps[:quarter] + steps[2 * quarter :]
    send_back(moved_steps, add_rows(early_own[block : 2 * block], moved))
    rows_m = jnp.concatenate([early_m, late_m], axis=0)
    grad_pre = jnp.concatenate([early_pre, late_pre], axis=0)
    total = tied(total, (out_half, leaving))
    totals = [total] + [over_experts(total, step) for step in range(1, experts)]
    grad_pre = tied(grad_pre, (out_half, leaving))
    in_leave = weight_gradient(0, 1, grad_pre, rows_m, BF16)
    in_pair = over_pair(in_leave)
    in_stay = weight_gradient(2, 1, tied(grad_pre, in_leave), rows_m, F32)
    hidden, grad_pre = tied((hidden, grad_pre), in_stay)
    out_rest = over_pair(weight_gradient(1, 1, hidden, grad_y, BF16))
    out_mine = weight_gradient(3, 1, hidden, grad_y, F32)
    in_rest = over_pair(weight_gradient(1, 1, grad_pre, rows_m, BF16))
    in_mine = weight_gradient(3, 1, grad_pre, rows_m, F32)

    moved_back = [returned[step] for step in moved_steps]
    stage = (out_other, rows_back, in_pair, in_stay, totals, moved_back)
    out_other, rows_back, in_pair, in_stay, totals, moved_back = tied(stage, stage)
    for step, value in zip(moved_steps, moved_back):
        returned[step] = value
    in_other = over_half(half_sum(in_stay, in_pair))
    own_rows = jnp.concatenate([early_own[:block], early_own[2 * block :], late_own], axis=0)
    send_back(other_steps, add_rows(own_rows, rows_back))
    totals = over_groups(sum(totals[1:], totals[0]))
    grad_out = (out_mine + out_rest.astype(F32) + out_other.astype(F32)).astype(BF16)[None]

    returned = tied(returned, (in_other, grad_out))
    norm, deviation, places = prepared
    input_grad, grad_in, grad_router, grad_gain = call(
        finish_kernel,
        "finish",
        [
            shape(BF16, tokens, width),
            shape(BF16, units, width),
            shape(F32, experts, width),
            shape(F32, 1, width),
        ],
        (
            norm,
            deviation,
            places,
            gain_row,
            cotangent,
            jnp.concatenate(returned, axis=0),
            in_mine,
            in_rest,
            in_other,
            *totals,
        ),
    )
    return (input_grad, grad_in.T[None], grad_out, grad_router.T, grad_gain[0])


def solution(mesh):
    in_specs = (
        P(("expert", "dp"), None),
        P(),
        P(),
        P(("expert", "dp"), None),
        P("expert", None, "dp"),
        P("expert", "dp", None),
        P(("expert", "dp"), None),
    )
    out_specs = (
        P(("expert", "dp"), None),
        P("expert", None, "dp"),
        P("expert", "dp", None),
        P(),
        P(),
    )
    return jax.shard_map(body, mesh=mesh, in_specs=in_specs, out_specs=out_specs, check_vma=False)
```

```python
import functools
import math

import jax
import jax.numpy as jnp
from jax import lax
from jax.experimental import pallas as pl
from jax.experimental.pallas import tpu as pltpu
from jax.sharding import PartitionSpec as P

F32 = jnp.float32
BF16 = jnp.bfloat16
VMEM = pl.BlockSpec(memory_space=pltpu.VMEM)
SMEM = pl.BlockSpec(memory_space=pltpu.SMEM)
ANY = pl.BlockSpec(memory_space=pl.ANY)


def gelu_parts(pre):
    coeff = math.sqrt(2.0 / math.pi)
    inner = coeff * (pre + 0.044715 * pre * pre * pre)
    tanh_val = jnp.tanh(inner)
    value = 0.5 * pre * (1.0 + tanh_val)
    slope = 0.5 * (1.0 + tanh_val) + 0.5 * pre * (1.0 - tanh_val * tanh_val) * coeff * (
        1.0 + 3.0 * 0.044715 * pre * pre
    )
    return (value, slope)


def dot(a, b, a_dim, b_dim):
    return lax.dot_general(a, b, (((a_dim,), (b_dim,)), ((), ())), preferred_element_type=F32)


def spans(total, size=256):
    return [(at, min(size, total - at)) for at in range(0, total, size)]


def norm_pieces(block):
    values = block.astype(F32)
    centred_rows = values - jnp.mean(values, axis=1, keepdims=True)
    inverse_deviation = lax.rsqrt(
        jnp.mean(centred_rows * centred_rows, axis=1, keepdims=True) + 1e-06
    )
    return centred_rows * inverse_deviation, inverse_deviation


def slot_of(own, routes, experts, capacity):
    top, tokens = routes.shape
    relative = routes - own
    relative = jnp.where(relative < 0, relative + experts, relative)
    lanes = max(16, experts)
    expert = lax.broadcasted_iota(jnp.int32, (lanes, tokens), 0)
    picks = [expert == relative[j : j + 1, :] for j in range(top)]
    chosen = sum(jnp.where(pick, 1.0, 0.0) for pick in picks)
    earlier = lax.broadcasted_iota(jnp.int32, (tokens, tokens), 0) < lax.broadcasted_iota(
        jnp.int32, (tokens, tokens), 1
    )
    before = dot(chosen.astype(BF16), jnp.where(earlier, 1.0, 0.0).astype(BF16), 1, 0)
    return [
        relative[j : j + 1, :] * capacity
        + jnp.sum(jnp.where(pick, before, 0.0), axis=0, keepdims=True).astype(jnp.int32)
        for j, pick in enumerate(picks)
    ]


def place_matrix(slots, first, count, tokens):
    row = lax.broadcasted_iota(jnp.int32, (count, tokens), 0) + first
    hit = slots[0] == row
    for slot in slots[1:]:
        hit = hit | (slot == row)
    return jnp.where(hit, 1.0, 0.0).astype(BF16)


def dispatch_kernel(experts, capacity, own_ref, x_hbm, gain_ref, routes_ref, d_hbm, *refs):
    send_refs, (x_ref, d_ref, sems) = refs[:experts], refs[experts:]
    x_copy = pltpu.make_async_copy(x_hbm, x_ref, sems.at[0])
    d_copy = pltpu.make_async_copy(d_hbm, d_ref, sems.at[1])
    x_copy.start()
    d_copy.start()
    tokens = x_ref.shape[0]
    slots = slot_of(own_ref[0], routes_ref[...], experts, capacity)
    x_copy.wait()
    normalized_rows, _ = norm_pieces(x_ref[...])
    mixed_rows = (normalized_rows * gain_ref[...][None, :]).astype(BF16)
    d_copy.wait()
    cotangent = d_ref[...]
    for step in range(experts):
        places = place_matrix(slots, step * capacity, capacity, tokens)
        send_refs[step][0] = dot(places, mixed_rows, 1, 0).astype(BF16)
        send_refs[step][1] = dot(places, cotangent, 1, 0).astype(BF16)


def prepare_kernel(experts, capacity, own_ref, x_ref, routes_ref, norm_ref, deviation_ref, places_ref):
    normalized_rows, inverse_deviation = norm_pieces(x_ref[...])
    norm_ref[...] = normalized_rows
    deviation_ref[...] = jnp.broadcast_to(inverse_deviation, deviation_ref.shape)
    slots = slot_of(own_ref[0], routes_ref[...], experts, capacity)
    places_ref[...] = place_matrix(slots, 0, experts * capacity, x_ref.shape[0])


def finish_kernel(
    norm_ref, deviation_ref, places_ref, gain_ref, d_ref, rows_ref, stay_ref, pair_ref, other_ref,
    total_ref, last_ref, out_ref, sum_ref, router_ref, gain_grad_ref
):
    sum_ref[...] = (
        stay_ref[...] + pair_ref[...].astype(F32) + other_ref[...].astype(F32)
    ).astype(BF16)
    normalized_rows = norm_ref[...]
    scaled_rows = dot(places_ref[...], rows_ref[...], 0, 0) * gain_ref[...][None, :]
    mean_first_term = jnp.mean(scaled_rows, axis=1, keepdims=True)
    mean_second_term = jnp.mean(scaled_rows * normalized_rows, axis=1, keepdims=True)
    norm_backward = deviation_ref[:, :1] * (
        scaled_rows - mean_first_term - normalized_rows * mean_second_term
    )
    out_ref[...] = (d_ref[...].astype(F32) + norm_backward).astype(BF16)
    experts = router_ref.shape[0]
    total = total_ref[...] + last_ref[...]
    router_ref[...] = total[:experts]
    gain_grad_ref[...] = jnp.sum(total[experts:], axis=0) / gain_ref[...]


def first_kernel(m_ref, d_ref, first_ref, router_ref, hidden_ref, slope_ref, y_ref, gate_ref):
    rows_m = m_ref[...]
    gate = jax.nn.sigmoid(jnp.sum(rows_m.astype(F32) * router_ref[...], axis=1, keepdims=True))
    y_ref[...] = (gate * d_ref[...].astype(F32)).astype(BF16)
    gate_ref[...] = jnp.broadcast_to(gate, gate_ref.shape)
    for at, size in spans(first_ref.shape[0]):
        units = pl.ds(at, size)
        value, slope = gelu_parts(dot(rows_m, first_ref[units, :], 1, 1))
        hidden_ref[:, units] = value.astype(BF16)
        slope_ref[:, units] = gate * slope


def second_kernel(d_ref, second_ref, hidden_ref, slope_ref, gate_ref, pre_ref, logit_ref):
    rows_d = d_ref[...]
    gate = gate_ref[:, :1]
    share = jnp.zeros_like(gate)
    for at, size in spans(second_ref.shape[0]):
        units = pl.ds(at, size)
        back = dot(rows_d, second_ref[units, :], 1, 1)
        pre_ref[:, units] = (back * slope_ref[:, units]).astype(BF16)
        share = share + jnp.sum(hidden_ref[:, units].astype(F32) * back, axis=1, keepdims=True)
    logit_ref[...] = jnp.broadcast_to(share * gate * (1.0 - gate), logit_ref.shape)


def rows_kernel(m_ref, pre_ref, logit_ref, first_ref, router_ref, own_ref, side_ref, sums_ref):
    count = own_ref.shape[0]
    pre = pre_ref[...]
    logit = logit_ref[:, :1]
    for at, size in spans(first_ref.shape[1]):
        lanes = pl.ds(at, size)
        rows = dot(pre, first_ref[:, lanes], 1, 0) + logit * router_ref[:, lanes]
        own_ref[:, lanes] = rows[:count]
        side_ref[:, lanes] = rows[count:].astype(BF16)
        rows_m = m_ref[:, lanes].astype(F32)
        router_part = jnp.sum(rows_m * logit, axis=0, keepdims=True)
        gain_part = jnp.sum(rows_m * rows, axis=0, keepdims=True)
        row = lax.broadcasted_iota(jnp.int32, (sums_ref.shape[0], size), 0)
        sums_ref[:, lanes] = jnp.where(row == 0, router_part, jnp.where(row == 1, gain_part, 0.0))


def weight_kernel(first, left_ref, right_ref, out_ref, turned):
    units = out_ref.shape[0]
    low = first // 128 * 128
    high = -(-(first + units) // 128) * 128
    turned[...] = left_ref[:, low:high].T
    for at, size in spans(right_ref.shape[1]):
        lanes = pl.ds(at, size)
        out_ref[:, lanes] = dot(
            turned[first - low : first - low + units, :], right_ref[:, lanes], 1, 0
        ).astype(out_ref.dtype)


def join_kernel(*refs):
    at = 0
    for ref in refs[:-1]:
        refs[-1][at : at + ref.shape[0], :] = ref[...]
        at += ref.shape[0]


def half_kernel(stay_ref, pair_ref, out_ref):
    out_ref[...] = (stay_ref[...] + pair_ref[...].astype(F32)).astype(BF16)


def tied(values, after):
    held, _ = lax.optimization_barrier((values, after))
    return held


def shape(kind, *sizes):
    return jax.ShapeDtypeStruct(sizes, kind)


def call(kernel, name, outs, args, flops=0, specs=None, scratch=(), mebibytes=18):
    return pl.pallas_call(
        kernel,
        out_shape=outs,
        in_specs=specs or [VMEM] * len(args),
        out_specs=jax.tree.map(lambda _: VMEM, outs),
        scratch_shapes=list(scratch),
        compiler_params=pltpu.CompilerParams(vmem_limit_bytes=mebibytes * 2**20),
        cost_estimate=pl.CostEstimate(flops=flops, bytes_accessed=flops // 512, transcendentals=0),
        name=name,
    )(*args)


def body(prenorm_input, gain, router, routes, w_in, w_out, cotangent):
    halves = lax.axis_size("expert")
    experts = halves // 2
    groups = lax.axis_size("dp")
    columns = groups // 2
    tokens, width = prenorm_input.shape
    top = routes.shape[1]
    capacity = max(2, 5 * tokens * top // (4 * experts))
    slots = experts * capacity
    own = lax.axis_index("expert") // 2

    def over_half(value):
        return lax.ppermute(value, "expert", [(i, i ^ 1) for i in range(halves)])

    def over_pair(value):
        return lax.ppermute(value, "dp", [(i, i ^ 1) for i in range(groups)])

    def over_columns(value):
        return [
            lax.ppermute(value, "dp", [(i, (i + 2 * step) % groups) for i in range(groups)])
            for step in range(1, columns)
        ]

    def back_over_columns(values):
        return [
            lax.ppermute(value, "dp", [(i, (i - 2 * step) % groups) for i in range(groups)])
            for step, value in enumerate(values, 1)
        ]

    def over_experts(value, step):
        return lax.ppermute(value, "expert", [(i, (i + 2 * step) % halves) for i in range(halves)])

    def pairwise(value, name, size, bit):
        return value + lax.ppermute(value, name, [(i, i ^ bit) for i in range(size)])

    first = w_in[0].T
    second = w_out[0]
    units = first.shape[0]
    hidden_units = 4 * units

    own_scalar = own.astype(jnp.int32).reshape(1)
    routes_t = routes.T
    send = call(
        functools.partial(dispatch_kernel, experts, capacity),
        "dispatch",
        [shape(BF16, 2, capacity, width)] * experts,
        (own_scalar, prenorm_input, gain, routes_t, cotangent),
        flops=4 * slots * tokens * width,
        specs=[SMEM, ANY, VMEM, VMEM, ANY],
        scratch=[
            pltpu.VMEM((tokens, width), BF16),
            pltpu.VMEM((tokens, width), BF16),
            pltpu.SemaphoreType.DMA((2,)),
        ],
        mebibytes=60,
    )

    steps = sorted(range(experts), key=lambda step: min(step, experts - step))
    quarter = experts // 4
    early, late = steps[: 3 * quarter], steps[3 * quarter :]
    near = {0: send[0]}
    for step in early[1:]:
        near[step] = over_experts(send[step], step)
    side = {0: over_columns(send[0])}
    first_y = over_half(tied(first, send[0]))
    first_c = over_pair(tied(first, send[0]))

    stage = (first_y, first_c, [near[step] for step in early], side[0])
    second_held, late_held, early_held, first_y, side[0] = tied(
        (second, [send[step] for step in late], [near[step] for step in early], first_y, side[0]),
        stage,
    )
    for step, value in zip(late, late_held):
        near[step] = over_experts(value, step)
    for step, value in zip(early, early_held):
        near[step] = value
        if step:
            side[step] = over_columns(value)
    second_y = over_half(second_held)
    first_yc = over_pair(first_y)
    prepared = call(
        functools.partial(prepare_kernel, experts, capacity),
        "prepare",
        [shape(F32, tokens, width), shape(F32, tokens, 128), shape(BF16, slots, tokens)],
        (own_scalar, prenorm_input, routes_t),
        specs=[SMEM, VMEM, VMEM],
    )

    stage = (
        second_y,
        first_yc,
        [near[step] for step in late],
        [side[step] for step in early[1:]],
        prepared,
    )
    late_held, second_held, second_y, early_held, first_yc, prepared = tied(
        (
            [near[step] for step in late],
            second_held,
            second_y,
            [side[step] for step in early[1:]],
            first_yc,
            prepared,
        ),
        stage,
    )
    for step, value in zip(early[1:], early_held):
        side[step] = value
    for step, value in zip(late, late_held):
        near[step] = value
        side[step] = over_columns(value)
    second_c = over_pair(second_held)
    second_yc = over_pair(second_y)

    def join(*parts):
        return call(join_kernel, "join", shape(BF16, hidden_units, width), parts)

    all_first = join(first_yc, first_c, first_y, first)
    all_second = join(second_yc, second_c, second_y, second_held)

    router_row = lax.dynamic_slice_in_dim(router, own, 1, 1).astype(F32).T

    def gather_rows(chosen):
        pieces = [near[step] for step in chosen]
        for turn in range(columns - 1):
            pieces = pieces + [side[step][turn] for step in chosen]
        return (
            jnp.concatenate([piece[0] for piece in pieces], axis=0),
            jnp.concatenate([piece[1] for piece in pieces], axis=0),
        )

    def first_product(rows_m, rows_d):
        count = rows_m.shape[0]
        return call(
            first_kernel,
            "first",
            [
                shape(BF16, count, hidden_units),
                shape(F32, count, hidden_units),
                shape(BF16, count, width),
                shape(F32, count, 128),
            ],
            (rows_m, rows_d, all_first, router_row),
            flops=2 * count * width * hidden_units,
        )

    def second_product(rows_d, hidden, slope, gate):
        count = rows_d.shape[0]
        return call(
            second_kernel,
            "second",
            [shape(BF16, count, hidden_units), shape(F32, count, 128)],
            (rows_d, all_second, hidden, slope, gate),
            flops=2 * count * width * hidden_units,
        )

    def row_gradients(rows_m, grad_pre, logit_gradient):
        count = grad_pre.shape[0]
        return call(
            rows_kernel,
            "rows",
            [
                shape(F32, count // columns, width),
                shape(BF16, count - count // columns, width),
                shape(F32, 8, width),
            ],
            (rows_m, grad_pre, logit_gradient, all_first, router_row),
            flops=2 * count * width * hidden_units,
        )

    def weight_gradient(at, blocks, left, right, kind):
        low = at * units // 128 * 128
        high = -(-(at + blocks) * units // 128) * 128
        return call(
            functools.partial(weight_kernel, at * units),
            "weights",
            shape(kind, blocks * units, width),
            (left, right),
            flops=2 * left.shape[0] * width * blocks * units,
            scratch=[pltpu.VMEM((high - low, left.shape[0]), BF16)],
        )

    def half_sum(stay, pair):
        return call(half_kernel, "half", shape(BF16, units, width), (stay, pair))

    early_m, early_d = gather_rows(early)
    early_hidden, early_slope, early_y, early_gate = first_product(early_m, early_d)
    early_pre, early_logit = second_product(early_d, early_hidden, early_slope, early_gate)
    early_own, early_side, early_sums = row_gradients(early_m, early_pre, early_logit)
    for step in late:
        near[step], side[step] = tied((near[step], side[step]), (early_own, early_side))
    late_m, late_d = gather_rows(late)

    late_hidden, late_slope, late_y, late_gate = first_product(late_m, late_d)
    hidden = jnp.concatenate([early_hidden, late_hidden], axis=0)
    grad_y = jnp.concatenate([early_y, late_y], axis=0)
    out_leave = weight_gradient(0, 1, hidden, grad_y, BF16)
    out_pair = over_pair(out_leave)
    hidden = tied(hidden, out_leave)
    out_stay = weight_gradient(2, 1, hidden, grad_y, F32)
    late_pre, late_logit = second_product(tied(late_d, out_stay), late_hidden, late_slope, late_gate)
    late_own, late_side, late_sums = row_gradients(late_m, late_pre, late_logit)
    sums = early_sums + late_sums
    line = jnp.arange(-(-(experts + 1) // 8) * 8, dtype=jnp.int32)[:, None]
    total = jnp.where(line == own, sums[:1], jnp.where(line == experts, sums[1:2], 0.0))
    total = pairwise(total, "expert", halves, 1)
    out_half = half_sum(out_stay, out_pair)

    def by_turn(rows):
        return rows.reshape(columns - 1, -1, width)

    leaving = jnp.concatenate([by_turn(early_side), by_turn(late_side)], axis=1)
    stage = (out_half, total, late_own, leaving)
    out_half, total, leaving, hidden = tied((out_half, total, leaving, hidden), stage)
    out_other = over_half(out_half)
    rows_back = back_over_columns(list(leaving))

    def add_rows(own_rows, pieces):
        for piece in pieces:
            own_rows = own_rows + piece.astype(F32)
        return own_rows.astype(BF16).reshape(-1, capacity, width)

    returned = [None] * experts

    def send_back(chosen, rows):
        for step, value in zip(chosen, rows):
            returned[step] = over_experts(value, experts - step) if step else value

    rows_m = jnp.concatenate([early_m, late_m], axis=0)
    grad_pre = jnp.concatenate([early_pre, late_pre], axis=0)
    grad_pre = tied(grad_pre, (out_half, leaving))
    in_leave = weight_gradient(0, 1, grad_pre, rows_m, BF16)
    in_pair = over_pair(in_leave)
    in_stay = weight_gradient(2, 1, tied(grad_pre, in_leave), rows_m, F32)
    total = tied(total, in_stay)
    bit = 2
    while bit < halves:
        total = pairwise(total, "expert", halves, bit)
        bit *= 2
    total = pairwise(total, "dp", groups, 1)
    hidden, grad_pre = tied((hidden, grad_pre), in_stay)
    out_rest = over_pair(weight_gradient(1, 1, hidden, grad_y, BF16))
    out_mine = weight_gradient(3, 1, hidden, grad_y, F32)
    in_rest = over_pair(weight_gradient(1, 1, grad_pre, rows_m, BF16))
    in_mine = weight_gradient(3, 1, grad_pre, rows_m, F32)

    stage = (out_other, rows_back, in_pair, in_stay, total)
    out_other, rows_back, in_pair, in_stay, total = tied(stage, stage)
    in_other = over_half(half_sum(in_stay, in_pair))
    send_back(steps, add_rows(jnp.concatenate([early_own, late_own], axis=0), rows_back))
    bit = 2
    while bit < groups // 2:
        total = pairwise(total, "dp", groups, bit)
        bit *= 2
    last = lax.ppermute(total, "dp", [(i, i ^ bit) for i in range(groups)])
    grad_out = (out_mine + out_rest.astype(F32) + out_other.astype(F32)).astype(BF16)[None]

    returned = tied(returned, (in_other, grad_out))
    norm, deviation, places = prepared
    input_grad, grad_in, grad_router, grad_gain = call(
        finish_kernel,
        "finish",
        [
            shape(BF16, tokens, width),
            shape(BF16, units, width),
            shape(F32, experts, width),
            shape(F32, width),
        ],
        (
            norm,
            deviation,
            places,
            gain,
            cotangent,
            jnp.concatenate(returned, axis=0),
            in_mine,
            in_rest,
            in_other,
            total,
            last,
        ),
    )
    return (input_grad, grad_in.T[None], grad_out, grad_router.T, grad_gain)


def solution(mesh):
    in_specs = (
        P(("expert", "dp"), None),
        P(),
        P(),
        P(("expert", "dp"), None),
        P("expert", None, "dp"),
        P("expert", "dp", None),
        P(("expert", "dp"), None),
    )
    out_specs = (
        P(("expert", "dp"), None),
        P("expert", None, "dp"),
        P("expert", "dp", None),
        P(),
        P(),
    )
    return jax.shard_map(body, mesh=mesh, in_specs=in_specs, out_specs=out_specs, check_vma=False)
```

```python
import functools
import math

import jax
import jax.numpy as jnp
from jax import lax
from jax.experimental import pallas as pl
from jax.experimental.pallas import tpu as pltpu
from jax.sharding import PartitionSpec as P

F32 = jnp.float32
BF16 = jnp.bfloat16
VMEM = pl.BlockSpec(memory_space=pltpu.VMEM)
ANY = pl.BlockSpec(memory_space=pl.ANY)


def gelu_parts(pre):
    coeff = math.sqrt(2.0 / math.pi)
    inner = coeff * (pre + 0.044715 * pre * pre * pre)
    tanh_val = jnp.tanh(inner)
    value = 0.5 * pre * (1.0 + tanh_val)
    slope = 0.5 * (1.0 + tanh_val) + 0.5 * pre * (1.0 - tanh_val * tanh_val) * coeff * (
        1.0 + 3.0 * 0.044715 * pre * pre
    )
    return (value, slope)


def dot(a, b, a_dim, b_dim):
    return lax.dot_general(a, b, (((a_dim,), (b_dim,)), ((), ())), preferred_element_type=F32)


def spans(total, size=256):
    return [(at, min(size, total - at)) for at in range(0, total, size)]


def norm_pieces(block):
    values = block.astype(F32)
    centred_rows = values - jnp.mean(values, axis=1, keepdims=True)
    inverse_deviation = lax.rsqrt(
        jnp.mean(centred_rows * centred_rows, axis=1, keepdims=True) + 1e-06
    )
    return centred_rows * inverse_deviation, inverse_deviation


def slot_of(own, routes, experts, capacity):
    top, tokens = routes.shape
    relative = routes - own
    relative = jnp.where(relative < 0, relative + experts, relative)
    lanes = max(16, experts)
    expert = lax.broadcasted_iota(jnp.int32, (lanes, tokens), 0)
    picks = [expert == relative[j : j + 1, :] for j in range(top)]
    chosen = sum(jnp.where(pick, 1.0, 0.0) for pick in picks)
    earlier = lax.broadcasted_iota(jnp.int32, (tokens, tokens), 0) < lax.broadcasted_iota(
        jnp.int32, (tokens, tokens), 1
    )
    before = dot(chosen.astype(BF16), jnp.where(earlier, 1.0, 0.0).astype(BF16), 1, 0)
    return [
        relative[j : j + 1, :] * capacity
        + jnp.sum(jnp.where(pick, before, 0.0), axis=0, keepdims=True).astype(jnp.int32)
        for j, pick in enumerate(picks)
    ]


def place_matrix(slots, first, count, tokens):
    row = lax.broadcasted_iota(jnp.int32, (count, tokens), 0) + first
    hit = slots[0] == row
    for slot in slots[1:]:
        hit = hit | (slot == row)
    return jnp.where(hit, 1.0, 0.0).astype(BF16)


def dispatch_kernel(experts, capacity, x_hbm, gain_hbm, routes_hbm, d_hbm, *refs):
    send_refs, (x_ref, gain_ref, routes_ref, d_ref, sems) = refs[:experts], refs[experts:]
    copies = [
        pltpu.make_async_copy(source, target, sems.at[at])
        for at, (source, target) in enumerate(
            ((routes_hbm, routes_ref), (x_hbm, x_ref), (gain_hbm, gain_ref), (d_hbm, d_ref))
        )
    ]
    for copy in copies:
        copy.start()
    tokens = x_ref.shape[0]
    copies[0].wait()
    slots = slot_of(lax.axis_index("expert") // 2, routes_ref[...], experts, capacity)
    copies[1].wait()
    normalized_rows, _ = norm_pieces(x_ref[...])
    copies[2].wait()
    mixed_rows = (normalized_rows * gain_ref[...][None, :]).astype(BF16)
    copies[3].wait()
    cotangent = d_ref[...]
    for step in range(experts):
        places = place_matrix(slots, step * capacity, capacity, tokens)
        send_refs[step][0] = dot(places, mixed_rows, 1, 0).astype(BF16)
        send_refs[step][1] = dot(places, cotangent, 1, 0).astype(BF16)


def prepare_kernel(experts, capacity, x_ref, routes_ref, norm_ref, deviation_ref, places_ref):
    normalized_rows, inverse_deviation = norm_pieces(x_ref[...])
    norm_ref[...] = normalized_rows
    deviation_ref[...] = jnp.broadcast_to(inverse_deviation, deviation_ref.shape)
    slots = slot_of(lax.axis_index("expert") // 2, routes_ref[...], experts, capacity)
    places_ref[...] = place_matrix(slots, 0, experts * capacity, x_ref.shape[0])


def finish_kernel(
    norm_ref, deviation_ref, places_ref, gain_ref, d_ref, rows_ref, stay_ref, pair_ref, other_ref,
    total_ref, last_ref, out_ref, sum_ref, router_ref, gain_grad_ref
):
    sum_ref[...] = (
        stay_ref[...] + pair_ref[...].astype(F32) + other_ref[...].astype(F32)
    ).astype(BF16)
    normalized_rows = norm_ref[...]
    scaled_rows = dot(places_ref[...], rows_ref[...], 0, 0) * gain_ref[...][None, :]
    mean_first_term = jnp.mean(scaled_rows, axis=1, keepdims=True)
    mean_second_term = jnp.mean(scaled_rows * normalized_rows, axis=1, keepdims=True)
    norm_backward = deviation_ref[:, :1] * (
        scaled_rows - mean_first_term - normalized_rows * mean_second_term
    )
    out_ref[...] = (d_ref[...].astype(F32) + norm_backward).astype(BF16)
    experts = router_ref.shape[0]
    total = total_ref[...] + last_ref[...]
    router_ref[...] = total[:experts]
    gain_grad_ref[...] = jnp.sum(total[experts:], axis=0) / gain_ref[...]


def first_kernel(m_ref, d_ref, first_ref, router_ref, hidden_ref, slope_ref, y_ref, gate_ref):
    rows_m = m_ref[...]
    gate = jax.nn.sigmoid(jnp.sum(rows_m.astype(F32) * router_ref[...], axis=1, keepdims=True))
    y_ref[...] = (gate * d_ref[...].astype(F32)).astype(BF16)
    gate_ref[...] = jnp.broadcast_to(gate, gate_ref.shape)
    for at, size in spans(first_ref.shape[0]):
        units = pl.ds(at, size)
        value, slope = gelu_parts(dot(rows_m, first_ref[units, :], 1, 1))
        hidden_ref[:, units] = value.astype(BF16)
        slope_ref[:, units] = gate * slope


def second_kernel(d_ref, second_ref, hidden_ref, slope_ref, gate_ref, pre_ref, logit_ref):
    rows_d = d_ref[...]
    gate = gate_ref[:, :1]
    share = jnp.zeros_like(gate)
    for at, size in spans(second_ref.shape[0]):
        units = pl.ds(at, size)
        back = dot(rows_d, second_ref[units, :], 1, 1)
        pre_ref[:, units] = (back * slope_ref[:, units]).astype(BF16)
        share = share + jnp.sum(hidden_ref[:, units].astype(F32) * back, axis=1, keepdims=True)
    logit_ref[...] = jnp.broadcast_to(share * gate * (1.0 - gate), logit_ref.shape)


def rows_kernel(m_ref, pre_ref, logit_ref, first_ref, router_ref, own_ref, side_ref, sums_ref):
    count = own_ref.shape[0]
    pre = pre_ref[...]
    logit = logit_ref[:, :1]
    for at, size in spans(first_ref.shape[1]):
        lanes = pl.ds(at, size)
        rows = dot(pre, first_ref[:, lanes], 1, 0) + logit * router_ref[:, lanes]
        own_ref[:, lanes] = rows[:count]
        side_ref[:, lanes] = rows[count:].astype(BF16)
        rows_m = m_ref[:, lanes].astype(F32)
        router_part = jnp.sum(rows_m * logit, axis=0, keepdims=True)
        gain_part = jnp.sum(rows_m * rows, axis=0, keepdims=True)
        row = lax.broadcasted_iota(jnp.int32, (sums_ref.shape[0], size), 0)
        sums_ref[:, lanes] = jnp.where(row == 0, router_part, jnp.where(row == 1, gain_part, 0.0))


def weight_kernel(first, left_ref, right_ref, out_ref, turned):
    units = out_ref.shape[0]
    low = first // 128 * 128
    high = -(-(first + units) // 128) * 128
    turned[...] = left_ref[:, low:high].T
    for at, size in spans(right_ref.shape[1]):
        lanes = pl.ds(at, size)
        out_ref[:, lanes] = dot(
            turned[first - low : first - low + units, :], right_ref[:, lanes], 1, 0
        ).astype(out_ref.dtype)


def join_kernel(*refs):
    at = 0
    for ref in refs[:-1]:
        refs[-1][at : at + ref.shape[0], :] = ref[...]
        at += ref.shape[0]


def gather_kernel(*refs):
    rows = refs[0].shape[1]
    for at, ref in enumerate(refs[:-2]):
        refs[-2][at * rows : (at + 1) * rows, :] = ref[0]
        refs[-1][at * rows : (at + 1) * rows, :] = ref[1]


def half_kernel(stay_ref, pair_ref, out_ref):
    out_ref[...] = (stay_ref[...] + pair_ref[...].astype(F32)).astype(BF16)


def tied(values, after):
    held, _ = lax.optimization_barrier((values, after))
    return held


def shape(kind, *sizes):
    return jax.ShapeDtypeStruct(sizes, kind)


def call(kernel, name, outs, args, flops=0, specs=None, scratch=(), mebibytes=18):
    return pl.pallas_call(
        kernel,
        out_shape=outs,
        in_specs=specs or [VMEM] * len(args),
        out_specs=jax.tree.map(lambda _: VMEM, outs),
        scratch_shapes=list(scratch),
        compiler_params=pltpu.CompilerParams(vmem_limit_bytes=mebibytes * 2**20),
        cost_estimate=pl.CostEstimate(flops=flops, bytes_accessed=flops // 512, transcendentals=0),
        name=name,
    )(*args)


def body(prenorm_input, gain, router, routes, w_in, w_out, cotangent):
    halves = lax.axis_size("expert")
    experts = halves // 2
    groups = lax.axis_size("dp")
    columns = groups // 2
    tokens, width = prenorm_input.shape
    top = routes.shape[1]
    capacity = max(2, 5 * tokens * top // (4 * experts))
    slots = experts * capacity
    own = lax.axis_index("expert") // 2

    def over_half(value):
        return lax.ppermute(value, "expert", [(i, i ^ 1) for i in range(halves)])

    def over_pair(value):
        return lax.ppermute(value, "dp", [(i, i ^ 1) for i in range(groups)])

    def over_columns(value):
        return [
            lax.ppermute(value, "dp", [(i, (i + 2 * step) % groups) for i in range(groups)])
            for step in range(1, columns)
        ]

    def back_over_columns(values):
        return [
            lax.ppermute(value, "dp", [(i, (i - 2 * step) % groups) for i in range(groups)])
            for step, value in enumerate(values, 1)
        ]

    def over_experts(value, step):
        return lax.ppermute(value, "expert", [(i, (i + 2 * step) % halves) for i in range(halves)])

    def pairwise(value, name, size, bit):
        return value + lax.ppermute(value, name, [(i, i ^ bit) for i in range(size)])

    first = w_in[0].T
    second = w_out[0]
    units = first.shape[0]
    hidden_units = 4 * units

    routes_t = routes.T
    send = call(
        functools.partial(dispatch_kernel, experts, capacity),
        "dispatch",
        [shape(BF16, 2, capacity, width)] * experts,
        (prenorm_input, gain, routes_t, cotangent),
        flops=4 * slots * tokens * width,
        specs=[ANY] * 4,
        scratch=[
            pltpu.VMEM((tokens, width), BF16),
            pltpu.VMEM((width,), F32),
            pltpu.VMEM((top, tokens), jnp.int32),
            pltpu.VMEM((tokens, width), BF16),
            pltpu.SemaphoreType.DMA((4,)),
        ],
        mebibytes=60,
    )

    steps = sorted(range(experts), key=lambda step: min(step, experts - step))
    quarter = experts // 4
    early, late = steps[: 3 * quarter], steps[3 * quarter :]
    near = {0: send[0]}
    for step in early[1:]:
        near[step] = over_experts(send[step], step)
    side = {0: over_columns(send[0])}
    first_y = over_half(tied(first, send[0]))
    first_c = over_pair(tied(first, send[0]))

    stage = (first_y, first_c, [near[step] for step in early], side[0])
    second_held, late_held, early_held, first_y, side[0] = tied(
        (second, [send[step] for step in late], [near[step] for step in early], first_y, side[0]),
        stage,
    )
    for step, value in zip(late, late_held):
        near[step] = over_experts(value, step)
    for step, value in zip(early, early_held):
        near[step] = value
        if step:
            side[step] = over_columns(value)
    second_y = over_half(second_held)
    first_yc = over_pair(first_y)
    prepared = call(
        functools.partial(prepare_kernel, experts, capacity),
        "prepare",
        [shape(F32, tokens, width), shape(F32, tokens, 128), shape(BF16, slots, tokens)],
        (prenorm_input, routes_t),
    )

    stage = (
        second_y,
        first_yc,
        [near[step] for step in late],
        [side[step] for step in early[1:]],
        prepared,
    )
    late_held, second_held, second_y, early_held, first_yc, prepared = tied(
        (
            [near[step] for step in late],
            second_held,
            second_y,
            [side[step] for step in early[1:]],
            first_yc,
            prepared,
        ),
        stage,
    )
    for step, value in zip(early[1:], early_held):
        side[step] = value
    for step, value in zip(late, late_held):
        near[step] = value
        side[step] = over_columns(value)
    second_c = over_pair(second_held)
    second_yc = over_pair(second_y)

    def join(*parts):
        return call(join_kernel, "join", shape(BF16, hidden_units, width), parts)

    all_first = join(first_yc, first_c, first_y, first)
    all_second = join(second_yc, second_c, second_y, second_held)

    router_row = lax.dynamic_slice_in_dim(router, own, 1, 1).astype(F32).T

    def gather_rows(chosen):
        pieces = [near[step] for step in chosen]
        for turn in range(columns - 1):
            pieces = pieces + [side[step][turn] for step in chosen]
        if capacity % 16 == 0:
            outs = [shape(BF16, len(pieces) * capacity, width)] * 2
            return call(gather_kernel, "gather", outs, pieces)
        return (
            jnp.concatenate([piece[0] for piece in pieces], axis=0),
            jnp.concatenate([piece[1] for piece in pieces], axis=0),
        )

    def first_product(rows_m, rows_d):
        count = rows_m.shape[0]
        return call(
            first_kernel,
            "first",
            [
                shape(BF16, count, hidden_units),
                shape(F32, count, hidden_units),
                shape(BF16, count, width),
                shape(F32, count, 128),
            ],
            (rows_m, rows_d, all_first, router_row),
            flops=2 * count * width * hidden_units,
        )

    def second_product(rows_d, hidden, slope, gate):
        count = rows_d.shape[0]
        return call(
            second_kernel,
            "second",
            [shape(BF16, count, hidden_units), shape(F32, count, 128)],
            (rows_d, all_second, hidden, slope, gate),
            flops=2 * count * width * hidden_units,
        )

    def row_gradients(rows_m, grad_pre, logit_gradient):
        count = grad_pre.shape[0]
        return call(
            rows_kernel,
            "rows",
            [
                shape(F32, count // columns, width),
                shape(BF16, count - count // columns, width),
                shape(F32, 8, width),
            ],
            (rows_m, grad_pre, logit_gradient, all_first, router_row),
            flops=2 * count * width * hidden_units,
        )

    def weight_gradient(at, blocks, left, right, kind):
        low = at * units // 128 * 128
        high = -(-(at + blocks) * units // 128) * 128
        return call(
            functools.partial(weight_kernel, at * units),
            "weights",
            shape(kind, blocks * units, width),
            (left, right),
            flops=2 * left.shape[0] * width * blocks * units,
            scratch=[pltpu.VMEM((high - low, left.shape[0]), BF16)],
        )

    def half_sum(stay, pair):
        return call(half_kernel, "half", shape(BF16, units, width), (stay, pair))

    early_m, early_d = gather_rows(early)
    early_hidden, early_slope, early_y, early_gate = first_product(early_m, early_d)
    early_pre, early_logit = second_product(early_d, early_hidden, early_slope, early_gate)
    early_own, early_side, early_sums = row_gradients(early_m, early_pre, early_logit)
    for step in late:
        near[step], side[step] = tied((near[step], side[step]), (early_own, early_side))
    late_m, late_d = gather_rows(late)

    def by_turn(rows):
        return list(rows.reshape(columns - 1, -1, width))

    def add_rows(own_rows, pieces):
        for piece in pieces:
            own_rows = own_rows + piece.astype(F32)
        return own_rows.astype(BF16).reshape(-1, capacity, width)

    returned = [None] * experts

    def send_back(chosen, rows):
        for step, value in zip(chosen, rows):
            returned[step] = over_experts(value, experts - step) if step else value

    early_back = back_over_columns(by_turn(early_side))
    late_hidden, late_slope, late_y, late_gate = first_product(late_m, late_d)
    hidden = jnp.concatenate([early_hidden, late_hidden], axis=0)
    grad_y = jnp.concatenate([early_y, late_y], axis=0)
    out_leave = weight_gradient(0, 1, hidden, grad_y, BF16)
    out_pair = over_pair(out_leave)
    hidden = tied(hidden, out_leave)
    out_stay = weight_gradient(2, 1, hidden, grad_y, F32)
    late_pre, late_logit = second_product(tied(late_d, out_stay), late_hidden, late_slope, late_gate)
    late_own, late_side, late_sums = row_gradients(late_m, late_pre, late_logit)
    sums = early_sums + late_sums
    line = jnp.arange(-(-(experts + 1) // 8) * 8, dtype=jnp.int32)[:, None]
    total = jnp.where(line == own, sums[:1], jnp.where(line == experts, sums[1:2], 0.0))
    out_half = half_sum(out_stay, out_pair)

    stage = (out_half, total, late_own, late_side)
    out_half, total, late_side, hidden = tied((out_half, total, late_side, hidden), stage)
    out_other = over_half(out_half)
    late_back = back_over_columns(by_turn(late_side))
    rows_m = jnp.concatenate([early_m, late_m], axis=0)
    grad_pre = jnp.concatenate([early_pre, late_pre], axis=0)
    grad_pre = tied(grad_pre, (out_half, late_side))
    in_leave = weight_gradient(0, 1, grad_pre, rows_m, BF16)
    in_pair = over_pair(in_leave)
    in_stay = weight_gradient(2, 1, tied(grad_pre, in_leave), rows_m, F32)
    total = tied(total, in_stay)
    bit = 2
    while bit < halves:
        total = pairwise(total, "expert", halves, bit)
        bit *= 2
    total = pairwise(total, "dp", groups, 1)
    early_back, late_back = tied((early_back, late_back), total)
    early_rows = add_rows(early_own, early_back)
    late_rows = add_rows(late_own, late_back)
    total = tied(total, (early_rows, late_rows))
    total = pairwise(total, "expert", halves, 1)
    hidden, grad_pre = tied((hidden, grad_pre), in_stay)
    out_rest = over_pair(weight_gradient(1, 1, hidden, grad_y, BF16))
    out_mine = weight_gradient(3, 1, hidden, grad_y, F32)
    in_rest = over_pair(weight_gradient(1, 1, grad_pre, rows_m, BF16))
    in_mine = weight_gradient(3, 1, grad_pre, rows_m, F32)

    stage = (out_other, early_rows, late_rows, in_pair, in_stay, total)
    out_other, early_rows, late_rows, in_pair, in_stay, total = tied(stage, stage)
    in_other = over_half(half_sum(in_stay, in_pair))
    send_back(early, early_rows)
    send_back(late, late_rows)
    bit = 2
    while bit < groups // 2:
        total = pairwise(total, "dp", groups, bit)
        bit *= 2
    last = lax.ppermute(total, "dp", [(i, i ^ bit) for i in range(groups)])
    grad_out = (out_mine + out_rest.astype(F32) + out_other.astype(F32)).astype(BF16)[None]

    returned = tied(returned, (in_other, grad_out))
    norm, deviation, places = prepared
    input_grad, grad_in, grad_router, grad_gain = call(
        finish_kernel,
        "finish",
        [
            shape(BF16, tokens, width),
            shape(BF16, units, width),
            shape(F32, experts, width),
            shape(F32, width),
        ],
        (
            norm,
            deviation,
            places,
            gain,
            cotangent,
            jnp.concatenate(returned, axis=0),
            in_mine,
            in_rest,
            in_other,
            total,
            last,
        ),
    )
    return (input_grad, grad_in.T[None], grad_out, grad_router.T, grad_gain)


def solution(mesh):
    in_specs = (
        P(("expert", "dp"), None),
        P(),
        P(),
        P(("expert", "dp"), None),
        P("expert", None, "dp"),
        P("expert", "dp", None),
        P(("expert", "dp"), None),
    )
    out_specs = (
        P(("expert", "dp"), None),
        P("expert", None, "dp"),
        P("expert", "dp", None),
        P(),
        P(),
    )
    return jax.shard_map(body, mesh=mesh, in_specs=in_specs, out_specs=out_specs, check_vma=False)
```

```python
import functools
import math

import jax
import jax.numpy as jnp
from jax import lax
from jax.experimental import pallas as pl
from jax.experimental.pallas import tpu as pltpu
from jax.sharding import PartitionSpec as P

F32 = jnp.float32
BF16 = jnp.bfloat16
VMEM = pl.BlockSpec(memory_space=pltpu.VMEM)
ANY = pl.BlockSpec(memory_space=pl.ANY)


def gelu_parts(pre):
    coeff = math.sqrt(2.0 / math.pi)
    inner = coeff * (pre + 0.044715 * pre * pre * pre)
    tanh_val = jnp.tanh(inner)
    value = 0.5 * pre * (1.0 + tanh_val)
    slope = 0.5 * (1.0 + tanh_val) + 0.5 * pre * (1.0 - tanh_val * tanh_val) * coeff * (
        1.0 + 3.0 * 0.044715 * pre * pre
    )
    return (value, slope)


def dot(a, b, a_dim, b_dim):
    return lax.dot_general(a, b, (((a_dim,), (b_dim,)), ((), ())), preferred_element_type=F32)


def spans(total, size=256):
    return [(at, min(size, total - at)) for at in range(0, total, size)]


def norm_pieces(block):
    values = block.astype(F32)
    centred_rows = values - jnp.mean(values, axis=1, keepdims=True)
    inverse_deviation = lax.rsqrt(
        jnp.mean(centred_rows * centred_rows, axis=1, keepdims=True) + 1e-06
    )
    return centred_rows * inverse_deviation, inverse_deviation


def slot_of(own, routes, experts, capacity):
    top, tokens = routes.shape
    relative = routes - own
    relative = jnp.where(relative < 0, relative + experts, relative)
    lanes = max(16, experts)
    expert = lax.broadcasted_iota(jnp.int32, (lanes, tokens), 0)
    picks = [expert == relative[j : j + 1, :] for j in range(top)]
    chosen = sum(jnp.where(pick, 1.0, 0.0) for pick in picks)
    earlier = lax.broadcasted_iota(jnp.int32, (tokens, tokens), 0) < lax.broadcasted_iota(
        jnp.int32, (tokens, tokens), 1
    )
    before = dot(chosen.astype(BF16), jnp.where(earlier, 1.0, 0.0).astype(BF16), 1, 0)
    return [
        relative[j : j + 1, :] * capacity
        + jnp.sum(jnp.where(pick, before, 0.0), axis=0, keepdims=True).astype(jnp.int32)
        for j, pick in enumerate(picks)
    ]


def place_matrix(slots, first, count, tokens):
    row = lax.broadcasted_iota(jnp.int32, (count, tokens), 0) + first
    hit = slots[0] == row
    for slot in slots[1:]:
        hit = hit | (slot == row)
    return jnp.where(hit, 1.0, 0.0).astype(BF16)


def dispatch_kernel(experts, capacity, x_hbm, gain_hbm, routes_hbm, d_hbm, *refs):
    send_refs, (x_ref, gain_ref, routes_ref, d_ref, sems) = refs[:experts], refs[experts:]
    copies = [
        pltpu.make_async_copy(source, target, sems.at[at])
        for at, (source, target) in enumerate(
            ((routes_hbm, routes_ref), (x_hbm, x_ref), (gain_hbm, gain_ref), (d_hbm, d_ref))
        )
    ]
    for copy in copies:
        copy.start()
    tokens = x_ref.shape[0]
    copies[0].wait()
    slots = slot_of(lax.axis_index("expert") // 2, routes_ref[...], experts, capacity)
    copies[1].wait()
    normalized_rows, _ = norm_pieces(x_ref[...])
    copies[2].wait()
    mixed_rows = (normalized_rows * gain_ref[...][None, :]).astype(BF16)
    copies[3].wait()
    cotangent = d_ref[...]
    for step in range(experts):
        places = place_matrix(slots, step * capacity, capacity, tokens)
        send_refs[step][0] = dot(places, mixed_rows, 1, 0).astype(BF16)
        send_refs[step][1] = dot(places, cotangent, 1, 0).astype(BF16)


def prepare_kernel(experts, capacity, x_ref, routes_ref, norm_ref, deviation_ref, places_ref):
    normalized_rows, inverse_deviation = norm_pieces(x_ref[...])
    norm_ref[...] = normalized_rows
    deviation_ref[...] = jnp.broadcast_to(inverse_deviation, deviation_ref.shape)
    slots = slot_of(lax.axis_index("expert") // 2, routes_ref[...], experts, capacity)
    places_ref[...] = place_matrix(slots, 0, experts * capacity, x_ref.shape[0])


def finish_kernel(
    norm_ref, deviation_ref, places_ref, gain_ref, d_ref, rows_ref, stay_ref, pair_ref, other_ref,
    total_ref, last_ref, out_ref, sum_ref, router_ref, gain_grad_ref
):
    sum_ref[...] = (
        stay_ref[...] + pair_ref[...].astype(F32) + other_ref[...].astype(F32)
    ).astype(BF16)
    normalized_rows = norm_ref[...]
    scaled_rows = dot(places_ref[...], rows_ref[...], 0, 0) * gain_ref[...][None, :]
    mean_first_term = jnp.mean(scaled_rows, axis=1, keepdims=True)
    mean_second_term = jnp.mean(scaled_rows * normalized_rows, axis=1, keepdims=True)
    norm_backward = deviation_ref[:, :1] * (
        scaled_rows - mean_first_term - normalized_rows * mean_second_term
    )
    out_ref[...] = (d_ref[...].astype(F32) + norm_backward).astype(BF16)
    experts = router_ref.shape[0]
    total = total_ref[...] + last_ref[...]
    router_ref[...] = total[:experts]
    gain_grad_ref[...] = jnp.sum(total[experts:], axis=0) / gain_ref[...]


def first_kernel(m_ref, d_ref, first_ref, router_ref, hidden_ref, slope_ref, y_ref, gate_ref):
    rows_m = m_ref[...]
    gate = jax.nn.sigmoid(jnp.sum(rows_m.astype(F32) * router_ref[...], axis=1, keepdims=True))
    y_ref[...] = (gate * d_ref[...].astype(F32)).astype(BF16)
    gate_ref[...] = jnp.broadcast_to(gate, gate_ref.shape)
    for at, size in spans(first_ref.shape[0]):
        units = pl.ds(at, size)
        value, slope = gelu_parts(dot(rows_m, first_ref[units, :], 1, 1))
        hidden_ref[:, units] = value.astype(BF16)
        slope_ref[:, units] = gate * slope


def second_kernel(d_ref, second_ref, hidden_ref, slope_ref, gate_ref, pre_ref, logit_ref):
    rows_d = d_ref[...]
    gate = gate_ref[:, :1]
    share = jnp.zeros_like(gate)
    for at, size in spans(second_ref.shape[0]):
        units = pl.ds(at, size)
        back = dot(rows_d, second_ref[units, :], 1, 1)
        pre_ref[:, units] = (back * slope_ref[:, units]).astype(BF16)
        share = share + jnp.sum(hidden_ref[:, units].astype(F32) * back, axis=1, keepdims=True)
    logit_ref[...] = jnp.broadcast_to(share * gate * (1.0 - gate), logit_ref.shape)


def rows_kernel(count, m_ref, pre_ref, logit_ref, first_ref, router_ref, sums_ref, *refs):
    pre = pre_ref[...]
    logit = logit_ref[:, :1]
    for at, size in spans(first_ref.shape[1]):
        lanes = pl.ds(at, size)
        rows = dot(pre, first_ref[:, lanes], 1, 0) + logit * router_ref[:, lanes]
        if count:
            refs[0][:, lanes] = rows[:count]
        if count < pre.shape[0]:
            refs[-1][:, lanes] = rows[count:].astype(BF16)
        rows_m = m_ref[:, lanes].astype(F32)
        router_part = jnp.sum(rows_m * logit, axis=0, keepdims=True)
        gain_part = jnp.sum(rows_m * rows, axis=0, keepdims=True)
        row = lax.broadcasted_iota(jnp.int32, (sums_ref.shape[0], size), 0)
        sums_ref[:, lanes] = jnp.where(row == 0, router_part, jnp.where(row == 1, gain_part, 0.0))


def weight_kernel(first, left_ref, right_ref, out_ref, turned):
    units = out_ref.shape[0]
    low = first // 128 * 128
    high = -(-(first + units) // 128) * 128
    turned[...] = left_ref[:, low:high].T
    for at, size in spans(right_ref.shape[1]):
        lanes = pl.ds(at, size)
        out_ref[:, lanes] = dot(
            turned[first - low : first - low + units, :], right_ref[:, lanes], 1, 0
        ).astype(out_ref.dtype)


def copy_all(pairs, sems):
    copies = [
        pltpu.make_async_copy(source, target, sems.at[at]) for at, (source, target) in enumerate(pairs)
    ]
    for copy in copies:
        copy.start()
    for copy in copies:
        copy.wait()


def join_kernel(*refs):
    parts, (out_ref, sems) = refs[:-2], refs[-2:]
    rows = parts[0].shape[0]
    copy_all([(ref, out_ref.at[pl.ds(at * rows, rows)]) for at, ref in enumerate(parts)], sems)


def gather_kernel(*refs):
    parts, (m_ref, d_ref, sems) = refs[:-3], refs[-3:]
    rows = parts[0].shape[1]
    copy_all(
        [
            (ref.at[kind], out_ref.at[pl.ds(at * rows, rows)])
            for at, ref in enumerate(parts)
            for kind, out_ref in enumerate((m_ref, d_ref))
        ],
        sems,
    )


def half_kernel(stay_ref, pair_ref, out_ref):
    out_ref[...] = (stay_ref[...] + pair_ref[...].astype(F32)).astype(BF16)


def tied(values, after):
    held, _ = lax.optimization_barrier((values, after))
    return held


def shape(kind, *sizes):
    return jax.ShapeDtypeStruct(sizes, kind)


def call(kernel, name, outs, args, flops=0, specs=None, scratch=(), mebibytes=18):
    return pl.pallas_call(
        kernel,
        out_shape=outs,
        in_specs=specs or [VMEM] * len(args),
        out_specs=jax.tree.map(lambda _: VMEM, outs),
        scratch_shapes=list(scratch),
        compiler_params=pltpu.CompilerParams(vmem_limit_bytes=mebibytes * 2**20),
        cost_estimate=pl.CostEstimate(flops=flops, bytes_accessed=flops // 512, transcendentals=0),
        name=name,
    )(*args)


def body(prenorm_input, gain, router, routes, w_in, w_out, cotangent):
    halves = lax.axis_size("expert")
    experts = halves // 2
    groups = lax.axis_size("dp")
    columns = groups // 2
    tokens, width = prenorm_input.shape
    top = routes.shape[1]
    capacity = max(2, 5 * tokens * top // (4 * experts))
    slots = experts * capacity
    own = lax.axis_index("expert") // 2

    def over_half(value):
        return lax.ppermute(value, "expert", [(i, i ^ 1) for i in range(halves)])

    def over_pair(value):
        return lax.ppermute(value, "dp", [(i, i ^ 1) for i in range(groups)])

    def over_columns(value):
        return [
            lax.ppermute(value, "dp", [(i, (i + 2 * step) % groups) for i in range(groups)])
            for step in range(1, columns)
        ]

    def back_over_columns(values):
        return [
            lax.ppermute(value, "dp", [(i, (i - 2 * step) % groups) for i in range(groups)])
            for step, value in enumerate(values, 1)
        ]

    def over_experts(value, step):
        return lax.ppermute(value, "expert", [(i, (i + 2 * step) % halves) for i in range(halves)])

    def pairwise(value, name, size, bit):
        return value + lax.ppermute(value, name, [(i, i ^ bit) for i in range(size)])

    first = w_in[0].T
    second = w_out[0]
    units = first.shape[0]
    hidden_units = 4 * units

    routes_t = routes.T
    send = call(
        functools.partial(dispatch_kernel, experts, capacity),
        "dispatch",
        [shape(BF16, 2, capacity, width)] * experts,
        (prenorm_input, gain, routes_t, cotangent),
        flops=4 * slots * tokens * width,
        specs=[ANY] * 4,
        scratch=[
            pltpu.VMEM((tokens, width), BF16),
            pltpu.VMEM((width,), F32),
            pltpu.VMEM((top, tokens), jnp.int32),
            pltpu.VMEM((tokens, width), BF16),
            pltpu.SemaphoreType.DMA((4,)),
        ],
        mebibytes=60,
    )

    steps = sorted(range(experts), key=lambda step: min(step, experts - step))
    quarter = experts // 4
    early, late = steps[: 3 * quarter], steps[3 * quarter :]
    near = {0: send[0]}
    for step in early[1:]:
        near[step] = over_experts(send[step], step)
    side = {0: over_columns(send[0])}
    first_y = over_half(tied(first, send[0]))
    first_c = over_pair(tied(first, send[0]))

    stage = (first_y, first_c, [near[step] for step in early], side[0])
    second_held, late_held, early_held, first_y, side[0] = tied(
        (second, [send[step] for step in late], [near[step] for step in early], first_y, side[0]),
        stage,
    )
    for step, value in zip(late, late_held):
        near[step] = over_experts(value, step)
    for step, value in zip(early, early_held):
        near[step] = value
        if step:
            side[step] = over_columns(value)
    second_y = over_half(second_held)
    first_yc = over_pair(first_y)
    prepared = call(
        functools.partial(prepare_kernel, experts, capacity),
        "prepare",
        [shape(F32, tokens, width), shape(F32, tokens, 128), shape(BF16, slots, tokens)],
        (prenorm_input, routes_t),
    )

    def join(*parts):
        return call(
            join_kernel,
            "join",
            shape(BF16, hidden_units, width),
            parts,
            specs=[ANY] * len(parts),
            scratch=[pltpu.SemaphoreType.DMA((len(parts),))],
        )

    def gather_rows(pieces):
        if capacity % 16 == 0:
            return call(
                gather_kernel,
                "gather",
                [shape(BF16, len(pieces) * capacity, width)] * 2,
                pieces,
                specs=[ANY] * len(pieces),
                scratch=[pltpu.SemaphoreType.DMA((2 * len(pieces),))],
            )
        return [jnp.concatenate([piece[kind] for piece in pieces], axis=0) for kind in range(2)]

    def side_pieces(chosen):
        return [side[step][turn] for turn in range(columns - 1) for step in chosen]

    router_row = lax.dynamic_slice_in_dim(router, own, 1, 1).astype(F32).T

    def first_product(rows_m, rows_d):
        count = rows_m.shape[0]
        return call(
            first_kernel,
            "first",
            [
                shape(BF16, count, hidden_units),
                shape(F32, count, hidden_units),
                shape(BF16, count, width),
                shape(F32, count, 128),
            ],
            (rows_m, rows_d, all_first, router_row),
            flops=2 * count * width * hidden_units,
        )

    def second_product(rows_d, hidden, slope, gate):
        count = rows_d.shape[0]
        return call(
            second_kernel,
            "second",
            [shape(BF16, count, hidden_units), shape(F32, count, 128)],
            (rows_d, all_second, hidden, slope, gate),
            flops=2 * count * width * hidden_units,
        )

    def row_gradients(stay, rows_m, grad_pre, logit_gradient):
        count = grad_pre.shape[0]
        outs = [shape(F32, 8, width)]
        if stay:
            outs.append(shape(F32, stay, width))
        if stay < count:
            outs.append(shape(BF16, count - stay, width))
        return call(
            functools.partial(rows_kernel, stay),
            "rows",
            outs,
            (rows_m, grad_pre, logit_gradient, all_first, router_row),
            flops=2 * count * width * hidden_units,
        )

    def weight_gradient(at, blocks, left, right, kind):
        low = at * units // 128 * 128
        high = -(-(at + blocks) * units // 128) * 128
        return call(
            functools.partial(weight_kernel, at * units),
            "weights",
            shape(kind, blocks * units, width),
            (left, right),
            flops=2 * left.shape[0] * width * blocks * units,
            scratch=[pltpu.VMEM((high - low, left.shape[0]), BF16)],
        )

    def half_sum(stay, pair):
        return call(half_kernel, "half", shape(BF16, units, width), (stay, pair))

    all_first = join(first_yc, first_c, first_y, first)
    near_m, near_d = gather_rows([near[step] for step in early])
    near_first = first_product(near_m, near_d)

    stage = (
        second_y,
        near_first,
        [near[step] for step in late],
        [side[step] for step in early[1:]],
        prepared,
    )
    late_held, second_held, second_y, early_held, near_first, prepared = tied(
        (
            [near[step] for step in late],
            second_held,
            second_y,
            [side[step] for step in early[1:]],
            near_first,
            prepared,
        ),
        stage,
    )
    for step, value in zip(early[1:], early_held):
        side[step] = value
    for step, value in zip(late, late_held):
        near[step] = value
        side[step] = over_columns(value)
    second_c = over_pair(second_held)
    second_yc = over_pair(second_y)

    side_m, side_d = gather_rows(side_pieces(early))
    side_hidden, side_slope, side_y, side_gate = first_product(side_m, side_d)
    all_second = join(second_yc, second_c, second_y, second_held)
    side_pre, side_logit = second_product(side_d, side_hidden, side_slope, side_gate)
    side_sums, side_rows = row_gradients(0, side_m, side_pre, side_logit)
    near_hidden, near_slope, near_y, near_gate = near_first
    near_pre, near_logit = second_product(tied(near_d, side_rows), near_hidden, near_slope, near_gate)
    near_sums, near_rows = row_gradients(near_m.shape[0], near_m, near_pre, near_logit)
    for step in late:
        near[step], side[step] = tied((near[step], side[step]), near_rows)
    late_m, late_d = gather_rows([near[step] for step in late] + side_pieces(late))

    def by_turn(rows):
        return list(rows.reshape(columns - 1, -1, width))

    def add_rows(own_rows, pieces):
        for piece in pieces:
            own_rows = own_rows + piece.astype(F32)
        return own_rows.astype(BF16).reshape(-1, capacity, width)

    returned = [None] * experts

    def send_back(chosen, rows):
        for step, value in zip(chosen, rows):
            returned[step] = over_experts(value, experts - step) if step else value

    early_back = back_over_columns(by_turn(side_rows))
    late_hidden, late_slope, late_y, late_gate = first_product(late_m, late_d)
    hidden = jnp.concatenate([near_hidden, side_hidden, late_hidden], axis=0)
    grad_y = jnp.concatenate([near_y, side_y, late_y], axis=0)
    out_leave = weight_gradient(0, 1, hidden, grad_y, BF16)
    out_pair = over_pair(out_leave)
    hidden = tied(hidden, out_leave)
    out_stay = weight_gradient(2, 1, hidden, grad_y, F32)
    late_pre, late_logit = second_product(tied(late_d, out_stay), late_hidden, late_slope, late_gate)
    late_sums, late_rows, late_side = row_gradients(
        late_m.shape[0] // columns, late_m, late_pre, late_logit
    )
    sums = near_sums + side_sums + late_sums
    line = jnp.arange(-(-(experts + 1) // 8) * 8, dtype=jnp.int32)[:, None]
    total = jnp.where(line == own, sums[:1], jnp.where(line == experts, sums[1:2], 0.0))
    out_half = half_sum(out_stay, out_pair)

    stage = (out_half, late_rows, late_side, total)
    out_half, late_side, total, hidden = tied((out_half, late_side, total, hidden), stage)
    out_other = over_half(out_half)
    late_back = back_over_columns(by_turn(late_side))
    total = pairwise(total, "dp", groups, 1)
    pair_total = total
    bit = 2
    while bit < halves:
        total = pairwise(total, "expert", halves, bit)
        bit *= 2
    early_back, late_back = tied((early_back, late_back), total)
    early_rows = add_rows(near_rows, early_back)
    moved = range(quarter, 2 * quarter)
    send_back([steps[at] for at in moved], [early_rows[at] for at in moved])
    late_rows = add_rows(late_rows, late_back)
    total = pairwise(tied(total, (early_rows, late_rows)), "expert", halves, 1)
    rows_m = jnp.concatenate([near_m, side_m, late_m], axis=0)
    grad_pre = jnp.concatenate([near_pre, side_pre, late_pre], axis=0)
    grad_pre = tied(grad_pre, pair_total)
    in_leave = weight_gradient(0, 1, grad_pre, rows_m, BF16)
    in_pair = over_pair(in_leave)
    in_stay = weight_gradient(2, 1, tied(grad_pre, in_leave), rows_m, F32)
    hidden, grad_pre = tied((hidden, grad_pre), in_stay)
    out_rest = over_pair(weight_gradient(1, 1, hidden, grad_y, BF16))
    out_mine = weight_gradient(3, 1, hidden, grad_y, F32)
    in_rest = over_pair(weight_gradient(1, 1, grad_pre, rows_m, BF16))
    in_mine = weight_gradient(3, 1, grad_pre, rows_m, F32)

    moved_rows = [returned[steps[at]] for at in moved]
    stage = (out_other, early_rows, late_rows, moved_rows, in_pair, in_stay, total)
    out_other, early_rows, late_rows, moved_rows, in_pair, in_stay, total = tied(stage, stage)
    for at, value in zip(moved, moved_rows):
        returned[steps[at]] = value
    in_other = over_half(half_sum(in_stay, in_pair))
    rest = [at for at in range(len(early)) if at not in moved]
    send_back([steps[at] for at in rest], [early_rows[at] for at in rest])
    send_back(late, late_rows)
    bit = 2
    while bit < groups // 2:
        total = pairwise(total, "dp", groups, bit)
        bit *= 2
    last = lax.ppermute(total, "dp", [(i, i ^ bit) for i in range(groups)])
    grad_out = (out_mine + out_rest.astype(F32) + out_other.astype(F32)).astype(BF16)[None]

    returned = tied(returned, (in_other, grad_out))
    norm, deviation, places = prepared
    input_grad, grad_in, grad_router, grad_gain = call(
        finish_kernel,
        "finish",
        [
            shape(BF16, tokens, width),
            shape(BF16, units, width),
            shape(F32, experts, width),
            shape(F32, width),
        ],
        (
            norm,
            deviation,
            places,
            gain,
            cotangent,
            jnp.concatenate(returned, axis=0),
            in_mine,
            in_rest,
            in_other,
            total,
            last,
        ),
    )
    return (input_grad, grad_in.T[None], grad_out, grad_router.T, grad_gain)


def solution(mesh):
    in_specs = (
        P(("expert", "dp"), None),
        P(),
        P(),
        P(("expert", "dp"), None),
        P("expert", None, "dp"),
        P("expert", "dp", None),
        P(("expert", "dp"), None),
    )
    out_specs = (
        P(("expert", "dp"), None),
        P("expert", None, "dp"),
        P("expert", "dp", None),
        P(),
        P(),
    )
    return jax.shard_map(body, mesh=mesh, in_specs=in_specs, out_specs=out_specs, check_vma=False)
```

```python
import functools
import math
import random

import jax
import jax.numpy as jnp
from jax import lax
from jax.experimental import pallas as pl
from jax.experimental.pallas import tpu as pltpu
from jax.sharding import PartitionSpec as P

F32 = jnp.float32
ORDER = 14
BF16 = jnp.bfloat16
VMEM = pl.BlockSpec(memory_space=pltpu.VMEM)
ANY = pl.BlockSpec(memory_space=pl.ANY)


def gelu_parts(pre):
    coeff = math.sqrt(2.0 / math.pi)
    inner = coeff * (pre + 0.044715 * pre * pre * pre)
    tanh_val = jnp.tanh(inner)
    value = 0.5 * pre * (1.0 + tanh_val)
    slope = 0.5 * (1.0 + tanh_val) + 0.5 * pre * (1.0 - tanh_val * tanh_val) * coeff * (
        1.0 + 3.0 * 0.044715 * pre * pre
    )
    return (value, slope)


def dot(a, b, a_dim, b_dim):
    return lax.dot_general(a, b, (((a_dim,), (b_dim,)), ((), ())), preferred_element_type=F32)


def spans(total, size=256):
    return [(at, min(size, total - at)) for at in range(0, total, size)]


def norm_pieces(block):
    values = block.astype(F32)
    centred_rows = values - jnp.mean(values, axis=1, keepdims=True)
    inverse_deviation = lax.rsqrt(
        jnp.mean(centred_rows * centred_rows, axis=1, keepdims=True) + 1e-06
    )
    return centred_rows * inverse_deviation, inverse_deviation


def slot_of(own, routes, experts, capacity):
    top, tokens = routes.shape
    relative = routes - own
    relative = jnp.where(relative < 0, relative + experts, relative)
    lanes = max(16, experts)
    expert = lax.broadcasted_iota(jnp.int32, (lanes, tokens), 0)
    picks = [expert == relative[j : j + 1, :] for j in range(top)]
    chosen = sum(jnp.where(pick, 1.0, 0.0) for pick in picks)
    earlier = lax.broadcasted_iota(jnp.int32, (tokens, tokens), 0) < lax.broadcasted_iota(
        jnp.int32, (tokens, tokens), 1
    )
    before = dot(chosen.astype(BF16), jnp.where(earlier, 1.0, 0.0).astype(BF16), 1, 0)
    return [
        relative[j : j + 1, :] * capacity
        + jnp.sum(jnp.where(pick, before, 0.0), axis=0, keepdims=True).astype(jnp.int32)
        for j, pick in enumerate(picks)
    ]


def place_matrix(slots, first, count, tokens):
    row = lax.broadcasted_iota(jnp.int32, (count, tokens), 0) + first
    hit = slots[0] == row
    for slot in slots[1:]:
        hit = hit | (slot == row)
    return jnp.where(hit, 1.0, 0.0).astype(BF16)


def dispatch_kernel(experts, capacity, x_hbm, gain_hbm, routes_hbm, d_hbm, *refs):
    send_refs, (x_ref, gain_ref, routes_ref, d_ref, sems) = refs[:experts], refs[experts:]
    copies = [
        pltpu.make_async_copy(source, target, sems.at[at])
        for at, (source, target) in enumerate(
            ((routes_hbm, routes_ref), (x_hbm, x_ref), (gain_hbm, gain_ref), (d_hbm, d_ref))
        )
    ]
    for copy in copies:
        copy.start()
    tokens = x_ref.shape[0]
    copies[0].wait()
    slots = slot_of(lax.axis_index("expert") // 2, routes_ref[...], experts, capacity)
    copies[1].wait()
    normalized_rows, _ = norm_pieces(x_ref[...])
    copies[2].wait()
    mixed_rows = (normalized_rows * gain_ref[...][None, :]).astype(BF16)
    copies[3].wait()
    cotangent = d_ref[...]
    for step in range(experts):
        places = place_matrix(slots, step * capacity, capacity, tokens)
        send_refs[step][0] = dot(places, mixed_rows, 1, 0).astype(BF16)
        send_refs[step][1] = dot(places, cotangent, 1, 0).astype(BF16)


def prepare_kernel(experts, capacity, x_ref, routes_ref, norm_ref, deviation_ref, places_ref):
    normalized_rows, inverse_deviation = norm_pieces(x_ref[...])
    norm_ref[...] = normalized_rows
    deviation_ref[...] = jnp.broadcast_to(inverse_deviation, deviation_ref.shape)
    slots = slot_of(lax.axis_index("expert") // 2, routes_ref[...], experts, capacity)
    places_ref[...] = place_matrix(slots, 0, experts * capacity, x_ref.shape[0])


def finish_kernel(
    norm_ref, deviation_ref, places_ref, gain_ref, d_ref, rows_ref, stay_ref, pair_ref, other_ref,
    total_ref, last_ref, out_hbm, sum_hbm, router_ref, gain_grad_ref, out_ref, sum_ref, sems
):
    sum_ref[...] = (
        stay_ref[...] + pair_ref[...].astype(F32) + other_ref[...].astype(F32)
    ).astype(BF16)
    sum_copy = pltpu.make_async_copy(sum_ref, sum_hbm, sems.at[0])
    sum_copy.start()
    normalized_rows = norm_ref[...]
    scaled_rows = dot(places_ref[...], rows_ref[...], 0, 0) * gain_ref[...][None, :]
    mean_first_term = jnp.mean(scaled_rows, axis=1, keepdims=True)
    mean_second_term = jnp.mean(scaled_rows * normalized_rows, axis=1, keepdims=True)
    norm_backward = deviation_ref[:, :1] * (
        scaled_rows - mean_first_term - normalized_rows * mean_second_term
    )
    out_ref[...] = (d_ref[...].astype(F32) + norm_backward).astype(BF16)
    out_copy = pltpu.make_async_copy(out_ref, out_hbm, sems.at[1])
    out_copy.start()
    experts = router_ref.shape[0]
    total = total_ref[...] + last_ref[...]
    router_ref[...] = total[:experts]
    gain_grad_ref[...] = jnp.sum(total[experts:], axis=0) / gain_ref[...]
    sum_copy.wait()
    out_copy.wait()


def first_kernel(m_ref, d_ref, first_ref, router_ref, hidden_ref, slope_ref, y_ref, gate_ref):
    rows_m = m_ref[...]
    gate = jax.nn.sigmoid(jnp.sum(rows_m.astype(F32) * router_ref[...], axis=1, keepdims=True))
    y_ref[...] = (gate * d_ref[...].astype(F32)).astype(BF16)
    gate_ref[...] = jnp.broadcast_to(gate, gate_ref.shape)
    for at, size in spans(first_ref.shape[0]):
        units = pl.ds(at, size)
        value, slope = gelu_parts(dot(rows_m, first_ref[units, :], 1, 1))
        hidden_ref[:, units] = value.astype(BF16)
        slope_ref[:, units] = gate * slope


def second_kernel(d_ref, second_ref, hidden_ref, slope_ref, gate_ref, pre_ref, logit_ref):
    rows_d = d_ref[...]
    gate = gate_ref[:, :1]
    share = jnp.zeros_like(gate)
    for at, size in spans(second_ref.shape[0]):
        units = pl.ds(at, size)
        back = dot(rows_d, second_ref[units, :], 1, 1)
        pre_ref[:, units] = (back * slope_ref[:, units]).astype(BF16)
        share = share + jnp.sum(hidden_ref[:, units].astype(F32) * back, axis=1, keepdims=True)
    logit_ref[...] = jnp.broadcast_to(share * gate * (1.0 - gate), logit_ref.shape)


def rows_kernel(m_ref, pre_ref, logit_ref, first_ref, router_ref, own_ref, side_ref, sums_ref):
    count = own_ref.shape[0]
    pre = pre_ref[...]
    logit = logit_ref[:, :1]
    for at, size in spans(first_ref.shape[1]):
        lanes = pl.ds(at, size)
        rows = dot(pre, first_ref[:, lanes], 1, 0) + logit * router_ref[:, lanes]
        own_ref[:, lanes] = rows[:count]
        side_ref[:, lanes] = rows[count:].astype(BF16)
        rows_m = m_ref[:, lanes].astype(F32)
        router_part = jnp.sum(rows_m * logit, axis=0, keepdims=True)
        gain_part = jnp.sum(rows_m * rows, axis=0, keepdims=True)
        row = lax.broadcasted_iota(jnp.int32, (sums_ref.shape[0], size), 0)
        sums_ref[:, lanes] = jnp.where(row == 0, router_part, jnp.where(row == 1, gain_part, 0.0))


def weight_kernel(first, left_ref, right_ref, out_ref, turned):
    units = out_ref.shape[0]
    low = first // 128 * 128
    high = -(-(first + units) // 128) * 128
    turned[...] = left_ref[:, low:high].T
    for at, size in spans(right_ref.shape[1]):
        lanes = pl.ds(at, size)
        out_ref[:, lanes] = dot(
            turned[first - low : first - low + units, :], right_ref[:, lanes], 1, 0
        ).astype(out_ref.dtype)


def join_kernel(*refs):
    at = 0
    for ref in refs[:-1]:
        refs[-1][at : at + ref.shape[0], :] = ref[...]
        at += ref.shape[0]


def half_kernel(stay_ref, pair_ref, out_ref):
    out_ref[...] = (stay_ref[...] + pair_ref[...].astype(F32)).astype(BF16)


def tied(values, after):
    leaves, tree = jax.tree.flatten(values)
    operands = {id(leaf): leaf for leaf in leaves + jax.tree.leaves(after)}
    keys = list(operands)
    random.Random(ORDER + len(keys)).shuffle(keys)
    held = dict(zip(keys, lax.optimization_barrier([operands[key] for key in keys])))
    return jax.tree.unflatten(tree, [held[id(leaf)] for leaf in leaves])


def shape(kind, *sizes):
    return jax.ShapeDtypeStruct(sizes, kind)


def call(kernel, name, outs, args, flops=0, specs=None, out_specs=None, scratch=(), mebibytes=18):
    return pl.pallas_call(
        kernel,
        out_shape=outs,
        in_specs=specs or [VMEM] * len(args),
        out_specs=out_specs or jax.tree.map(lambda _: VMEM, outs),
        scratch_shapes=list(scratch),
        compiler_params=pltpu.CompilerParams(vmem_limit_bytes=mebibytes * 2**20),
        cost_estimate=pl.CostEstimate(flops=flops, bytes_accessed=flops // 512, transcendentals=0),
        name=name,
    )(*args)


def body(prenorm_input, gain, router, routes, w_in, w_out, cotangent):
    halves = lax.axis_size("expert")
    experts = halves // 2
    groups = lax.axis_size("dp")
    columns = groups // 2
    tokens, width = prenorm_input.shape
    top = routes.shape[1]
    capacity = max(2, 5 * tokens * top // (4 * experts))
    slots = experts * capacity
    own = lax.axis_index("expert") // 2

    def over_half(value):
        return lax.ppermute(value, "expert", [(i, i ^ 1) for i in range(halves)])

    def over_pair(value):
        return lax.ppermute(value, "dp", [(i, i ^ 1) for i in range(groups)])

    def over_columns(value):
        return [
            lax.ppermute(value, "dp", [(i, (i + 2 * step) % groups) for i in range(groups)])
            for step in range(1, columns)
        ]

    def back_over_columns(values):
        return [
            lax.ppermute(value, "dp", [(i, (i - 2 * step) % groups) for i in range(groups)])
            for step, value in enumerate(values, 1)
        ]

    def over_experts(value, step):
        return lax.ppermute(value, "expert", [(i, (i + 2 * step) % halves) for i in range(halves)])

    def pairwise(value, name, size, bit):
        return value + lax.ppermute(value, name, [(i, i ^ bit) for i in range(size)])

    first = w_in[0].T
    second = w_out[0]
    units = first.shape[0]
    hidden_units = 4 * units

    routes_t = routes.T
    send = call(
        functools.partial(dispatch_kernel, experts, capacity),
        "dispatch",
        [shape(BF16, 2, capacity, width)] * experts,
        (prenorm_input, gain, routes_t, cotangent),
        flops=4 * slots * tokens * width,
        specs=[ANY] * 4,
        scratch=[
            pltpu.VMEM((tokens, width), BF16),
            pltpu.VMEM((width,), F32),
            pltpu.VMEM((top, tokens), jnp.int32),
            pltpu.VMEM((tokens, width), BF16),
            pltpu.SemaphoreType.DMA((4,)),
        ],
        mebibytes=60,
    )

    steps = sorted(range(experts), key=lambda step: min(step, experts - step))
    quarter = experts // 4
    early, late = steps[: 3 * quarter], steps[3 * quarter :]
    near = {0: send[0]}
    for step in early[1:]:
        near[step] = over_experts(send[step], step)
    side = {0: over_columns(send[0])}
    first_y = over_half(tied(first, send[0]))
    first_c = over_pair(tied(first, send[0]))

    stage = (first_y, first_c, [near[step] for step in early], side[0])
    second_held, late_held, early_held, first_y, side[0] = tied(
        (second, [send[step] for step in late], [near[step] for step in early], first_y, side[0]),
        stage,
    )
    for step, value in zip(late, late_held):
        near[step] = over_experts(value, step)
    for step, value in zip(early, early_held):
        near[step] = value
        if step:
            side[step] = over_columns(value)
    second_y = over_half(second_held)
    first_yc = over_pair(first_y)
    prepared = call(
        functools.partial(prepare_kernel, experts, capacity),
        "prepare",
        [shape(F32, tokens, width), shape(F32, tokens, 128), shape(BF16, slots, tokens)],
        (prenorm_input, routes_t),
    )

    stage = (
        second_y,
        first_yc,
        [near[step] for step in late],
        [side[step] for step in early[1:]],
        prepared,
    )
    late_held, second_held, second_y, early_held, first_yc, prepared = tied(
        (
            [near[step] for step in late],
            second_held,
            second_y,
            [side[step] for step in early[1:]],
            first_yc,
            prepared,
        ),
        stage,
    )
    for step, value in zip(early[1:], early_held):
        side[step] = value
    for step, value in zip(late, late_held):
        near[step] = value
        side[step] = over_columns(value)
    second_c = over_pair(second_held)
    second_yc = over_pair(second_y)

    def join(*parts):
        return call(join_kernel, "join", shape(BF16, hidden_units, width), parts)

    all_first = join(first_yc, first_c, first_y, first)
    all_second = join(second_yc, second_c, second_y, second_held)

    router_row = lax.dynamic_slice_in_dim(router, own, 1, 1).astype(F32).T

    def gather_rows(chosen):
        pieces = [near[step] for step in chosen]
        for turn in range(columns - 1):
            pieces = pieces + [side[step][turn] for step in chosen]
        return (
            jnp.concatenate([piece[0] for piece in pieces], axis=0),
            jnp.concatenate([piece[1] for piece in pieces], axis=0),
        )

    def first_product(rows_m, rows_d):
        count = rows_m.shape[0]
        return call(
            first_kernel,
            "first",
            [
                shape(BF16, count, hidden_units),
                shape(F32, count, hidden_units),
                shape(BF16, count, width),
                shape(F32, count, 128),
            ],
            (rows_m, rows_d, all_first, router_row),
            flops=2 * count * width * hidden_units,
        )

    def second_product(rows_d, hidden, slope, gate):
        count = rows_d.shape[0]
        return call(
            second_kernel,
            "second",
            [shape(BF16, count, hidden_units), shape(F32, count, 128)],
            (rows_d, all_second, hidden, slope, gate),
            flops=2 * count * width * hidden_units,
        )

    def row_gradients(rows_m, grad_pre, logit_gradient):
        count = grad_pre.shape[0]
        return call(
            rows_kernel,
            "rows",
            [
                shape(F32, count // columns, width),
                shape(BF16, count - count // columns, width),
                shape(F32, 8, width),
            ],
            (rows_m, grad_pre, logit_gradient, all_first, router_row),
            flops=2 * count * width * hidden_units,
        )

    def weight_gradient(at, blocks, left, right, kind):
        low = at * units // 128 * 128
        high = -(-(at + blocks) * units // 128) * 128
        return call(
            functools.partial(weight_kernel, at * units),
            "weights",
            shape(kind, blocks * units, width),
            (left, right),
            flops=2 * left.shape[0] * width * blocks * units,
            scratch=[pltpu.VMEM((high - low, left.shape[0]), BF16)],
        )

    def half_sum(stay, pair):
        return call(half_kernel, "half", shape(BF16, units, width), (stay, pair))

    early_m, early_d = gather_rows(early)
    early_hidden, early_slope, early_y, early_gate = first_product(early_m, early_d)
    early_pre, early_logit = second_product(early_d, early_hidden, early_slope, early_gate)
    early_own, early_side, early_sums = row_gradients(early_m, early_pre, early_logit)
    for step in late:
        near[step], side[step] = tied((near[step], side[step]), (early_own, early_side))
    late_m, late_d = gather_rows(late)

    def by_turn(rows):
        return list(rows.reshape(columns - 1, -1, width))

    def add_rows(own_rows, pieces):
        for piece in pieces:
            own_rows = own_rows + piece.astype(F32)
        return own_rows.astype(BF16).reshape(-1, capacity, width)

    returned = [None] * experts

    def send_back(chosen, rows):
        for step, value in zip(chosen, rows):
            returned[step] = over_experts(value, experts - step) if step else value

    early_back = back_over_columns(by_turn(early_side))
    late_hidden, late_slope, late_y, late_gate = first_product(late_m, late_d)
    hidden = jnp.concatenate([early_hidden, late_hidden], axis=0)
    grad_y = jnp.concatenate([early_y, late_y], axis=0)
    out_leave = weight_gradient(0, 1, hidden, grad_y, BF16)
    out_pair = over_pair(out_leave)
    hidden = tied(hidden, out_leave)
    out_stay = weight_gradient(2, 1, hidden, grad_y, F32)
    late_pre, late_logit = second_product(tied(late_d, out_stay), late_hidden, late_slope, late_gate)
    late_own, late_side, late_sums = row_gradients(late_m, late_pre, late_logit)
    sums = early_sums + late_sums
    line = jnp.arange(-(-(experts + 1) // 8) * 8, dtype=jnp.int32)[:, None]
    total = jnp.where(line == own, sums[:1], jnp.where(line == experts, sums[1:2], 0.0))
    out_half = half_sum(out_stay, out_pair)

    stage = (out_half, total, late_own, late_side)
    out_half, total, late_side, hidden = tied((out_half, total, late_side, hidden), stage)
    out_other = over_half(out_half)
    rows_m = jnp.concatenate([early_m, late_m], axis=0)
    grad_pre = jnp.concatenate([early_pre, late_pre], axis=0)
    total = pairwise(total, "dp", groups, 1)
    grad_pre, late_side = tied((grad_pre, late_side), total)
    bit = 2
    while bit < halves:
        total = pairwise(total, "expert", halves, bit)
        bit *= 2
    late_back = back_over_columns(by_turn(late_side))
    in_leave = weight_gradient(0, 1, grad_pre, rows_m, BF16)
    in_pair = over_pair(in_leave)
    in_stay = weight_gradient(2, 1, tied(grad_pre, in_leave), rows_m, F32)
    early_back, late_back = tied((early_back, late_back), total)
    early_rows = add_rows(early_own, early_back)
    late_rows = add_rows(late_own, late_back)
    total = tied(total, (early_rows, late_rows))
    total = pairwise(total, "expert", halves, 1)
    hidden, grad_pre = tied((hidden, grad_pre), in_stay)
    out_rest = over_pair(weight_gradient(1, 1, hidden, grad_y, BF16))
    out_mine = weight_gradient(3, 1, hidden, grad_y, F32)
    in_rest = over_pair(weight_gradient(1, 1, grad_pre, rows_m, BF16))
    in_mine = weight_gradient(3, 1, grad_pre, rows_m, F32)

    stage = (out_other, early_rows, late_rows, in_pair, in_stay, total)
    out_other, early_rows, late_rows, in_pair, in_stay, total = tied(stage, stage)
    in_other = over_half(half_sum(in_stay, in_pair))
    send_back(early, early_rows)
    send_back(late, late_rows)
    bit = 2
    while bit < groups // 2:
        total = pairwise(total, "dp", groups, bit)
        bit *= 2
    last = lax.ppermute(total, "dp", [(i, i ^ bit) for i in range(groups)])
    grad_out = (out_mine + out_rest.astype(F32) + out_other.astype(F32)).astype(BF16)[None]

    returned = tied(returned, (in_other, grad_out))
    norm, deviation, places = prepared
    input_grad, grad_in, grad_router, grad_gain = call(
        finish_kernel,
        "finish",
        [
            shape(BF16, tokens, width),
            shape(BF16, units, width),
            shape(F32, experts, width),
            shape(F32, width),
        ],
        (
            norm,
            deviation,
            places,
            gain,
            cotangent,
            jnp.concatenate(returned, axis=0),
            in_mine,
            in_rest,
            in_other,
            total,
            last,
        ),
        out_specs=[ANY, ANY, VMEM, VMEM],
        scratch=[
            pltpu.VMEM((tokens, width), BF16),
            pltpu.VMEM((units, width), BF16),
            pltpu.SemaphoreType.DMA((2,)),
        ],
    )
    return (input_grad, grad_in.T[None], grad_out, grad_router.T, grad_gain)


def solution(mesh):
    in_specs = (
        P(("expert", "dp"), None),
        P(),
        P(),
        P(("expert", "dp"), None),
        P("expert", None, "dp"),
        P("expert", "dp", None),
        P(("expert", "dp"), None),
    )
    out_specs = (
        P(("expert", "dp"), None),
        P("expert", None, "dp"),
        P("expert", "dp", None),
        P(),
        P(),
    )
    return jax.shard_map(body, mesh=mesh, in_specs=in_specs, out_specs=out_specs, check_vma=False)
```

```python
import functools
import math
import random

import jax
import jax.numpy as jnp
from jax import lax
from jax.experimental import pallas as pl
from jax.experimental.pallas import tpu as pltpu
from jax.sharding import PartitionSpec as P

F32 = jnp.float32
ORDER = 24
BF16 = jnp.bfloat16
VMEM = pl.BlockSpec(memory_space=pltpu.VMEM)
ANY = pl.BlockSpec(memory_space=pl.ANY)


def gelu_parts(pre):
    coeff = math.sqrt(2.0 / math.pi)
    inner = coeff * (pre + 0.044715 * pre * pre * pre)
    tanh_val = jnp.tanh(inner)
    value = 0.5 * pre * (1.0 + tanh_val)
    slope = 0.5 * (1.0 + tanh_val) + 0.5 * pre * (1.0 - tanh_val * tanh_val) * coeff * (
        1.0 + 3.0 * 0.044715 * pre * pre
    )
    return (value, slope)


def dot(a, b, a_dim, b_dim):
    return lax.dot_general(a, b, (((a_dim,), (b_dim,)), ((), ())), preferred_element_type=F32)


def spans(total, size=256):
    return [(at, min(size, total - at)) for at in range(0, total, size)]


def norm_pieces(block):
    values = block.astype(F32)
    centred_rows = values - jnp.mean(values, axis=1, keepdims=True)
    inverse_deviation = lax.rsqrt(
        jnp.mean(centred_rows * centred_rows, axis=1, keepdims=True) + 1e-06
    )
    return centred_rows * inverse_deviation, inverse_deviation


def slot_of(own, routes, experts, capacity):
    top, tokens = routes.shape
    relative = routes - own
    relative = jnp.where(relative < 0, relative + experts, relative)
    lanes = max(16, experts)
    expert = lax.broadcasted_iota(jnp.int32, (lanes, tokens), 0)
    picks = [expert == relative[j : j + 1, :] for j in range(top)]
    chosen = sum(jnp.where(pick, 1.0, 0.0) for pick in picks)
    earlier = lax.broadcasted_iota(jnp.int32, (tokens, tokens), 0) < lax.broadcasted_iota(
        jnp.int32, (tokens, tokens), 1
    )
    before = dot(chosen.astype(BF16), jnp.where(earlier, 1.0, 0.0).astype(BF16), 1, 0)
    return [
        relative[j : j + 1, :] * capacity
        + jnp.sum(jnp.where(pick, before, 0.0), axis=0, keepdims=True).astype(jnp.int32)
        for j, pick in enumerate(picks)
    ]


def place_matrix(slots, first, count, tokens):
    row = lax.broadcasted_iota(jnp.int32, (count, tokens), 0) + first
    hit = slots[0] == row
    for slot in slots[1:]:
        hit = hit | (slot == row)
    return jnp.where(hit, 1.0, 0.0).astype(BF16)


def dispatch_kernel(experts, capacity, x_hbm, gain_hbm, routes_hbm, d_hbm, *refs):
    send_refs, (x_ref, gain_ref, routes_ref, d_ref, sems) = refs[:experts], refs[experts:]
    copies = [
        pltpu.make_async_copy(source, target, sems.at[at])
        for at, (source, target) in enumerate(
            ((routes_hbm, routes_ref), (x_hbm, x_ref), (gain_hbm, gain_ref), (d_hbm, d_ref))
        )
    ]
    for copy in copies:
        copy.start()
    tokens = x_ref.shape[0]
    copies[0].wait()
    slots = slot_of(lax.axis_index("expert") // 2, routes_ref[...], experts, capacity)
    copies[1].wait()
    normalized_rows, _ = norm_pieces(x_ref[...])
    copies[2].wait()
    mixed_rows = (normalized_rows * gain_ref[...][None, :]).astype(BF16)
    copies[3].wait()
    cotangent = d_ref[...]
    for step in range(experts):
        places = place_matrix(slots, step * capacity, capacity, tokens)
        send_refs[step][0] = dot(places, mixed_rows, 1, 0).astype(BF16)
        send_refs[step][1] = dot(places, cotangent, 1, 0).astype(BF16)


def prepare_kernel(experts, capacity, x_ref, routes_ref, norm_ref, deviation_ref, places_ref):
    normalized_rows, inverse_deviation = norm_pieces(x_ref[...])
    norm_ref[...] = normalized_rows
    deviation_ref[...] = jnp.broadcast_to(inverse_deviation, deviation_ref.shape)
    slots = slot_of(lax.axis_index("expert") // 2, routes_ref[...], experts, capacity)
    places_ref[...] = place_matrix(slots, 0, experts * capacity, x_ref.shape[0])


def finish_kernel(
    norm_ref, deviation_ref, places_ref, gain_ref, d_ref, rows_ref, stay_ref, pair_ref, other_ref,
    total_ref, last_ref, out_ref, sum_ref, router_ref, gain_grad_ref
):
    sum_ref[...] = (
        stay_ref[...] + pair_ref[...].astype(F32) + other_ref[...].astype(F32)
    ).astype(BF16)
    normalized_rows = norm_ref[...]
    scaled_rows = dot(places_ref[...], rows_ref[...], 0, 0) * gain_ref[...][None, :]
    mean_first_term = jnp.mean(scaled_rows, axis=1, keepdims=True)
    mean_second_term = jnp.mean(scaled_rows * normalized_rows, axis=1, keepdims=True)
    norm_backward = deviation_ref[:, :1] * (
        scaled_rows - mean_first_term - normalized_rows * mean_second_term
    )
    out_ref[...] = (d_ref[...].astype(F32) + norm_backward).astype(BF16)
    experts = router_ref.shape[0]
    total = total_ref[...] + last_ref[...]
    router_ref[...] = total[:experts]
    gain_grad_ref[...] = jnp.sum(total[experts:], axis=0) / gain_ref[...]


def first_kernel(m_ref, d_ref, first_ref, router_ref, hidden_ref, slope_ref, y_ref, gate_ref):
    rows_m = m_ref[...]
    gate = jax.nn.sigmoid(jnp.sum(rows_m.astype(F32) * router_ref[...], axis=1, keepdims=True))
    y_ref[...] = (gate * d_ref[...].astype(F32)).astype(BF16)
    gate_ref[...] = jnp.broadcast_to(gate, gate_ref.shape)
    for at, size in spans(first_ref.shape[0]):
        units = pl.ds(at, size)
        value, slope = gelu_parts(dot(rows_m, first_ref[units, :], 1, 1))
        hidden_ref[:, units] = value.astype(BF16)
        slope_ref[:, units] = gate * slope


def second_kernel(d_ref, second_ref, hidden_ref, slope_ref, gate_ref, pre_ref, logit_ref):
    rows_d = d_ref[...]
    gate = gate_ref[:, :1]
    share = jnp.zeros_like(gate)
    for at, size in spans(second_ref.shape[0]):
        units = pl.ds(at, size)
        back = dot(rows_d, second_ref[units, :], 1, 1)
        pre_ref[:, units] = (back * slope_ref[:, units]).astype(BF16)
        share = share + jnp.sum(hidden_ref[:, units].astype(F32) * back, axis=1, keepdims=True)
    logit_ref[...] = jnp.broadcast_to(share * gate * (1.0 - gate), logit_ref.shape)


def rows_kernel(m_ref, pre_ref, logit_ref, first_ref, router_ref, own_ref, side_ref, sums_ref):
    count = own_ref.shape[0]
    pre = pre_ref[...]
    logit = logit_ref[:, :1]
    for at, size in spans(first_ref.shape[1]):
        lanes = pl.ds(at, size)
        rows = dot(pre, first_ref[:, lanes], 1, 0) + logit * router_ref[:, lanes]
        own_ref[:, lanes] = rows[:count]
        side_ref[:, lanes] = rows[count:].astype(BF16)
        rows_m = m_ref[:, lanes].astype(F32)
        router_part = jnp.sum(rows_m * logit, axis=0, keepdims=True)
        gain_part = jnp.sum(rows_m * rows, axis=0, keepdims=True)
        row = lax.broadcasted_iota(jnp.int32, (sums_ref.shape[0], size), 0)
        sums_ref[:, lanes] = jnp.where(row == 0, router_part, jnp.where(row == 1, gain_part, 0.0))


def weight_kernel(first, left_ref, right_ref, out_ref, turned):
    units = out_ref.shape[0]
    low = first // 128 * 128
    high = -(-(first + units) // 128) * 128
    turned[...] = left_ref[:, low:high].T
    for at, size in spans(right_ref.shape[1]):
        lanes = pl.ds(at, size)
        out_ref[:, lanes] = dot(
            turned[first - low : first - low + units, :], right_ref[:, lanes], 1, 0
        ).astype(out_ref.dtype)


def join_kernel(*refs):
    at = 0
    for ref in refs[:-1]:
        refs[-1][at : at + ref.shape[0], :] = ref[...]
        at += ref.shape[0]


def half_kernel(stay_ref, pair_ref, out_ref):
    out_ref[...] = (stay_ref[...] + pair_ref[...].astype(F32)).astype(BF16)


def tied(values, after):
    leaves, tree = jax.tree.flatten(values)
    operands = {id(leaf): leaf for leaf in leaves + jax.tree.leaves(after)}
    keys = list(operands)
    random.Random(ORDER + len(keys)).shuffle(keys)
    held = dict(zip(keys, lax.optimization_barrier([operands[key] for key in keys])))
    return jax.tree.unflatten(tree, [held[id(leaf)] for leaf in leaves])


def shape(kind, *sizes):
    return jax.ShapeDtypeStruct(sizes, kind)


def call(kernel, name, outs, args, flops=0, specs=None, out_specs=None, scratch=(), mebibytes=18):
    return pl.pallas_call(
        kernel,
        out_shape=outs,
        in_specs=specs or [VMEM] * len(args),
        out_specs=out_specs or jax.tree.map(lambda _: VMEM, outs),
        scratch_shapes=list(scratch),
        compiler_params=pltpu.CompilerParams(vmem_limit_bytes=mebibytes * 2**20),
        cost_estimate=pl.CostEstimate(flops=flops, bytes_accessed=flops // 512, transcendentals=0),
        name=name,
    )(*args)


def body(prenorm_input, gain, router, routes, w_in, w_out, cotangent):
    halves = lax.axis_size("expert")
    experts = halves // 2
    groups = lax.axis_size("dp")
    columns = groups // 2
    tokens, width = prenorm_input.shape
    top = routes.shape[1]
    capacity = max(2, 5 * tokens * top // (4 * experts))
    slots = experts * capacity
    own = lax.axis_index("expert") // 2

    def over_half(value):
        return lax.ppermute(value, "expert", [(i, i ^ 1) for i in range(halves)])

    def over_pair(value):
        return lax.ppermute(value, "dp", [(i, i ^ 1) for i in range(groups)])

    def over_columns(value):
        return [
            lax.ppermute(value, "dp", [(i, (i + 2 * step) % groups) for i in range(groups)])
            for step in range(1, columns)
        ]

    def back_over_columns(values):
        return [
            lax.ppermute(value, "dp", [(i, (i - 2 * step) % groups) for i in range(groups)])
            for step, value in enumerate(values, 1)
        ]

    def over_experts(value, step):
        return lax.ppermute(value, "expert", [(i, (i + 2 * step) % halves) for i in range(halves)])

    def pairwise(value, name, size, bit):
        return value + lax.ppermute(value, name, [(i, i ^ bit) for i in range(size)])

    first = w_in[0].T
    second = w_out[0]
    units = first.shape[0]
    hidden_units = 4 * units

    routes_t = routes.T
    send = call(
        functools.partial(dispatch_kernel, experts, capacity),
        "dispatch",
        [shape(BF16, 2, capacity, width)] * experts,
        (prenorm_input, gain, routes_t, cotangent),
        flops=4 * slots * tokens * width,
        specs=[ANY] * 4,
        scratch=[
            pltpu.VMEM((tokens, width), BF16),
            pltpu.VMEM((width,), F32),
            pltpu.VMEM((top, tokens), jnp.int32),
            pltpu.VMEM((tokens, width), BF16),
            pltpu.SemaphoreType.DMA((4,)),
        ],
        mebibytes=60,
    )

    steps = sorted(range(experts), key=lambda step: min(step, experts - step))
    quarter = experts // 4
    early, late = steps[: 3 * quarter], steps[3 * quarter :]
    near = {0: send[0]}
    for step in early[1:]:
        near[step] = over_experts(send[step], step)
    side = {0: over_columns(send[0])}
    first_y = over_half(tied(first, send[0]))
    first_c = over_pair(tied(first, send[0]))

    stage = (first_y, first_c, [near[step] for step in early], side[0])
    second_held, late_held, early_held, first_y, side[0] = tied(
        (second, [send[step] for step in late], [near[step] for step in early], first_y, side[0]),
        stage,
    )
    for step, value in zip(late, late_held):
        near[step] = over_experts(value, step)
    for step, value in zip(early, early_held):
        near[step] = value
        if step:
            side[step] = over_columns(value)
    second_y = over_half(second_held)
    first_yc = over_pair(first_y)
    prepared = call(
        functools.partial(prepare_kernel, experts, capacity),
        "prepare",
        [shape(F32, tokens, width), shape(F32, tokens, 128), shape(BF16, slots, tokens)],
        (prenorm_input, routes_t),
    )

    stage = (
        first_yc,
        [near[step] for step in late],
        [side[step] for step in early[1:]],
        prepared,
    )
    late_held, second_held, early_held, first_yc, prepared = tied(
        (
            [near[step] for step in late],
            second_held,
            [side[step] for step in early[1:]],
            first_yc,
            prepared,
        ),
        stage,
    )
    for step, value in zip(early[1:], early_held):
        side[step] = value
    for step, value in zip(late, late_held):
        near[step] = value
        side[step] = over_columns(value)
    second_c = over_pair(second_held)
    second_yc = over_pair(second_y)

    def join(*parts):
        return call(join_kernel, "join", shape(BF16, hidden_units, width), parts)

    all_first = join(first_yc, first_c, first_y, first)
    all_second = join(second_yc, second_c, second_y, second_held)

    router_row = lax.dynamic_slice_in_dim(router, own, 1, 1).astype(F32).T

    def gather_rows(chosen):
        pieces = [near[step] for step in chosen]
        for turn in range(columns - 1):
            pieces = pieces + [side[step][turn] for step in chosen]
        return (
            jnp.concatenate([piece[0] for piece in pieces], axis=0),
            jnp.concatenate([piece[1] for piece in pieces], axis=0),
        )

    def first_product(rows_m, rows_d):
        count = rows_m.shape[0]
        return call(
            first_kernel,
            "first",
            [
                shape(BF16, count, hidden_units),
                shape(F32, count, hidden_units),
                shape(BF16, count, width),
                shape(F32, count, 128),
            ],
            (rows_m, rows_d, all_first, router_row),
            flops=2 * count * width * hidden_units,
        )

    def second_product(rows_d, hidden, slope, gate):
        count = rows_d.shape[0]
        return call(
            second_kernel,
            "second",
            [shape(BF16, count, hidden_units), shape(F32, count, 128)],
            (rows_d, all_second, hidden, slope, gate),
            flops=2 * count * width * hidden_units,
        )

    def row_gradients(rows_m, grad_pre, logit_gradient):
        count = grad_pre.shape[0]
        return call(
            rows_kernel,
            "rows",
            [
                shape(F32, count // columns, width),
                shape(BF16, count - count // columns, width),
                shape(F32, 8, width),
            ],
            (rows_m, grad_pre, logit_gradient, all_first, router_row),
            flops=2 * count * width * hidden_units,
        )

    def weight_gradient(at, blocks, left, right, kind):
        low = at * units // 128 * 128
        high = -(-(at + blocks) * units // 128) * 128
        return call(
            functools.partial(weight_kernel, at * units),
            "weights",
            shape(kind, blocks * units, width),
            (left, right),
            flops=2 * left.shape[0] * width * blocks * units,
            scratch=[pltpu.VMEM((high - low, left.shape[0]), BF16)],
        )

    def half_sum(stay, pair):
        return call(half_kernel, "half", shape(BF16, units, width), (stay, pair))

    early_m, early_d = gather_rows(early)
    early_hidden, early_slope, early_y, early_gate = first_product(early_m, early_d)
    early_pre, early_logit = second_product(early_d, early_hidden, early_slope, early_gate)
    early_own, early_side, early_sums = row_gradients(early_m, early_pre, early_logit)
    for step in late:
        near[step], side[step] = tied((near[step], side[step]), (early_own, early_side))
    late_m, late_d = gather_rows(late)

    def by_turn(rows):
        return list(rows.reshape(columns - 1, -1, width))

    def add_rows(own_rows, pieces):
        for piece in pieces:
            own_rows = own_rows + piece.astype(F32)
        return own_rows.astype(BF16).reshape(-1, capacity, width)

    returned = [None] * experts

    def send_back(chosen, rows):
        for step, value in zip(chosen, rows):
            returned[step] = over_experts(value, experts - step) if step else value

    early_back = back_over_columns(by_turn(early_side))
    late_hidden, late_slope, late_y, late_gate = first_product(late_m, late_d)
    hidden = jnp.concatenate([early_hidden, late_hidden], axis=0)
    grad_y = jnp.concatenate([early_y, late_y], axis=0)
    out_leave = weight_gradient(0, 1, hidden, grad_y, BF16)
    out_pair = over_pair(out_leave)
    hidden = tied(hidden, out_leave)
    out_stay = weight_gradient(2, 1, hidden, grad_y, F32)
    late_pre, late_logit = second_product(tied(late_d, out_stay), late_hidden, late_slope, late_gate)
    late_own, late_side, late_sums = row_gradients(late_m, late_pre, late_logit)
    sums = early_sums + late_sums
    line = jnp.arange(-(-(experts + 1) // 8) * 8, dtype=jnp.int32)[:, None]
    total = jnp.where(line == own, sums[:1], jnp.where(line == experts, sums[1:2], 0.0))
    out_half = half_sum(out_stay, out_pair)

    stage = (out_half, total, late_own, late_side)
    out_half, total, late_side, hidden = tied((out_half, total, late_side, hidden), stage)
    out_other = over_half(out_half)
    rows_m = jnp.concatenate([early_m, late_m], axis=0)
    grad_pre = jnp.concatenate([early_pre, late_pre], axis=0)
    total = pairwise(total, "dp", groups, 1)
    grad_pre, late_side = tied((grad_pre, late_side), total)
    bit = 2
    while bit < halves:
        total = pairwise(total, "expert", halves, bit)
        bit *= 2
    late_back = back_over_columns(by_turn(late_side))
    in_leave = weight_gradient(0, 1, grad_pre, rows_m, BF16)
    in_pair = over_pair(in_leave)
    in_stay = weight_gradient(2, 1, tied(grad_pre, in_leave), rows_m, F32)
    early_back, late_back = tied((early_back, late_back), total)
    early_rows = add_rows(early_own, early_back)
    late_rows = add_rows(late_own, late_back)
    total = tied(total, (early_rows, late_rows))
    total = pairwise(total, "expert", halves, 1)
    hidden, grad_pre = tied((hidden, grad_pre), in_stay)
    out_rest = over_pair(weight_gradient(1, 1, hidden, grad_y, BF16))
    out_mine = weight_gradient(3, 1, hidden, grad_y, F32)
    in_rest = over_pair(weight_gradient(1, 1, grad_pre, rows_m, BF16))
    in_mine = weight_gradient(3, 1, grad_pre, rows_m, F32)

    stage = (out_other, early_rows, late_rows, in_pair, in_stay, total)
    out_other, early_rows, late_rows, in_pair, in_stay, total = tied(stage, stage)
    in_other = over_half(half_sum(in_stay, in_pair))
    send_back(early, early_rows)
    send_back(late, late_rows)
    bit = 2
    while bit < groups // 2:
        total = pairwise(total, "dp", groups, bit)
        bit *= 2
    last = lax.ppermute(total, "dp", [(i, i ^ bit) for i in range(groups)])
    grad_out = (out_mine + out_rest.astype(F32) + out_other.astype(F32)).astype(BF16)[None]

    returned = tied(returned, (in_other, grad_out))
    norm, deviation, places = prepared
    input_grad, grad_in, grad_router, grad_gain = call(
        finish_kernel,
        "finish",
        [
            shape(BF16, tokens, width),
            shape(BF16, units, width),
            shape(F32, experts, width),
            shape(F32, width),
        ],
        (
            norm,
            deviation,
            places,
            gain,
            cotangent,
            jnp.concatenate(returned, axis=0),
            in_mine,
            in_rest,
            in_other,
            total,
            last,
        ),
    )
    return (input_grad, grad_in.T[None], grad_out, grad_router.T, grad_gain)


def solution(mesh):
    in_specs = (
        P(("expert", "dp"), None),
        P(),
        P(),
        P(("expert", "dp"), None),
        P("expert", None, "dp"),
        P("expert", "dp", None),
        P(("expert", "dp"), None),
    )
    out_specs = (
        P(("expert", "dp"), None),
        P("expert", None, "dp"),
        P("expert", "dp", None),
        P(),
        P(),
    )
    return jax.shard_map(body, mesh=mesh, in_specs=in_specs, out_specs=out_specs, check_vma=False)
```

```python
import functools
import math
import random

import jax
import jax.numpy as jnp
from jax import lax
from jax.experimental import pallas as pl
from jax.experimental.pallas import tpu as pltpu
from jax.sharding import PartitionSpec as P

F32 = jnp.float32
ORDER = 27
BF16 = jnp.bfloat16
VMEM = pl.BlockSpec(memory_space=pltpu.VMEM)
ANY = pl.BlockSpec(memory_space=pl.ANY)


def gelu_parts(pre):
    coeff = math.sqrt(2.0 / math.pi)
    inner = coeff * (pre + 0.044715 * pre * pre * pre)
    tanh_val = jnp.tanh(inner)
    value = 0.5 * pre * (1.0 + tanh_val)
    slope = 0.5 * (1.0 + tanh_val) + 0.5 * pre * (1.0 - tanh_val * tanh_val) * coeff * (
        1.0 + 3.0 * 0.044715 * pre * pre
    )
    return (value, slope)


def dot(a, b, a_dim, b_dim):
    return lax.dot_general(a, b, (((a_dim,), (b_dim,)), ((), ())), preferred_element_type=F32)


def spans(total, size=256):
    return [(at, min(size, total - at)) for at in range(0, total, size)]


def norm_pieces(block):
    values = block.astype(F32)
    centred_rows = values - jnp.mean(values, axis=1, keepdims=True)
    inverse_deviation = lax.rsqrt(
        jnp.mean(centred_rows * centred_rows, axis=1, keepdims=True) + 1e-06
    )
    return centred_rows * inverse_deviation, inverse_deviation


def slot_of(own, routes, experts, capacity):
    top, tokens = routes.shape
    relative = routes - own
    relative = jnp.where(relative < 0, relative + experts, relative)
    lanes = max(16, experts)
    expert = lax.broadcasted_iota(jnp.int32, (lanes, tokens), 0)
    picks = [expert == relative[j : j + 1, :] for j in range(top)]
    chosen = sum(jnp.where(pick, 1.0, 0.0) for pick in picks)
    earlier = lax.broadcasted_iota(jnp.int32, (tokens, tokens), 0) < lax.broadcasted_iota(
        jnp.int32, (tokens, tokens), 1
    )
    before = dot(chosen.astype(BF16), jnp.where(earlier, 1.0, 0.0).astype(BF16), 1, 0)
    return [
        relative[j : j + 1, :] * capacity
        + jnp.sum(jnp.where(pick, before, 0.0), axis=0, keepdims=True).astype(jnp.int32)
        for j, pick in enumerate(picks)
    ]


def place_matrix(slots, first, count, tokens):
    row = lax.broadcasted_iota(jnp.int32, (count, tokens), 0) + first
    hit = slots[0] == row
    for slot in slots[1:]:
        hit = hit | (slot == row)
    return jnp.where(hit, 1.0, 0.0).astype(BF16)


def dispatch_kernel(experts, capacity, x_hbm, gain_hbm, routes_hbm, d_hbm, *refs):
    send_refs, (x_ref, gain_ref, routes_ref, d_ref, sems) = refs[:experts], refs[experts:]
    copies = [
        pltpu.make_async_copy(source, target, sems.at[at])
        for at, (source, target) in enumerate(
            ((routes_hbm, routes_ref), (x_hbm, x_ref), (gain_hbm, gain_ref), (d_hbm, d_ref))
        )
    ]
    for copy in copies:
        copy.start()
    tokens = x_ref.shape[0]
    copies[0].wait()
    slots = slot_of(lax.axis_index("expert") // 2, routes_ref[...], experts, capacity)
    copies[1].wait()
    normalized_rows, _ = norm_pieces(x_ref[...])
    copies[2].wait()
    mixed_rows = (normalized_rows * gain_ref[...][None, :]).astype(BF16)
    copies[3].wait()
    cotangent = d_ref[...]
    for step in range(experts):
        places = place_matrix(slots, step * capacity, capacity, tokens)
        send_refs[step][0] = dot(places, mixed_rows, 1, 0).astype(BF16)
        send_refs[step][1] = dot(places, cotangent, 1, 0).astype(BF16)


def prepare_kernel(experts, capacity, x_ref, routes_ref, norm_ref, deviation_ref, places_ref):
    normalized_rows, inverse_deviation = norm_pieces(x_ref[...])
    norm_ref[...] = normalized_rows
    deviation_ref[...] = jnp.broadcast_to(inverse_deviation, deviation_ref.shape)
    slots = slot_of(lax.axis_index("expert") // 2, routes_ref[...], experts, capacity)
    places_ref[...] = place_matrix(slots, 0, experts * capacity, x_ref.shape[0])


def finish_kernel(
    norm_ref, deviation_ref, places_ref, gain_ref, d_ref, rows_ref, stay_ref, pair_ref, other_ref,
    total_ref, last_ref, out_ref, sum_ref, router_ref, gain_grad_ref
):
    sum_ref[...] = (
        stay_ref[...] + pair_ref[...].astype(F32) + other_ref[...].astype(F32)
    ).astype(BF16)
    normalized_rows = norm_ref[...]
    scaled_rows = dot(places_ref[...], rows_ref[...], 0, 0) * gain_ref[...][None, :]
    mean_first_term = jnp.mean(scaled_rows, axis=1, keepdims=True)
    mean_second_term = jnp.mean(scaled_rows * normalized_rows, axis=1, keepdims=True)
    norm_backward = deviation_ref[:, :1] * (
        scaled_rows - mean_first_term - normalized_rows * mean_second_term
    )
    out_ref[...] = (d_ref[...].astype(F32) + norm_backward).astype(BF16)
    experts = router_ref.shape[0]
    total = total_ref[...] + last_ref[...]
    router_ref[...] = total[:experts]
    gain_grad_ref[...] = jnp.sum(total[experts:], axis=0) / gain_ref[...]


def first_kernel(m_ref, d_ref, first_ref, router_ref, hidden_ref, slope_ref, y_ref, gate_ref):
    rows_m = m_ref[...]
    gate = jax.nn.sigmoid(jnp.sum(rows_m.astype(F32) * router_ref[...], axis=1, keepdims=True))
    y_ref[...] = (gate * d_ref[...].astype(F32)).astype(BF16)
    gate_ref[...] = jnp.broadcast_to(gate, gate_ref.shape)
    for at, size in spans(first_ref.shape[0]):
        units = pl.ds(at, size)
        value, slope = gelu_parts(dot(rows_m, first_ref[units, :], 1, 1))
        hidden_ref[:, units] = value.astype(BF16)
        slope_ref[:, units] = gate * slope


def second_kernel(d_ref, second_ref, hidden_ref, slope_ref, gate_ref, pre_ref, logit_ref):
    rows_d = d_ref[...]
    gate = gate_ref[:, :1]
    share = jnp.zeros_like(gate)
    for at, size in spans(second_ref.shape[0]):
        units = pl.ds(at, size)
        back = dot(rows_d, second_ref[units, :], 1, 1)
        pre_ref[:, units] = (back * slope_ref[:, units]).astype(BF16)
        share = share + jnp.sum(hidden_ref[:, units].astype(F32) * back, axis=1, keepdims=True)
    logit_ref[...] = jnp.broadcast_to(share * gate * (1.0 - gate), logit_ref.shape)


def rows_kernel(m_ref, pre_ref, logit_ref, first_ref, router_ref, own_ref, side_ref, sums_ref):
    count = own_ref.shape[0]
    pre = pre_ref[...]
    logit = logit_ref[:, :1]
    for at, size in spans(first_ref.shape[1]):
        lanes = pl.ds(at, size)
        rows = dot(pre, first_ref[:, lanes], 1, 0) + logit * router_ref[:, lanes]
        own_ref[:, lanes] = rows[:count]
        side_ref[:, lanes] = rows[count:].astype(BF16)
        rows_m = m_ref[:, lanes].astype(F32)
        router_part = jnp.sum(rows_m * logit, axis=0, keepdims=True)
        gain_part = jnp.sum(rows_m * rows, axis=0, keepdims=True)
        row = lax.broadcasted_iota(jnp.int32, (sums_ref.shape[0], size), 0)
        sums_ref[:, lanes] = jnp.where(row == 0, router_part, jnp.where(row == 1, gain_part, 0.0))


def weight_kernel(first, left_ref, right_ref, out_ref, turned):
    units = out_ref.shape[0]
    low = first // 128 * 128
    high = -(-(first + units) // 128) * 128
    turned[...] = left_ref[:, low:high].T
    for at, size in spans(right_ref.shape[1]):
        lanes = pl.ds(at, size)
        out_ref[:, lanes] = dot(
            turned[first - low : first - low + units, :], right_ref[:, lanes], 1, 0
        ).astype(out_ref.dtype)


def join_kernel(*refs):
    at = 0
    for ref in refs[:-1]:
        refs[-1][at : at + ref.shape[0], :] = ref[...]
        at += ref.shape[0]


def half_kernel(stay_ref, pair_ref, out_ref):
    out_ref[...] = (stay_ref[...] + pair_ref[...].astype(F32)).astype(BF16)


def tied(values, after):
    leaves, tree = jax.tree.flatten(values)
    operands = {id(leaf): leaf for leaf in leaves + jax.tree.leaves(after)}
    keys = list(operands)
    random.Random(ORDER + len(keys)).shuffle(keys)
    held = dict(zip(keys, lax.optimization_barrier([operands[key] for key in keys])))
    return jax.tree.unflatten(tree, [held[id(leaf)] for leaf in leaves])


def shape(kind, *sizes):
    return jax.ShapeDtypeStruct(sizes, kind)


def call(kernel, name, outs, args, flops=0, specs=None, out_specs=None, scratch=(), mebibytes=18):
    return pl.pallas_call(
        kernel,
        out_shape=outs,
        in_specs=specs or [VMEM] * len(args),
        out_specs=out_specs or jax.tree.map(lambda _: VMEM, outs),
        scratch_shapes=list(scratch),
        compiler_params=pltpu.CompilerParams(vmem_limit_bytes=mebibytes * 2**20),
        cost_estimate=pl.CostEstimate(flops=flops, bytes_accessed=flops // 512, transcendentals=0),
        name=name,
    )(*args)


def body(prenorm_input, gain, router, routes, w_in, w_out, cotangent):
    halves = lax.axis_size("expert")
    experts = halves // 2
    groups = lax.axis_size("dp")
    columns = groups // 2
    tokens, width = prenorm_input.shape
    top = routes.shape[1]
    capacity = max(2, 5 * tokens * top // (4 * experts))
    slots = experts * capacity
    own = lax.axis_index("expert") // 2

    def over_half(value):
        return lax.ppermute(value, "expert", [(i, i ^ 1) for i in range(halves)])

    def over_pair(value):
        return lax.ppermute(value, "dp", [(i, i ^ 1) for i in range(groups)])

    def over_columns(value):
        return [
            lax.ppermute(value, "dp", [(i, (i + 2 * step) % groups) for i in range(groups)])
            for step in range(1, columns)
        ]

    def back_over_columns(values):
        return [
            lax.ppermute(value, "dp", [(i, (i - 2 * step) % groups) for i in range(groups)])
            for step, value in enumerate(values, 1)
        ]

    def over_experts(value, step):
        return lax.ppermute(value, "expert", [(i, (i + 2 * step) % halves) for i in range(halves)])

    def pairwise(value, name, size, bit):
        return value + lax.ppermute(value, name, [(i, i ^ bit) for i in range(size)])

    first = w_in[0].T
    second = w_out[0]
    units = first.shape[0]
    hidden_units = 4 * units

    routes_t = routes.T
    send = call(
        functools.partial(dispatch_kernel, experts, capacity),
        "dispatch",
        [shape(BF16, 2, capacity, width)] * experts,
        (prenorm_input, gain, routes_t, cotangent),
        flops=4 * slots * tokens * width,
        specs=[ANY] * 4,
        scratch=[
            pltpu.VMEM((tokens, width), BF16),
            pltpu.VMEM((width,), F32),
            pltpu.VMEM((top, tokens), jnp.int32),
            pltpu.VMEM((tokens, width), BF16),
            pltpu.SemaphoreType.DMA((4,)),
        ],
        mebibytes=60,
    )

    steps = sorted(range(experts), key=lambda step: min(step, experts - step))
    quarter = experts // 4
    early, late = steps[: 3 * quarter], steps[3 * quarter :]
    near = {0: send[0]}
    for step in early[1:]:
        near[step] = over_experts(send[step], step)
    side = {0: over_columns(send[0])}
    first_y = over_half(tied(first, send[0]))
    first_c = over_pair(tied(first, send[0]))

    stage = (first_y, first_c, [near[step] for step in early], side[0])
    second_held, late_held, early_held, first_y, side[0] = tied(
        (second, [send[step] for step in late], [near[step] for step in early], first_y, side[0]),
        stage,
    )
    for step, value in zip(late, late_held):
        near[step] = over_experts(value, step)
    for step, value in zip(early, early_held):
        near[step] = value
        if step:
            side[step] = over_columns(value)
    second_y = over_half(second_held)
    first_yc = over_pair(first_y)
    prepared = call(
        functools.partial(prepare_kernel, experts, capacity),
        "prepare",
        [shape(F32, tokens, width), shape(F32, tokens, 128), shape(BF16, slots, tokens)],
        (prenorm_input, routes_t),
    )

    stage = (
        first_yc,
        [near[step] for step in late],
        [side[step] for step in early[1:]],
        prepared,
    )
    late_held, second_held, early_held, first_yc, prepared = tied(
        (
            [near[step] for step in late],
            second_held,
            [side[step] for step in early[1:]],
            first_yc,
            prepared,
        ),
        stage,
    )
    for step, value in zip(early[1:], early_held):
        side[step] = value
    for step, value in zip(late, late_held):
        near[step] = value
        side[step] = over_columns(value)
    second_c = over_pair(second_held)
    second_yc = over_pair(second_y)

    def join(*parts):
        return call(join_kernel, "join", shape(BF16, hidden_units, width), parts)

    all_first = join(first_yc, first_c, first_y, first)
    all_second = join(second_yc, second_c, second_y, second_held)

    router_row = lax.dynamic_slice_in_dim(router, own, 1, 1).astype(F32).T

    def gather_rows(chosen):
        pieces = [near[step] for step in chosen]
        for turn in range(columns - 1):
            pieces = pieces + [side[step][turn] for step in chosen]
        return (
            jnp.concatenate([piece[0] for piece in pieces], axis=0),
            jnp.concatenate([piece[1] for piece in pieces], axis=0),
        )

    def first_product(rows_m, rows_d):
        count = rows_m.shape[0]
        return call(
            first_kernel,
            "first",
            [
                shape(BF16, count, hidden_units),
                shape(F32, count, hidden_units),
                shape(BF16, count, width),
                shape(F32, count, 128),
            ],
            (rows_m, rows_d, all_first, router_row),
            flops=2 * count * width * hidden_units,
        )

    def second_product(rows_d, hidden, slope, gate):
        count = rows_d.shape[0]
        return call(
            second_kernel,
            "second",
            [shape(BF16, count, hidden_units), shape(F32, count, 128)],
            (rows_d, all_second, hidden, slope, gate),
            flops=2 * count * width * hidden_units,
        )

    def row_gradients(rows_m, grad_pre, logit_gradient):
        count = grad_pre.shape[0]
        return call(
            rows_kernel,
            "rows",
            [
                shape(F32, count // columns, width),
                shape(BF16, count - count // columns, width),
                shape(F32, 8, width),
            ],
            (rows_m, grad_pre, logit_gradient, all_first, router_row),
            flops=2 * count * width * hidden_units,
        )

    def weight_gradient(at, blocks, left, right, kind):
        low = at * units // 128 * 128
        high = -(-(at + blocks) * units // 128) * 128
        return call(
            functools.partial(weight_kernel, at * units),
            "weights",
            shape(kind, blocks * units, width),
            (left, right),
            flops=2 * left.shape[0] * width * blocks * units,
            scratch=[pltpu.VMEM((high - low, left.shape[0]), BF16)],
        )

    def half_sum(stay, pair):
        return call(half_kernel, "half", shape(BF16, units, width), (stay, pair))

    early_m, early_d = gather_rows(early)
    early_hidden, early_slope, early_y, early_gate = first_product(early_m, early_d)
    early_pre, early_logit = second_product(early_d, early_hidden, early_slope, early_gate)
    early_own, early_side, early_sums = row_gradients(early_m, early_pre, early_logit)
    for step in late:
        near[step], side[step] = tied((near[step], side[step]), (early_own, early_side))
    late_m, late_d = gather_rows(late)

    def by_turn(rows):
        return list(rows.reshape(columns - 1, -1, width))

    def add_rows(own_rows, pieces):
        for piece in pieces:
            own_rows = own_rows + piece.astype(F32)
        return own_rows.astype(BF16).reshape(-1, capacity, width)

    returned = [None] * experts

    def send_back(chosen, rows):
        for step, value in zip(chosen, rows):
            returned[step] = over_experts(value, experts - step) if step else value

    early_back = back_over_columns(by_turn(early_side))
    late_hidden, late_slope, late_y, late_gate = first_product(late_m, late_d)
    hidden = jnp.concatenate([early_hidden, late_hidden], axis=0)
    grad_y = jnp.concatenate([early_y, late_y], axis=0)
    out_leave = weight_gradient(0, 1, hidden, grad_y, BF16)
    out_pair = over_pair(out_leave)
    hidden = tied(hidden, out_leave)
    out_stay = weight_gradient(2, 1, hidden, grad_y, F32)
    late_pre, late_logit = second_product(tied(late_d, out_stay), late_hidden, late_slope, late_gate)
    late_own, late_side, late_sums = row_gradients(late_m, late_pre, late_logit)
    sums = early_sums + late_sums
    line = jnp.arange(-(-(experts + 1) // 8) * 8, dtype=jnp.int32)[:, None]
    total = jnp.where(line == own, sums[:1], jnp.where(line == experts, sums[1:2], 0.0))
    out_half = half_sum(out_stay, out_pair)

    stage = (out_half, total, late_own, late_side)
    out_half, total, late_side, hidden = tied((out_half, total, late_side, hidden), stage)
    out_other = over_half(out_half)
    rows_m = jnp.concatenate([early_m, late_m], axis=0)
    grad_pre = jnp.concatenate([early_pre, late_pre], axis=0)
    total = pairwise(total, "dp", groups, 1)
    grad_pre, late_side = tied((grad_pre, late_side), total)
    bit = 2
    while bit < halves:
        total = pairwise(total, "expert", halves, bit)
        bit *= 2
    late_back = back_over_columns(by_turn(late_side))
    in_leave = weight_gradient(0, 1, grad_pre, rows_m, BF16)
    in_pair = over_pair(in_leave)
    in_stay = weight_gradient(2, 1, tied(grad_pre, in_leave), rows_m, F32)
    early_back, late_back = tied((early_back, late_back), total)
    early_rows = add_rows(early_own, early_back)
    late_rows = add_rows(late_own, late_back)
    moved = range(quarter, 2 * quarter)
    send_back([steps[at] for at in moved], [early_rows[at] for at in moved])
    moved_rows = [returned[steps[at]] for at in moved]
    total = tied(total, (early_rows, late_rows))
    total = pairwise(total, "expert", halves, 1)
    hidden, grad_pre = tied((hidden, grad_pre), in_stay)
    out_rest = over_pair(weight_gradient(1, 1, hidden, grad_y, BF16))
    out_mine = weight_gradient(3, 1, hidden, grad_y, F32)
    in_rest = over_pair(weight_gradient(1, 1, grad_pre, rows_m, BF16))
    in_mine = weight_gradient(3, 1, grad_pre, rows_m, F32)

    stage = (out_other, early_rows, late_rows, moved_rows, in_pair, in_stay, total)
    out_other, early_rows, late_rows, moved_rows, in_pair, in_stay, total = tied(stage, stage)
    for at, value in zip(moved, moved_rows):
        returned[steps[at]] = value
    in_other = over_half(half_sum(in_stay, in_pair))
    rest = [at for at in range(len(early)) if at not in moved]
    send_back([steps[at] for at in rest], [early_rows[at] for at in rest])
    send_back(late, late_rows)
    bit = 2
    while bit < groups // 2:
        total = pairwise(total, "dp", groups, bit)
        bit *= 2
    last = lax.ppermute(total, "dp", [(i, i ^ bit) for i in range(groups)])
    grad_out = (out_mine + out_rest.astype(F32) + out_other.astype(F32)).astype(BF16)[None]

    returned = tied(returned, (in_other, grad_out))
    norm, deviation, places = prepared
    input_grad, grad_in, grad_router, grad_gain = call(
        finish_kernel,
        "finish",
        [
            shape(BF16, tokens, width),
            shape(BF16, units, width),
            shape(F32, experts, width),
            shape(F32, width),
        ],
        (
            norm,
            deviation,
            places,
            gain,
            cotangent,
            jnp.concatenate(returned, axis=0),
            in_mine,
            in_rest,
            in_other,
            total,
            last,
        ),
    )
    return (input_grad, grad_in.T[None], grad_out, grad_router.T, grad_gain)


def solution(mesh):
    in_specs = (
        P(("expert", "dp"), None),
        P(),
        P(),
        P(("expert", "dp"), None),
        P("expert", None, "dp"),
        P("expert", "dp", None),
        P(("expert", "dp"), None),
    )
    out_specs = (
        P(("expert", "dp"), None),
        P("expert", None, "dp"),
        P("expert", "dp", None),
        P(),
        P(),
    )
    return jax.shard_map(body, mesh=mesh, in_specs=in_specs, out_specs=out_specs, check_vma=False)
```

```python
import functools
import math
import random

import jax
import jax.numpy as jnp
from jax import lax
from jax.experimental import pallas as pl
from jax.experimental.pallas import tpu as pltpu
from jax.sharding import PartitionSpec as P

F32 = jnp.float32
ORDER = 27
BF16 = jnp.bfloat16
VMEM = pl.BlockSpec(memory_space=pltpu.VMEM)
ANY = pl.BlockSpec(memory_space=pl.ANY)


def gelu_parts(pre):
    coeff = math.sqrt(2.0 / math.pi)
    inner = coeff * (pre + 0.044715 * pre * pre * pre)
    tanh_val = jnp.tanh(inner)
    value = 0.5 * pre * (1.0 + tanh_val)
    slope = 0.5 * (1.0 + tanh_val) + 0.5 * pre * (1.0 - tanh_val * tanh_val) * coeff * (
        1.0 + 3.0 * 0.044715 * pre * pre
    )
    return (value, slope)


def dot(a, b, a_dim, b_dim):
    return lax.dot_general(a, b, (((a_dim,), (b_dim,)), ((), ())), preferred_element_type=F32)


def spans(total, size=256):
    return [(at, min(size, total - at)) for at in range(0, total, size)]


def norm_pieces(block):
    values = block.astype(F32)
    centred_rows = values - jnp.mean(values, axis=1, keepdims=True)
    inverse_deviation = lax.rsqrt(
        jnp.mean(centred_rows * centred_rows, axis=1, keepdims=True) + 1e-06
    )
    return centred_rows * inverse_deviation, inverse_deviation


def slot_of(own, routes, experts, capacity):
    top, tokens = routes.shape
    relative = routes - own
    relative = jnp.where(relative < 0, relative + experts, relative)
    lanes = max(16, experts)
    expert = lax.broadcasted_iota(jnp.int32, (lanes, tokens), 0)
    picks = [expert == relative[j : j + 1, :] for j in range(top)]
    chosen = sum(jnp.where(pick, 1.0, 0.0) for pick in picks)
    earlier = lax.broadcasted_iota(jnp.int32, (tokens, tokens), 0) < lax.broadcasted_iota(
        jnp.int32, (tokens, tokens), 1
    )
    before = dot(chosen.astype(BF16), jnp.where(earlier, 1.0, 0.0).astype(BF16), 1, 0)
    return [
        relative[j : j + 1, :] * capacity
        + jnp.sum(jnp.where(pick, before, 0.0), axis=0, keepdims=True).astype(jnp.int32)
        for j, pick in enumerate(picks)
    ]


def place_matrix(slots, first, count, tokens):
    row = lax.broadcasted_iota(jnp.int32, (count, tokens), 0) + first
    hit = slots[0] == row
    for slot in slots[1:]:
        hit = hit | (slot == row)
    return jnp.where(hit, 1.0, 0.0).astype(BF16)


def dispatch_kernel(experts, capacity, x_hbm, gain_hbm, routes_hbm, d_hbm, *refs):
    send_refs, (x_ref, gain_ref, routes_ref, d_ref, sems) = refs[:experts], refs[experts:]
    copies = [
        pltpu.make_async_copy(source, target, sems.at[at])
        for at, (source, target) in enumerate(
            ((routes_hbm, routes_ref), (x_hbm, x_ref), (gain_hbm, gain_ref), (d_hbm, d_ref))
        )
    ]
    for copy in copies:
        copy.start()
    tokens = x_ref.shape[0]
    copies[0].wait()
    slots = slot_of(lax.axis_index("expert") // 2, routes_ref[...], experts, capacity)
    copies[1].wait()
    normalized_rows, _ = norm_pieces(x_ref[...])
    copies[2].wait()
    mixed_rows = (normalized_rows * gain_ref[...][None, :]).astype(BF16)
    copies[3].wait()
    cotangent = d_ref[...]
    for step in range(experts):
        places = place_matrix(slots, step * capacity, capacity, tokens)
        send_refs[step][0] = dot(places, mixed_rows, 1, 0).astype(BF16)
        send_refs[step][1] = dot(places, cotangent, 1, 0).astype(BF16)


def prepare_kernel(experts, capacity, x_ref, routes_ref, norm_ref, deviation_ref, places_ref):
    normalized_rows, inverse_deviation = norm_pieces(x_ref[...])
    norm_ref[...] = normalized_rows
    deviation_ref[...] = jnp.broadcast_to(inverse_deviation, deviation_ref.shape)
    slots = slot_of(lax.axis_index("expert") // 2, routes_ref[...], experts, capacity)
    places_ref[...] = place_matrix(slots, 0, experts * capacity, x_ref.shape[0])


def finish_kernel(
    norm_ref, deviation_ref, places_ref, gain_ref, d_ref, rows_ref, stay_ref, pair_ref, other_ref,
    sent_ref, out_ref, sum_ref, router_ref, gain_grad_ref
):
    units = sum_ref.shape[0]
    sum_ref[...] = (
        stay_ref[...] + pair_ref[...].astype(F32) + other_ref[:units, :].astype(F32)
    ).astype(BF16)
    normalized_rows = norm_ref[...]
    scaled_rows = dot(places_ref[...], rows_ref[...], 0, 0) * gain_ref[...][None, :]
    mean_first_term = jnp.mean(scaled_rows, axis=1, keepdims=True)
    mean_second_term = jnp.mean(scaled_rows * normalized_rows, axis=1, keepdims=True)
    norm_backward = deviation_ref[:, :1] * (
        scaled_rows - mean_first_term - normalized_rows * mean_second_term
    )
    out_ref[...] = (d_ref[...].astype(F32) + norm_backward).astype(BF16)
    experts = router_ref.shape[0]
    mine, others = sent_ref[units:, :].astype(F32), other_ref[units:, :].astype(F32)
    lines = mine.shape[0] // 2
    total = (mine[:lines] + mine[lines:]) + (others[:lines] + others[lines:])
    router_ref[...] = total[:experts]
    gain_grad_ref[...] = jnp.sum(total[experts:], axis=0) / gain_ref[...]


def first_kernel(m_ref, d_ref, first_ref, router_ref, hidden_ref, slope_ref, y_ref, gate_ref):
    rows_m = m_ref[...]
    gate = jax.nn.sigmoid(jnp.sum(rows_m.astype(F32) * router_ref[...], axis=1, keepdims=True))
    y_ref[...] = (gate * d_ref[...].astype(F32)).astype(BF16)
    gate_ref[...] = jnp.broadcast_to(gate, gate_ref.shape)
    for at, size in spans(first_ref.shape[0]):
        units = pl.ds(at, size)
        value, slope = gelu_parts(dot(rows_m, first_ref[units, :], 1, 1))
        hidden_ref[:, units] = value.astype(BF16)
        slope_ref[:, units] = gate * slope


def second_kernel(d_ref, second_ref, hidden_ref, slope_ref, gate_ref, pre_ref, logit_ref):
    rows_d = d_ref[...]
    gate = gate_ref[:, :1]
    share = jnp.zeros_like(gate)
    for at, size in spans(second_ref.shape[0]):
        units = pl.ds(at, size)
        back = dot(rows_d, second_ref[units, :], 1, 1)
        pre_ref[:, units] = (back * slope_ref[:, units]).astype(BF16)
        share = share + jnp.sum(hidden_ref[:, units].astype(F32) * back, axis=1, keepdims=True)
    logit_ref[...] = jnp.broadcast_to(share * gate * (1.0 - gate), logit_ref.shape)


def rows_kernel(m_ref, pre_ref, logit_ref, first_ref, router_ref, own_ref, side_ref, sums_ref):
    count = own_ref.shape[0]
    pre = pre_ref[...]
    logit = logit_ref[:, :1]
    for at, size in spans(first_ref.shape[1]):
        lanes = pl.ds(at, size)
        rows = dot(pre, first_ref[:, lanes], 1, 0) + logit * router_ref[:, lanes]
        own_ref[:, lanes] = rows[:count]
        side_ref[:, lanes] = rows[count:].astype(BF16)
        rows_m = m_ref[:, lanes].astype(F32)
        router_part = jnp.sum(rows_m * logit, axis=0, keepdims=True)
        gain_part = jnp.sum(rows_m * rows, axis=0, keepdims=True)
        row = lax.broadcasted_iota(jnp.int32, (sums_ref.shape[0], size), 0)
        sums_ref[:, lanes] = jnp.where(row == 0, router_part, jnp.where(row == 1, gain_part, 0.0))


def weight_kernel(first, left_ref, right_ref, out_ref, turned):
    units = out_ref.shape[0]
    low = first // 128 * 128
    high = -(-(first + units) // 128) * 128
    turned[...] = left_ref[:, low:high].T
    for at, size in spans(right_ref.shape[1]):
        lanes = pl.ds(at, size)
        out_ref[:, lanes] = dot(
            turned[first - low : first - low + units, :], right_ref[:, lanes], 1, 0
        ).astype(out_ref.dtype)


def join_kernel(*refs):
    at = 0
    for ref in refs[:-1]:
        refs[-1][at : at + ref.shape[0], :] = ref[...]
        at += ref.shape[0]


def half_kernel(stay_ref, pair_ref, out_ref):
    out_ref[...] = (stay_ref[...] + pair_ref[...].astype(F32)).astype(BF16)


def half_total_kernel(stay_ref, pair_ref, total_ref, out_ref):
    units = stay_ref.shape[0]
    out_ref[:units, :] = (stay_ref[...] + pair_ref[...].astype(F32)).astype(BF16)
    total = total_ref[...]
    rounded = total.astype(BF16).astype(F32)
    out_ref[units:, :] = jnp.concatenate([rounded, total - rounded], axis=0).astype(BF16)


def tied(values, after):
    leaves, tree = jax.tree.flatten(values)
    operands = {id(leaf): leaf for leaf in leaves + jax.tree.leaves(after)}
    keys = list(operands)
    random.Random(ORDER + len(keys)).shuffle(keys)
    held = dict(zip(keys, lax.optimization_barrier([operands[key] for key in keys])))
    return jax.tree.unflatten(tree, [held[id(leaf)] for leaf in leaves])


def shape(kind, *sizes):
    return jax.ShapeDtypeStruct(sizes, kind)


def call(kernel, name, outs, args, flops=0, specs=None, out_specs=None, scratch=(), mebibytes=18):
    return pl.pallas_call(
        kernel,
        out_shape=outs,
        in_specs=specs or [VMEM] * len(args),
        out_specs=out_specs or jax.tree.map(lambda _: VMEM, outs),
        scratch_shapes=list(scratch),
        compiler_params=pltpu.CompilerParams(vmem_limit_bytes=mebibytes * 2**20),
        cost_estimate=pl.CostEstimate(flops=flops, bytes_accessed=flops // 512, transcendentals=0),
        name=name,
    )(*args)


def body(prenorm_input, gain, router, routes, w_in, w_out, cotangent):
    halves = lax.axis_size("expert")
    experts = halves // 2
    groups = lax.axis_size("dp")
    columns = groups // 2
    tokens, width = prenorm_input.shape
    top = routes.shape[1]
    capacity = max(2, 5 * tokens * top // (4 * experts))
    slots = experts * capacity
    own = lax.axis_index("expert") // 2

    def over_half(value):
        return lax.ppermute(value, "expert", [(i, i ^ 1) for i in range(halves)])

    def over_pair(value):
        return lax.ppermute(value, "dp", [(i, i ^ 1) for i in range(groups)])

    def over_columns(value):
        return [
            lax.ppermute(value, "dp", [(i, (i + 2 * step) % groups) for i in range(groups)])
            for step in range(1, columns)
        ]

    def back_over_columns(values):
        return [
            lax.ppermute(value, "dp", [(i, (i - 2 * step) % groups) for i in range(groups)])
            for step, value in enumerate(values, 1)
        ]

    def over_experts(value, step):
        return lax.ppermute(value, "expert", [(i, (i + 2 * step) % halves) for i in range(halves)])

    def pairwise(value, name, size, bit):
        return value + lax.ppermute(value, name, [(i, i ^ bit) for i in range(size)])

    first = w_in[0].T
    second = w_out[0]
    units = first.shape[0]
    hidden_units = 4 * units

    routes_t = routes.T
    send = call(
        functools.partial(dispatch_kernel, experts, capacity),
        "dispatch",
        [shape(BF16, 2, capacity, width)] * experts,
        (prenorm_input, gain, routes_t, cotangent),
        flops=4 * slots * tokens * width,
        specs=[ANY] * 4,
        scratch=[
            pltpu.VMEM((tokens, width), BF16),
            pltpu.VMEM((width,), F32),
            pltpu.VMEM((top, tokens), jnp.int32),
            pltpu.VMEM((tokens, width), BF16),
            pltpu.SemaphoreType.DMA((4,)),
        ],
        mebibytes=60,
    )

    steps = sorted(range(experts), key=lambda step: min(step, experts - step))
    quarter = experts // 4
    early, late = steps[: 3 * quarter], steps[3 * quarter :]
    near = {0: send[0]}
    for step in early[1:]:
        near[step] = over_experts(send[step], step)
    side = {0: over_columns(send[0])}
    first_y = over_half(tied(first, send[0]))
    first_c = over_pair(tied(first, send[0]))

    stage = (first_y, first_c, [near[step] for step in early], side[0])
    second_held, late_held, early_held, first_y, side[0] = tied(
        (second, [send[step] for step in late], [near[step] for step in early], first_y, side[0]),
        stage,
    )
    for step, value in zip(late, late_held):
        near[step] = over_experts(value, step)
    for step, value in zip(early, early_held):
        near[step] = value
        if step:
            side[step] = over_columns(value)
    second_y = over_half(second_held)
    first_yc = over_pair(first_y)
    prepared = call(
        functools.partial(prepare_kernel, experts, capacity),
        "prepare",
        [shape(F32, tokens, width), shape(F32, tokens, 128), shape(BF16, slots, tokens)],
        (prenorm_input, routes_t),
    )

    stage = (
        first_yc,
        [near[step] for step in late],
        [side[step] for step in early[1:]],
        prepared,
    )
    late_held, second_held, early_held, first_yc, prepared = tied(
        (
            [near[step] for step in late],
            second_held,
            [side[step] for step in early[1:]],
            first_yc,
            prepared,
        ),
        stage,
    )
    for step, value in zip(early[1:], early_held):
        side[step] = value
    for step, value in zip(late, late_held):
        near[step] = value
        side[step] = over_columns(value)
    second_c = over_pair(second_held)
    second_yc = over_pair(second_y)

    def join(*parts):
        return call(join_kernel, "join", shape(BF16, hidden_units, width), parts)

    all_first = join(first_yc, first_c, first_y, first)
    all_second = join(second_yc, second_c, second_y, second_held)

    router_row = lax.dynamic_slice_in_dim(router, own, 1, 1).astype(F32).T

    def gather_rows(chosen):
        pieces = [near[step] for step in chosen]
        for turn in range(columns - 1):
            pieces = pieces + [side[step][turn] for step in chosen]
        return (
            jnp.concatenate([piece[0] for piece in pieces], axis=0),
            jnp.concatenate([piece[1] for piece in pieces], axis=0),
        )

    def first_product(rows_m, rows_d):
        count = rows_m.shape[0]
        return call(
            first_kernel,
            "first",
            [
                shape(BF16, count, hidden_units),
                shape(F32, count, hidden_units),
                shape(BF16, count, width),
                shape(F32, count, 128),
            ],
            (rows_m, rows_d, all_first, router_row),
            flops=2 * count * width * hidden_units,
        )

    def second_product(rows_d, hidden, slope, gate):
        count = rows_d.shape[0]
        return call(
            second_kernel,
            "second",
            [shape(BF16, count, hidden_units), shape(F32, count, 128)],
            (rows_d, all_second, hidden, slope, gate),
            flops=2 * count * width * hidden_units,
        )

    def row_gradients(rows_m, grad_pre, logit_gradient):
        count = grad_pre.shape[0]
        return call(
            rows_kernel,
            "rows",
            [
                shape(F32, count // columns, width),
                shape(BF16, count - count // columns, width),
                shape(F32, 8, width),
            ],
            (rows_m, grad_pre, logit_gradient, all_first, router_row),
            flops=2 * count * width * hidden_units,
        )

    def weight_gradient(at, blocks, left, right, kind):
        low = at * units // 128 * 128
        high = -(-(at + blocks) * units // 128) * 128
        return call(
            functools.partial(weight_kernel, at * units),
            "weights",
            shape(kind, blocks * units, width),
            (left, right),
            flops=2 * left.shape[0] * width * blocks * units,
            scratch=[pltpu.VMEM((high - low, left.shape[0]), BF16)],
        )

    def half_sum(stay, pair):
        return call(half_kernel, "half", shape(BF16, units, width), (stay, pair))

    early_m, early_d = gather_rows(early)
    early_hidden, early_slope, early_y, early_gate = first_product(early_m, early_d)
    early_pre, early_logit = second_product(early_d, early_hidden, early_slope, early_gate)
    early_own, early_side, early_sums = row_gradients(early_m, early_pre, early_logit)
    for step in late:
        near[step], side[step] = tied((near[step], side[step]), (early_own, early_side))
    late_m, late_d = gather_rows(late)

    def by_turn(rows):
        return list(rows.reshape(columns - 1, -1, width))

    def add_rows(own_rows, pieces):
        for piece in pieces:
            own_rows = own_rows + piece.astype(F32)
        return own_rows.astype(BF16).reshape(-1, capacity, width)

    returned = [None] * experts

    def send_back(chosen, rows):
        for step, value in zip(chosen, rows):
            returned[step] = over_experts(value, experts - step) if step else value

    early_back = back_over_columns(by_turn(early_side))
    late_hidden, late_slope, late_y, late_gate = first_product(late_m, late_d)
    hidden = jnp.concatenate([early_hidden, late_hidden], axis=0)
    grad_y = jnp.concatenate([early_y, late_y], axis=0)
    out_leave = weight_gradient(0, 1, hidden, grad_y, BF16)
    out_pair = over_pair(out_leave)
    hidden = tied(hidden, out_leave)
    out_stay = weight_gradient(2, 1, hidden, grad_y, F32)
    late_pre, late_logit = second_product(tied(late_d, out_stay), late_hidden, late_slope, late_gate)
    late_own, late_side, late_sums = row_gradients(late_m, late_pre, late_logit)
    sums = early_sums + late_sums
    line = jnp.arange(-(-(experts + 1) // 8) * 8, dtype=jnp.int32)[:, None]
    total = jnp.where(line == own, sums[:1], jnp.where(line == experts, sums[1:2], 0.0))
    out_half = half_sum(out_stay, out_pair)

    stage = (out_half, total, late_own, late_side)
    out_half, total, late_side, hidden = tied((out_half, total, late_side, hidden), stage)
    out_other = over_half(out_half)
    rows_m = jnp.concatenate([early_m, late_m], axis=0)
    grad_pre = jnp.concatenate([early_pre, late_pre], axis=0)
    total = pairwise(total, "dp", groups, 1)
    grad_pre, late_side = tied((grad_pre, late_side), total)
    bit = 2
    while bit < halves:
        total = pairwise(total, "expert", halves, bit)
        bit *= 2
    late_back = back_over_columns(by_turn(late_side))
    in_leave = weight_gradient(0, 1, grad_pre, rows_m, BF16)
    in_pair = over_pair(in_leave)
    in_stay = weight_gradient(2, 1, tied(grad_pre, in_leave), rows_m, F32)
    early_back, late_back = tied((early_back, late_back), total)
    early_rows = add_rows(early_own, early_back)
    late_rows = add_rows(late_own, late_back)
    moved = range(quarter, 2 * quarter)
    send_back([steps[at] for at in moved], [early_rows[at] for at in moved])
    moved_rows = [returned[steps[at]] for at in moved]
    total = tied(total, (early_rows, late_rows))
    bit = 2
    while bit < groups:
        total = pairwise(total, "dp", groups, bit)
        bit *= 2
    hidden, grad_pre = tied((hidden, grad_pre), in_stay)
    out_rest = over_pair(weight_gradient(1, 1, hidden, grad_y, BF16))
    out_mine = weight_gradient(3, 1, hidden, grad_y, F32)
    in_rest = over_pair(weight_gradient(1, 1, grad_pre, rows_m, BF16))
    in_mine = weight_gradient(3, 1, grad_pre, rows_m, F32)

    in_half = call(
        half_total_kernel,
        "half",
        shape(BF16, units + 2 * total.shape[0], width),
        (in_stay, in_pair, total),
    )
    stage = (out_other, early_rows, late_rows, moved_rows, in_half, out_mine, in_mine)
    out_other, early_rows, late_rows, moved_rows, in_half, out_mine, in_mine = tied(stage, stage)
    for at, value in zip(moved, moved_rows):
        returned[steps[at]] = value
    in_other = over_half(in_half)
    grad_out = (out_mine + out_rest.astype(F32) + out_other.astype(F32)).astype(BF16)[None]
    early_rows, late_rows = tied((early_rows, late_rows), grad_out)
    rest = [at for at in range(len(early)) if at not in moved]
    send_back([steps[at] for at in rest], [early_rows[at] for at in rest])
    send_back(late, late_rows)

    returned = tied(returned, (in_other, grad_out))
    norm, deviation, places = prepared
    input_grad, grad_in, grad_router, grad_gain = call(
        finish_kernel,
        "finish",
        [
            shape(BF16, tokens, width),
            shape(BF16, units, width),
            shape(F32, experts, width),
            shape(F32, width),
        ],
        (
            norm,
            deviation,
            places,
            gain,
            cotangent,
            jnp.concatenate(returned, axis=0),
            in_mine,
            in_rest,
            in_other,
            in_half,
        ),
    )
    return (input_grad, grad_in.T[None], grad_out, grad_router.T, grad_gain)


def solution(mesh):
    in_specs = (
        P(("expert", "dp"), None),
        P(),
        P(),
        P(("expert", "dp"), None),
        P("expert", None, "dp"),
        P("expert", "dp", None),
        P(("expert", "dp"), None),
    )
    out_specs = (
        P(("expert", "dp"), None),
        P("expert", None, "dp"),
        P("expert", "dp", None),
        P(),
        P(),
    )
    return jax.shard_map(body, mesh=mesh, in_specs=in_specs, out_specs=out_specs, check_vma=False)
```
